256 devices in a mesh: dp: 8 (over z), section: 4 (over y), mp: 8 (over x, core).
Axes of the slice: x: 4, y: 4, z: 8, core: 2. Of those that a mesh axis runs over, the one named last changes fastest.
Arguments:
- patches: bfloat16 [1, 8192, 1280], P(None, ('dp', 'mp')), may hold values from -6 to 6
- windows: int32 [1, 8192], P(None, ('dp', 'mp')), may hold values from 0 to 8191, as said below
- gain: float32 [4, 1280], P('section'), may hold values from 0.25 to 1.75
- w_qkv: bfloat16 [4, 1280, 1920], P('section'), may hold values from -3 to 3
- w_out: bfloat16 [4, 640, 1280], P('section'), may hold values from -0.25 to 0.25
- cotangent: bfloat16 [1, 8192, 1280], P(None, ('dp', 'mp')), may hold values from -16 to 16
Outputs:
- activations: bfloat16 [4, 1, 8192, 1280], P('section', None, ('dp', 'mp'))
- input_grads: bfloat16 [4, 1, 8192, 1280], P('section', None, ('dp', 'mp'))
- grad_qkv: float32 [4, 1280, 1920], P('section', ('dp', 'mp'))
- grad_out: float32 [4, 640, 1280], P('section', None, ('dp', 'mp'))
- grad_gain: float32 [4, 1280], P('section', ('dp', 'mp'))
The draws below stay inside these ranges and needn't reach their ends.
Inputs may be any that keep to these rules, and one draw needn't show every extreme that they name: `windows`: A window's number is the index of its first patch among all patches of all micro-batches laid end to end, so numbers never fall; a window's patches are consecutive and lie inside one aligned block of 128 patches; every window holds 1 to 112 patches, and every block holds one window of exactly 112.
All inputs are finite; a program needn't handle non-finite values.
Results may differ from the reference program's by a relative error of at most 0.025.
Values may be sent and summed in bfloat16 or wider, within the bound.
A program may use at most 192 MiB of HBM per device.

```python
from functools import partial
import jax
import jax.numpy as jnp
from jax import lax

VD = 1280
HEAD = 80
HW = 640
WIN = 112
MB = 1
PDEV = 128
PATCHES = 8192
N_SECTION = 4


def draw_windows(key, part):
    key = jax.random.fold_in(key, 11)
    first_key, second_key = jax.random.split(key)
    block_total = PATCHES // PDEV
    offset = jax.random.randint(first_key, (MB, block_total, 1), 0, PDEV - WIN)
    coin_flip = jax.random.randint(second_key, (MB, block_total, PDEV), 0, 8)
    position = jnp.arange(PDEV, dtype=jnp.int32)[None, None, :]
    inside = (position > offset) & (position < offset + WIN)
    boundary = (coin_flip == 0) | (position % WIN == 0) | (position == offset) | (position == offset + WIN)
    boundary = boundary & jnp.logical_not(inside)
    flat = boundary.reshape(MB * PATCHES)
    global_index = jnp.arange(MB * PATCHES, dtype=jnp.int32)
    flat = flat | (global_index == MB * PATCHES - 1)
    starts = jnp.where(flat, global_index, jnp.zeros_like(global_index))
    counted = lax.cummax(starts, axis=0)
    return counted.reshape(MB, PATCHES).astype(jnp.int32)


def draw_w_qkv(key, part):
    key = jax.random.fold_in(key, 7)
    first_key = jax.random.fold_in(key, 0)
    base_draw = jnp.clip(jax.random.normal(first_key, (N_SECTION, VD, 3, HW), jnp.float32), -4.0, 4.0)
    scaled = base_draw * VD ** (-0.5)
    return scaled.reshape(N_SECTION, VD, 3 * HW).astype(jnp.bfloat16)


def spiked(drawn, stream_key, source, target, parts, factor):
    owner, partner = [(jnp.arange(drawn.shape[dim]) // (drawn.shape[dim] // parts)).reshape([-1 if axis == dim else 1 for axis in range(drawn.ndim)]) for dim in (source, target)]
    chosen = jax.random.permutation(stream_key, parts)[partner]
    strong = (owner == chosen) | (owner == (partner + parts // 2) % parts)
    return jnp.where(strong, factor * drawn, drawn)


def level_of(stream_key, shape, pieces, least, high):
    level, own = 1.0, jax.random.fold_in(stream_key, 6)
    for dim, shards_of in pieces:
        heights = jnp.exp(jax.random.uniform(jax.random.fold_in(own, dim), (shards_of,), jnp.float32, least / len(pieces), high / len(pieces)))
        level = level * jnp.repeat(heights, shape[dim] // shards_of).reshape([-1 if axis == dim else 1 for axis in range(len(shape))])
    return level


def normal_values(own_key, shape, deviation, bound, shards=(), kind=jnp.bfloat16):
    result = jax.random.normal(own_key, shape, jnp.float32) * deviation
    if len(shards) > 0:
        result = level_of(own_key, shape, shards, -0.22, 0.18) * result
    return jnp.clip(result, min=-bound, max=bound).astype(kind)


def heavy_noise(key, extent, scale, limit, cuts, heavy, kind=jnp.bfloat16):
    drawn = scale * jax.random.normal(key, extent, jnp.float32)
    if cuts:
        drawn = drawn * level_of(key, extent, cuts, -0.22, 0.18)
    return jnp.clip(spiked(drawn, jax.random.fold_in(key, 3), *heavy), -limit, limit).astype(kind)


def setup_inputs(seed: int = 0) -> dict:
    key_list = jax.random.split(jax.random.key(seed), 7)
    patches = normal_values(key_list[0], (MB, PATCHES, VD), 1.0, 6.0, ((1, 64),))
    windows = draw_windows(jax.random.fold_in(key_list[6], 71), 0)
    gain = jnp.clip(1.0 + 0.15 * jax.random.normal(key_list[2], (N_SECTION, VD), jnp.float32), 0.25, 1.75)
    w_qkv = draw_w_qkv(jax.random.fold_in(key_list[6], 71), 0)
    w_out = normal_values(key_list[4], (N_SECTION, HW, VD), HW ** -0.5, 0.25, ((0, 4),))
    cotangent = heavy_noise(key_list[5], (MB, PATCHES, VD), 1.0, 16.0, ((1, 64),), (1, 2, 64, 4.0))
    return {"patches": patches, "windows": windows, "gain": gain, "w_qkv": w_qkv, "w_out": w_out, "cotangent": cotangent}


def section_layer(window_ids, hidden, gain_row, proj_qkv, proj_out):
    row_count = hidden.shape[0]
    width_heads = proj_out.shape[0]
    head_count = width_heads // HEAD
    widened = hidden.astype(jnp.float32)
    spread = lax.rsqrt(lax.optimization_barrier(jnp.mean(widened * widened, axis=-1, keepdims=True)) + 1e-06)
    normed = (widened * spread * gain_row).astype(jnp.bfloat16)
    packed = jnp.dot(normed, proj_qkv, preferred_element_type=jnp.float32).astype(jnp.bfloat16)
    queries = packed[:, :width_heads].reshape(row_count, head_count, HEAD)
    key_rows = packed[:, width_heads:2 * width_heads].reshape(row_count, head_count, HEAD)
    values = packed[:, 2 * width_heads:].reshape(row_count, head_count, HEAD)
    scores = jnp.einsum('qhd,khd->hqk', queries.astype(jnp.float32), key_rows.astype(jnp.float32)) * HEAD ** (-0.5)
    same_window = window_ids[:, None] == window_ids[None, :]
    scores = jnp.where(same_window[None], scores, -1e+30)
    weights = jax.nn.softmax(scores, axis=-1).astype(jnp.bfloat16)
    attended = jnp.einsum('hqk,khd->qhd', weights.astype(jnp.float32), values.astype(jnp.float32))
    attended = attended.astype(jnp.bfloat16).reshape(row_count, width_heads)
    mixture = jnp.dot(attended, proj_out, preferred_element_type=jnp.float32)
    return (widened + mixture).astype(jnp.bfloat16)

def reference(patches, windows, gain, w_qkv, w_out, cotangent):
    block_count = MB * (PATCHES // PDEV)
    blocks_in = patches.reshape(block_count, PDEV, VD)
    blocks_ids = windows.reshape(block_count, PDEV)
    blocks_cot = cotangent.reshape(block_count, PDEV, VD)

    def one_block(running, block_data):
        entering, window_ids, upstream = block_data
        outputs = []
        pullers = []
        hidden = entering
        for section_index in range(N_SECTION):
            hidden, puller = jax.vjp(partial(section_layer, window_ids), hidden, gain[section_index], w_qkv[section_index], w_out[section_index])
            outputs.append(hidden)
            pullers.append(puller)
        incoming = upstream
        back_list = [None] * N_SECTION
        qkv_list = [None] * N_SECTION
        out_list = [None] * N_SECTION
        gain_list = [None] * N_SECTION
        for section_index in reversed(range(N_SECTION)):
            d_hidden, d_gain, d_qkv, d_out = pullers[section_index](incoming)
            back_list[section_index] = d_hidden
            qkv_list[section_index] = d_qkv.astype(jnp.float32)
            out_list[section_index] = d_out.astype(jnp.float32)
            gain_list[section_index] = d_gain.astype(jnp.float32)
            incoming = d_hidden
        sums_qkv, sums_out, sums_gain = running
        running = (sums_qkv + jnp.stack(qkv_list), sums_out + jnp.stack(out_list), sums_gain + jnp.stack(gain_list))
        return (running, (jnp.stack(outputs), jnp.stack(back_list)))
    start_sums = (jnp.zeros(w_qkv.shape, jnp.float32), jnp.zeros(w_out.shape, jnp.float32), jnp.zeros(gain.shape, jnp.float32))
    (grad_qkv, grad_out, grad_gain), (forward_all, backward_all) = lax.scan(one_block, start_sums, (blocks_in, blocks_ids, blocks_cot))
    per_device = PATCHES // PDEV
    activations = forward_all.reshape(MB, per_device, N_SECTION, PDEV, VD).transpose(2, 0, 1, 3, 4).reshape(N_SECTION, MB, PATCHES, VD)
    input_grads = backward_all.reshape(MB, per_device, N_SECTION, PDEV, VD).transpose(2, 0, 1, 3, 4).reshape(N_SECTION, MB, PATCHES, VD)
    return (activations, input_grads, grad_qkv, grad_out, grad_gain)
```

```python
import jax
import jax.numpy as jnp
from jax import lax
from jax.experimental import pallas as pl
from jax.experimental.pallas import tpu as pltpu
from jax.sharding import PartitionSpec as P

HEAD = 80
HEADS = 8
ROWS = 128
VD = 1280
HW = 640
NM = 8
NZ = 8
NS = 4
CHUNKS = 2
CR = ROWS // CHUNKS
ZR = VD // NZ
FR = ZR // NM
SCALE = HEAD**-0.5
MESH = pl.DeviceIdType.MESH
F32 = jnp.float32
BF16 = jnp.bfloat16


def nt(a, b):
    return lax.dot_general(a, b, (((1,), (1,)), ((), ())), preferred_element_type=F32)


def nn(a, b):
    return lax.dot_general(a, b, (((1,), (0,)), ((), ())), preferred_element_type=F32)


def tn(a, b):
    return lax.dot_general(a, b, (((0,), (0,)), ((), ())), preferred_element_type=F32)


def head_span(h):
    lo = HEAD * h
    t0 = lo // 128 * 128
    t1 = -(-(lo + HEAD) // 128) * 128
    return lo, t0, t1


def masked(x, h):
    lo, t0, t1 = head_span(h)
    cols = lax.broadcasted_iota(jnp.int32, (ROWS, t1 - t0), 1) + t0
    return jnp.where((cols >= lo) & (cols < lo + HEAD), x, jnp.zeros_like(x))


def add_head(acc, h, value):
    lo, t0, t1 = head_span(h)
    for t in range(t0, t1, 128):
        part = value[:, t - t0 : t - t0 + 128]
        if h > 0 and t < -(-lo // 128) * 128 and lo % 128 != 0 and t <= lo:
            acc[:, t : t + 128] += part
        else:
            acc[:, t : t + 128] = part


def kernel(
    patches, cot, win_row, win_col, gain, wq_hbm, wo_hbm,
    act, gin, out_q, out_o, out_gain,
    wq, wo, hbuf, gbuf, normed, packed, pt32, ptb, att, acc, acc2, datt, dp,
    ngt, atg, dpt, gt32, gperm, dpg, gpg, dgain, dgrecv, dgz, dgzrecv,
    rq, ro, sq, so, zq, zo, fin, finrecv, total,
    w_sem, hs, hr, gs, gr, ns, nr, as_, ar, ds, dr, ps, pr, vs, vr, us, ur, qs, qr, os_, or_, fs, fr,
):
    s = lax.axis_index("section")
    m = lax.axis_index("mp")
    z = lax.axis_index("dp")
    copies = []
    for i in range(3):
        cols = pl.ds(i * HW, HW)
        copies.append(pltpu.make_async_copy(wq_hbm.at[:, cols], wq.at[:, cols], w_sem.at[i]))
    copies.append(pltpu.make_async_copy(wo_hbm, wo, w_sem.at[3]))
    for c in copies:
        c.start()

    barrier = pltpu.get_barrier_semaphore()
    for d in range(1, NM):
        pl.semaphore_signal(barrier, inc=1, device_id={"mp": lax.rem(m + d, NM)}, device_id_type=MESH)
    for d in range(1, NZ):
        pl.semaphore_signal(barrier, inc=1, device_id={"dp": lax.rem(z + d, NZ)}, device_id_type=MESH)
    for d in (1, NS - 1):
        pl.semaphore_signal(barrier, inc=1, device_id={"section": lax.rem(s + d, NS)}, device_id_type=MESH)

    def remote(src, dst, ssem, rsem, where):
        return pltpu.make_async_remote_copy(
            src_ref=src, dst_ref=dst, send_sem=ssem, recv_sem=rsem, device_id=where, device_id_type=MESH
        )

    def rows_of(c):
        return pl.ds(c * CR, CR)

    def hop_forward(c):
        return remote(
            act.at[rows_of(c)], hbuf.at[rows_of(c)], hs.at[c], hr.at[c], {"section": lax.rem(s + 1, NS)}
        )

    def hop_back(c):
        return remote(
            gin.at[rows_of(c)], gbuf.at[rows_of(c)], gs.at[c], gr.at[c], {"section": lax.rem(s + NS - 1, NS)}
        )

    def mp_lanes(i):
        return pl.ds(pl.multiple_of(i * ROWS, ROWS), ROWS)

    same = win_col[...] == win_row[...]

    @pl.when(s == 0)
    def _():
        hbuf[...] = patches[...]

    pl.semaphore_wait(barrier, (NM - 1) + (NZ - 1) + 2)

    for c in range(CHUNKS):
        rows = rows_of(c)

        @pl.when(s > 0)
        def _():
            hop_forward(c).wait_recv()

        wide = hbuf[rows, :].astype(F32)
        spread = lax.rsqrt(jnp.mean(wide * wide, axis=-1, keepdims=True) + 1e-6)
        normed[rows, :] = (wide * spread * gain[...]).astype(BF16)
        for i in range(3):
            if c == 0:
                copies[i].wait()
            packed[rows, i * HW : (i + 1) * HW] = nn(
                normed[rows, :], wq[:, i * HW : (i + 1) * HW]
            ).astype(BF16)
    copies[3].wait()

    for h in range(HEADS):
        lo, t0, t1 = head_span(h)
        q = packed[:, t0:t1]
        k = masked(packed[:, HW + t0 : HW + t1], h)
        scores = nt(k, q) * SCALE
        scores = jnp.where(same, scores, -1e30)
        top = jnp.max(scores, axis=0, keepdims=True)
        e = jnp.exp(scores - top)
        p = e / jnp.sum(e, axis=0, keepdims=True)
        pt32[h] = p
        ptb[h] = p.astype(BF16)
    for h in range(HEADS):
        lo, t0, t1 = head_span(h)
        v = masked(packed[:, 2 * HW + t0 : 2 * HW + t1], h)
        add_head(acc, h, tn(ptb[h], v))
    att[...] = acc[...].astype(BF16)

    def project(c):
        rows = rows_of(c)
        act[rows, :] = (hbuf[rows, :].astype(F32) + nn(att[rows, :], wo[...])).astype(BF16)

    chip = m // 2
    core = lax.rem(m, 2)
    sibling = chip * 2 + 1 - core

    def gather_copies(slot, i, to):
        lanes = mp_lanes(slot)
        return (
            remote(ngt.at[:, lanes], ngt.at[:, lanes], ns.at[i], nr.at[i], {"mp": to}),
            remote(atg.at[lanes, :], atg.at[lanes, :], as_.at[i], ar.at[i], {"mp": to}),
        )

    def across(d):
        return lax.rem(chip + d, NM // 2) * 2 + core

    def gather_start():
        ngt[:, mp_lanes(m)] = normed[...].T
        atg[mp_lanes(m), :] = att[...]
        for d in range(1, NM // 2):
            for c in gather_copies(m, d, across(d)):
                c.start()
        for c in gather_copies(m, 0, sibling):
            c.start()

    def gather_forward():
        for d in range(1, NM // 2):
            source = across(NM // 2 - d)
            for c in gather_copies(source, d, across(d)):
                c.wait_recv()
            for c in gather_copies(source, NM // 2 - 1 + d, sibling):
                c.start()

    def gather_finish():
        for c in gather_copies(sibling, 0, sibling):
            c.wait_recv()
        for d in range(1, NM // 2):
            source = lax.rem(chip + NM // 2 - d, NM // 2) * 2 + 1 - core
            for c in gather_copies(source, NM // 2 - 1 + d, sibling):
                c.wait_recv()

    def gather_drain():
        for i in range(NM - 1):
            for c in gather_copies(m, i, sibling):
                c.wait_send()

    @pl.when(s < NS - 1)
    def _():
        for c in range(CHUNKS):
            project(c)
            hop_forward(c).start()
        gather_start()
        gather_forward()

    @pl.when(s == NS - 1)
    def _():
        gbuf[...] = cot[...]

    for c in range(CHUNKS):
        rows = rows_of(c)

        @pl.when(s < NS - 1)
        def _():
            hop_back(c).wait_recv()

        datt[rows, :] = nt(gbuf[rows, :], wo[...]).astype(BF16)

    for h in range(HEADS):
        lo, t0, t1 = head_span(h)
        q = masked(packed[:, t0:t1], h)
        k = masked(packed[:, HW + t0 : HW + t1], h)
        v = masked(packed[:, 2 * HW + t0 : 2 * HW + t1], h)
        da = datt[:, t0:t1]
        dprob = nt(v, da).astype(BF16).astype(F32)
        p = pt32[h]
        dsc = p * (dprob - jnp.sum(p * dprob, axis=0, keepdims=True))
        dsc = (dsc * SCALE).astype(BF16)
        add_head(acc, h, tn(dsc, k))
        add_head(acc2, h, nn(dsc, q))
        add_head(total, h, nn(ptb[h], masked(da, h)))
    dp[:, 0:HW] = acc[...].astype(BF16)
    dp[:, HW : 2 * HW] = acc2[...].astype(BF16)
    dp[:, 2 * HW : 3 * HW] = total[...].astype(BF16)

    def column_copies(d):
        to = lax.rem(m + d, NM)
        rows = pl.ds(pl.multiple_of(to * 256, 256), 256)
        lanes = mp_lanes(m)
        return (
            remote(dpt.at[rows], dpg.at[:, lanes], ds.at[d], dr.at[d], {"mp": to}),
            remote(gperm.at[rows], gpg.at[:, lanes], ps.at[d], pr.at[d], {"mp": to}),
        )

    def columns_q():
        dpt[0 : 3 * HW, :] = dp[...].T
        dpt[3 * HW : 2048, :] = jnp.zeros((128, ROWS), BF16)
        for d in range(1, NM):
            column_copies(d)[0].start()
        dpg[:, mp_lanes(m)] = dpt[pl.ds(pl.multiple_of(m * 256, 256), 256), :]

    def columns_g():
        gt32[0:VD, :] = gbuf[...].astype(F32).T
        gt32[VD : VD + 32, :] = jnp.zeros((32, ROWS), F32)
        for i in range(NM):
            for j in range(NZ):
                first = FR * (NM * j + i)
                gperm[i * 256 + j * 32 : i * 256 + j * 32 + 32, :] = gt32[first : first + 32, :].astype(BF16)
        for d in range(1, NM):
            column_copies(d)[1].start()
        gpg[:, mp_lanes(m)] = gperm[pl.ds(pl.multiple_of(m * 256, 256), 256), :]

    @pl.when(s == 0)
    def _():
        columns_q()

    for c in range(CHUNKS):
        rows = rows_of(c)
        dn = nt(dp[rows, :], wq[...]).astype(BF16).astype(F32)
        wide = hbuf[rows, :].astype(F32)
        spread = lax.rsqrt(jnp.mean(wide * wide, axis=-1, keepdims=True) + 1e-6)
        lifted = dn * gain[...]
        inner = jnp.mean(lifted * wide, axis=-1, keepdims=True)
        back = gbuf[rows, :].astype(F32) + spread * lifted - wide * (spread * spread * spread * inner)
        gin[rows, :] = back.astype(BF16)

        @pl.when(s > 0)
        def _():
            hop_back(c).start()

        part = jnp.sum(dn * (wide * spread), axis=0, keepdims=True)
        if c == 0:
            dgain[0] = part
        else:
            dgain[0] += part

    @pl.when(s > 0)
    def _():
        columns_q()

    @pl.when(s == NS - 1)
    def _():
        for c in range(CHUNKS):
            project(c)
        gather_start()
        gather_forward()

    columns_g()

    def gain_mp(d):
        return remote(dgain.at[0], dgrecv.at[d], vs.at[d], vr.at[d], {"mp": lax.rem(m + d, NM)})

    def gain_dp(d):
        return remote(dgz.at[0], dgzrecv.at[d], us.at[d], ur.at[d], {"dp": lax.rem(z + d, NZ)})

    for d in range(1, NM):
        gain_mp(d).start()

    gather_finish()
    for d in range(1, NM):
        column_copies(d)[0].wait_recv()

    def chunk_q(k):
        rows = pl.ds(pl.multiple_of(k * ZR, 16), ZR)
        return nt(ngt[rows, :], dpg[...])

    def chunk_o(k):
        rows = pl.ds(pl.multiple_of(k * 32, 32), 32)
        return nn(gpg[rows, :], atg[...])

    up = {"dp": lax.rem(z + 1, NZ)}
    down = {"dp": lax.rem(z + NZ - 1, NZ)}

    def ring_q(t):
        return remote(sq.at[t], zq.at[t], qs.at[t], qr.at[t], up if t < 4 else down)

    def ring_o(t):
        return remote(so.at[t], zo.at[t], os_.at[t], or_.at[t], up if t < 4 else down)

    def owner(t):
        if t < 4:
            return lax.rem(z + 4 - t, NZ)
        return lax.rem(z + NZ - 3 + (t - 4), NZ)

    for t in (0, 4):
        sq[t] = chunk_q(owner(t)).astype(BF16)
        ring_q(t).start()
    for d in range(1, NM):
        column_copies(d)[1].wait_recv()
    for t in (0, 4):
        so[t] = chunk_o(owner(t)).astype(BF16)
        ring_o(t).start()
    sum_gain = dgain[0]
    for d in range(1, NM):
        gain_mp(d).wait_recv()
        sum_gain = sum_gain + dgrecv[d]
    dgz[0] = sum_gain
    for d in range(1, NZ):
        gain_dp(d).start()
    for t in (1, 5, 2, 6, 3):
        mine = chunk_q(owner(t))
        ring_q(t - 1).wait_recv()
        sq[t] = (mine + zq[t - 1].astype(F32)).astype(BF16)
        ring_q(t).start()
        mine = chunk_o(owner(t))
        ring_o(t - 1).wait_recv()
        so[t] = (mine + zo[t - 1].astype(F32)).astype(BF16)
        ring_o(t).start()
    rq[0:ZR, :] = chunk_q(z)
    ro[...] = chunk_o(z)
    for t in (6, 3):
        ring_q(t).wait_recv()
        rq[0:ZR, :] += zq[t].astype(F32)

    def piece(d):
        return remote(fin.at[lax.rem(m + d, NM)], finrecv.at[m], fs.at[d], fr.at[d], {"mp": lax.rem(m + d, NM)})

    for i in range(NM):
        if FR * i + 24 <= ZR:
            fin[i] = rq[FR * i : FR * i + 24, :]
        else:
            fin[i, 0:FR] = rq[FR * i : FR * i + FR, :]
            fin[i, FR:24] = jnp.zeros((24 - FR, 256), F32)
    for d in range(1, NM):
        piece(d).start()
    finrecv[m] = fin[m]

    for t in (6, 3):
        ring_o(t).wait_recv()
        ro[...] += zo[t].astype(F32)
    out_o[...] = ro[...].T[:, 0:FR]
    sum_gain = dgz[0]
    for d in range(1, NZ):
        gain_dp(d).wait_recv()
        sum_gain = sum_gain + dgzrecv[d]
    out_gain[...] = sum_gain

    for d in range(1, NM):
        source = lax.rem(m + NM - d, NM)
        remote(fin.at[source], finrecv.at[source], fs.at[d], fr.at[d], {"mp": source}).wait_recv()
    for i in range(NM):
        wide = min(256, 3 * HW - 256 * i)
        out_q[:, 256 * i : 256 * i + wide] = finrecv[i, 0:FR, 0:wide]

    @pl.when(s < NS - 1)
    def _():
        for c in range(CHUNKS):
            hop_forward(c).wait_send()

    @pl.when(s > 0)
    def _():
        for c in range(CHUNKS):
            hop_back(c).wait_send()

    gather_drain()
    for d in range(1, NM):
        for c in column_copies(d):
            c.wait_send()
        gain_mp(d).wait_send()
        piece(d).wait_send()
    for d in range(1, NZ):
        gain_dp(d).wait_send()
    for t in range(7):
        ring_q(t).wait_send()
        ring_o(t).wait_send()


def on_device(patches, windows, gain, w_qkv, w_out, cotangent):
    vmem = pl.BlockSpec(memory_space=pltpu.VMEM)
    hbm = pl.BlockSpec(memory_space=pl.ANY)
    dma = pltpu.SemaphoreType.DMA
    scratch = [
        pltpu.VMEM((VD, 3 * HW), BF16),
        pltpu.VMEM((HW, VD), BF16),
        pltpu.VMEM((ROWS, VD), BF16),
        pltpu.VMEM((ROWS, VD), BF16),
        pltpu.VMEM((ROWS, VD), BF16),
        pltpu.VMEM((ROWS, 3 * HW), BF16),
        pltpu.VMEM((HEADS, ROWS, ROWS), F32),
        pltpu.VMEM((HEADS, ROWS, ROWS), BF16),
        pltpu.VMEM((ROWS, HW), BF16),
        pltpu.VMEM((ROWS, HW), F32),
        pltpu.VMEM((ROWS, HW), F32),
        pltpu.VMEM((ROWS, HW), BF16),
        pltpu.VMEM((ROWS, 3 * HW), BF16),
        pltpu.VMEM((VD, NM * ROWS), BF16),
        pltpu.VMEM((NM * ROWS, HW), BF16),
        pltpu.VMEM((2048, ROWS), BF16),
        pltpu.VMEM((VD + 32, ROWS), F32),
        pltpu.VMEM((2048, ROWS), BF16),
        pltpu.VMEM((256, NM * ROWS), BF16),
        pltpu.VMEM((256, NM * ROWS), BF16),
        pltpu.VMEM((1, 1, VD), F32),
        pltpu.VMEM((NM, 1, VD), F32),
        pltpu.VMEM((1, 1, VD), F32),
        pltpu.VMEM((NZ, 1, VD), F32),
        pltpu.VMEM((ZR, 256), F32),
        pltpu.VMEM((32, HW), F32),
        pltpu.VMEM((7, ZR, 256), BF16),
        pltpu.VMEM((7, 32, HW), BF16),
        pltpu.VMEM((7, ZR, 256), BF16),
        pltpu.VMEM((7, 32, HW), BF16),
        pltpu.VMEM((NM, 24, 256), F32),
        pltpu.VMEM((NM, 24, 256), F32),
        pltpu.VMEM((ROWS, HW), F32),
        dma((4,)),
        dma((CHUNKS,)), dma((CHUNKS,)), dma((CHUNKS,)), dma((CHUNKS,)),
    ] + [dma((8,)) for _ in range(18)]
    act, gin, out_q, out_o, out_gain = pl.pallas_call(
        kernel,
        out_shape=(
            jax.ShapeDtypeStruct((ROWS, VD), BF16),
            jax.ShapeDtypeStruct((ROWS, VD), BF16),
            jax.ShapeDtypeStruct((FR, 3 * HW), F32),
            jax.ShapeDtypeStruct((HW, FR), F32),
            jax.ShapeDtypeStruct((1, VD), F32),
        ),
        in_specs=[vmem] * 5 + [hbm] * 2,
        out_specs=(vmem,) * 5,
        scratch_shapes=scratch,
        compiler_params=pltpu.CompilerParams(
            collective_id=0, has_side_effects=True, vmem_limit_bytes=48 * 1024 * 1024
        ),
    )(
        patches[0], cotangent[0], windows, windows.reshape(ROWS, 1), gain, w_qkv[0], w_out[0]
    )
    place = (lax.axis_index("dp") * NM + lax.axis_index("mp")) * FR
    own_gain = lax.dynamic_slice(out_gain, (0, place), (1, FR))
    return (act[None, None], gin[None, None], out_q[None], out_o[None], own_gain)


def solution(mesh):
    in_specs = (
        P(None, ("dp", "mp"), None),
        P(None, ("dp", "mp")),
        P("section", None),
        P("section", None, None),
        P("section", None, None),
        P(None, ("dp", "mp"), None),
    )
    out_specs = (
        P("section", None, ("dp", "mp"), None),
        P("section", None, ("dp", "mp"), None),
        P("section", ("dp", "mp"), None),
        P("section", None, ("dp", "mp")),
        P("section", ("dp", "mp")),
    )
    return jax.shard_map(
        on_device, mesh=mesh, in_specs=in_specs, out_specs=out_specs, check_vma=False
    )
```

```python
import jax
import jax.numpy as jnp
from jax import lax
from jax.experimental import pallas as pl
from jax.experimental.pallas import tpu as pltpu
from jax.sharding import PartitionSpec as P

HEAD = 80
HEADS = 8
ROWS = 128
VD = 1280
HW = 640
NM = 8
NZ = 8
NS = 4
CHUNKS = 5
CW = VD // CHUNKS
ZR = VD // NZ
FR = ZR // NM
SCALE = HEAD**-0.5
MESH = pl.DeviceIdType.MESH
F32 = jnp.float32
BF16 = jnp.bfloat16


def nt(a, b):
    return lax.dot_general(a, b, (((1,), (1,)), ((), ())), preferred_element_type=F32)


def nn(a, b):
    return lax.dot_general(a, b, (((1,), (0,)), ((), ())), preferred_element_type=F32)


def tn(a, b):
    return lax.dot_general(a, b, (((0,), (0,)), ((), ())), preferred_element_type=F32)


def head_span(h):
    lo = HEAD * h
    t0 = lo // 128 * 128
    t1 = -(-(lo + HEAD) // 128) * 128
    return lo, t0, t1


def masked(x, h):
    lo, t0, t1 = head_span(h)
    cols = lax.broadcasted_iota(jnp.int32, (ROWS, t1 - t0), 1) + t0
    return jnp.where((cols >= lo) & (cols < lo + HEAD), x, jnp.zeros_like(x))


def add_head(acc, h, value):
    lo, t0, t1 = head_span(h)
    for t in range(t0, t1, 128):
        part = value[:, t - t0 : t - t0 + 128]
        if h > 0 and t < -(-lo // 128) * 128 and lo % 128 != 0 and t <= lo:
            acc[:, t : t + 128] += part
        else:
            acc[:, t : t + 128] = part


def kernel(
    patches, cot, win_hbm, gain_hbm, wq_hbm, wo_hbm,
    act, gin, out_q, out_o, out_gain,
    wq, wo, win, gain, hbuf, gbuf, hout, gout, pacc, dacc, packed, pt32, ptb, att, acc, acc2, acc3,
    datt, dp, lifted, rs,
    ngt, atg, dpt, gt32, gperm, dpg, gpg, dgain, dgrecv, dgz, dgzrecv,
    rq, ro, sq, so, zq, zo, fin, finrecv,
    w_sem, in_sem, o_sem, hs, hr, gs, gr, ns, nr, as_, ar, ds, dr, ps, pr, vs, vr, us, ur, qs, qr, os_, or_, fs, fr,
):
    s = lax.axis_index("section")
    m = lax.axis_index("mp")
    z = lax.axis_index("dp")

    def cols_of(j):
        return pl.ds(j * CW, CW)

    def load_patches(j):
        return pltpu.make_async_copy(patches.at[:, cols_of(j)], hbuf.at[j], in_sem.at[j])

    def load_cot(j):
        return pltpu.make_async_copy(cot.at[:, cols_of(j)], gbuf.at[j], in_sem.at[j])

    def load_wq(j):
        return pltpu.make_async_copy(wq_hbm.at[cols_of(j)], wq.at[cols_of(j)], w_sem.at[j])

    load_wo = pltpu.make_async_copy(wo_hbm, wo, w_sem.at[5])
    load_gain = pltpu.make_async_copy(gain_hbm, gain, w_sem.at[6])
    load_win = pltpu.make_async_copy(win_hbm, win, w_sem.at[7])

    load_gain.start()

    @pl.when(s == 0)
    def _():
        for j in range(CHUNKS):
            load_patches(j).start()

    for j in range(CHUNKS):
        load_wq(j).start()
    load_win.start()
    load_wo.start()

    @pl.when(s == NS - 1)
    def _():
        for j in range(CHUNKS):
            load_cot(j).start()

    barrier = pltpu.get_barrier_semaphore()
    for d in range(1, NM):
        pl.semaphore_signal(barrier, inc=1, device_id={"mp": lax.rem(m + d, NM)}, device_id_type=MESH)
    for d in range(1, NZ):
        pl.semaphore_signal(barrier, inc=1, device_id={"dp": lax.rem(z + d, NZ)}, device_id_type=MESH)
    for d in (1, NS - 1):
        pl.semaphore_signal(barrier, inc=1, device_id={"section": lax.rem(s + d, NS)}, device_id_type=MESH)

    dpt[3 * HW : 2048, :] = jnp.zeros((2048 - 3 * HW, ROWS), BF16)
    gt32[VD : VD + 32, :] = jnp.zeros((32, ROWS), F32)

    def remote(src, dst, ssem, rsem, where):
        return pltpu.make_async_remote_copy(
            src_ref=src, dst_ref=dst, send_sem=ssem, recv_sem=rsem, device_id=where, device_id_type=MESH
        )

    def hop_forward(j):
        return remote(hout.at[j], hbuf.at[j], hs.at[j], hr.at[j], {"section": lax.rem(s + 1, NS)})

    def hop_back(j):
        return remote(gout.at[j], gbuf.at[j], gs.at[j], gr.at[j], {"section": lax.rem(s + NS - 1, NS)})

    def mp_lanes(i):
        return pl.ds(pl.multiple_of(i * ROWS, ROWS), ROWS)

    def fold(x):
        return x[:, 0:128] + x[:, 128:256]

    load_gain.wait()
    squares = jnp.zeros((ROWS, 128), F32)
    for j in range(CHUNKS):

        @pl.when(s == 0)
        def _():
            load_patches(j).wait()

        @pl.when(s > 0)
        def _():
            hop_forward(j).wait_recv()

        load_wq(j).wait()
        wide = hbuf[j].astype(F32)
        squares = squares + fold(wide * wide)
        scaled = (wide * gain[:, j * CW : (j + 1) * CW]).astype(BF16)
        for i in range(3):
            part = nn(scaled, wq[j * CW : (j + 1) * CW, i * HW : (i + 1) * HW])
            if j == 0:
                pacc[:, i * HW : (i + 1) * HW] = part
            else:
                pacc[:, i * HW : (i + 1) * HW] += part
    spread = lax.rsqrt(jnp.sum(squares, axis=-1, keepdims=True) * (1.0 / VD) + 1e-6)
    rs[...] = spread
    packed[...] = (pacc[...] * spread).astype(BF16)
    load_win.wait()
    ids = jnp.broadcast_to(win[...].astype(F32), (ROWS, ROWS))
    same = ids.T == ids

    for h in range(HEADS):
        lo, t0, t1 = head_span(h)
        q = packed[:, t0:t1]
        k = masked(packed[:, HW + t0 : HW + t1], h)
        scores = nt(k, q) * SCALE
        scores = jnp.where(same, scores, -1e30)
        top = jnp.max(scores, axis=0, keepdims=True)
        e = jnp.exp(scores - top)
        p = e / jnp.sum(e, axis=0, keepdims=True)
        pt32[h] = p
        ptb[h] = p.astype(BF16)
    for h in range(HEADS):
        lo, t0, t1 = head_span(h)
        v = masked(packed[:, 2 * HW + t0 : 2 * HW + t1], h)
        add_head(acc, h, tn(ptb[h], v))
    att[...] = acc[...].astype(BF16)
    load_wo.wait()
    pl.semaphore_wait(barrier, (NM - 1) + (NZ - 1) + 2)

    def project(j):
        hout[j] = (hbuf[j].astype(F32) + nn(att[...], wo[:, j * CW : (j + 1) * CW])).astype(BF16)

    chip = m // 2
    core = lax.rem(m, 2)
    sibling = chip * 2 + 1 - core

    def gather_copy(which, slot, i, to):
        lanes = mp_lanes(slot)
        if which == 0:
            return remote(ngt.at[:, lanes], ngt.at[:, lanes], ns.at[i], nr.at[i], {"mp": to})
        return remote(atg.at[lanes, :], atg.at[lanes, :], as_.at[i], ar.at[i], {"mp": to})

    def across(d):
        return lax.rem(chip + d, NM // 2) * 2 + core

    def gather_start():
        for j in range(CHUNKS):
            wide = hbuf[j].astype(F32) * rs[...] * gain[:, j * CW : (j + 1) * CW]
            ngt[j * CW : (j + 1) * CW, mp_lanes(m)] = wide.astype(BF16).T
        atg[mp_lanes(m), :] = att[...]
        for w in range(2):
            for d in range(1, NM // 2):
                gather_copy(w, m, d, across(d)).start()
            gather_copy(w, m, 0, sibling).start()

    def gather_forward():
        for d in range(1, NM // 2):
            source = across(NM // 2 - d)
            for w in range(2):
                gather_copy(w, source, d, across(d)).wait_recv()
                gather_copy(w, source, NM // 2 - 1 + d, sibling).start()

    def gather_finish(w):
        gather_copy(w, sibling, 0, sibling).wait_recv()
        for d in range(1, NM // 2):
            source = lax.rem(chip + NM // 2 - d, NM // 2) * 2 + 1 - core
            gather_copy(w, source, NM // 2 - 1 + d, sibling).wait_recv()

    @pl.when(s < NS - 1)
    def _():
        for j in range(CHUNKS):
            project(j)
            hop_forward(j).start()

    gather_start()

    @pl.when(s < NS - 2)
    def _():
        gather_forward()

    def column_copy(which, d):
        to = lax.rem(m + d, NM)
        rows = pl.ds(pl.multiple_of(to * 256, 256), 256)
        lanes = mp_lanes(m)
        if which == 0:
            return remote(dpt.at[rows], dpg.at[:, lanes], ds.at[d], dr.at[d], {"mp": to})
        return remote(gperm.at[rows], gpg.at[:, lanes], ps.at[d], pr.at[d], {"mp": to})

    def columns_q():
        dpt[0 : 3 * HW, :] = dp[...].T
        for d in range(1, NM):
            column_copy(0, d).start()
        dpg[:, mp_lanes(m)] = dpt[pl.ds(pl.multiple_of(m * 256, 256), 256), :]

    def turn_g(j):
        gt32[j * CW : (j + 1) * CW, :] = gbuf[j].astype(F32).T

    def columns_g():
        for i in range(NM):
            for j in range(NZ):
                first = FR * (NM * j + i)
                gperm[i * 256 + j * 32 : i * 256 + j * 32 + 32, :] = gt32[first : first + 32, :].astype(BF16)
        for d in range(1, NM):
            column_copy(1, d).start()
        gpg[:, mp_lanes(m)] = gperm[pl.ds(pl.multiple_of(m * 256, 256), 256), :]

    for j in range(CHUNKS):

        @pl.when(s == NS - 1)
        def _():
            load_cot(j).wait()

        @pl.when(s < NS - 1)
        def _():
            hop_back(j).wait_recv()

        part = nt(gbuf[j], wo[:, j * CW : (j + 1) * CW])
        if j == 0:
            dacc[...] = part
        else:
            dacc[...] += part

        @pl.when(s == 0)
        def _():
            turn_g(j)

    datt[...] = dacc[...].astype(BF16)

    @pl.when(s == 0)
    def _():
        columns_g()

    for h in range(HEADS):
        lo, t0, t1 = head_span(h)
        q = masked(packed[:, t0:t1], h)
        k = masked(packed[:, HW + t0 : HW + t1], h)
        v = masked(packed[:, 2 * HW + t0 : 2 * HW + t1], h)
        da = datt[:, t0:t1]
        dprob = nt(v, da).astype(BF16).astype(F32)
        p = pt32[h]
        dsc = p * (dprob - jnp.sum(p * dprob, axis=0, keepdims=True))
        dsc = (dsc * SCALE).astype(BF16)
        add_head(acc, h, tn(dsc, k))
        add_head(acc2, h, nn(dsc, q))
        add_head(acc3, h, nn(ptb[h], masked(da, h)))
    dp[:, 0:HW] = acc[...].astype(BF16)
    dp[:, HW : 2 * HW] = acc2[...].astype(BF16)
    dp[:, 2 * HW : 3 * HW] = acc3[...].astype(BF16)

    @pl.when(s == 0)
    def _():
        columns_q()

    inner = jnp.zeros((ROWS, 128), F32)
    for j in range(CHUNKS):
        dn = nt(dp[...], wq[j * CW : (j + 1) * CW, :]).astype(BF16).astype(F32)
        wide = hbuf[j].astype(F32)
        up = dn * gain[:, j * CW : (j + 1) * CW]
        lifted[j] = up
        inner = inner + fold(up * wide)
        dgain[0, :, j * CW : (j + 1) * CW] = jnp.sum(dn * (wide * rs[...]), axis=0, keepdims=True)
    spread = rs[...]
    pull = jnp.sum(inner, axis=-1, keepdims=True) * (1.0 / VD) * (spread * spread * spread)
    for j in range(CHUNKS):
        back = gbuf[j].astype(F32) + spread * lifted[j] - hbuf[j].astype(F32) * pull
        gout[j] = back.astype(BF16)

        @pl.when(s > 0)
        def _():
            hop_back(j).start()

    def store_act(j):
        return pltpu.make_async_copy(hout.at[j], act.at[:, cols_of(j)], o_sem.at[j])

    def store_gin(j):
        return pltpu.make_async_copy(gout.at[j], gin.at[:, cols_of(j)], o_sem.at[CHUNKS + j])

    for j in range(CHUNKS):
        store_gin(j).start()

    @pl.when(s > 0)
    def _():
        columns_q()
        for j in range(CHUNKS):
            turn_g(j)
        columns_g()

    @pl.when(s == NS - 1)
    def _():
        for j in range(CHUNKS):
            project(j)

    @pl.when(s >= NS - 2)
    def _():
        gather_forward()

    for j in range(CHUNKS):
        store_act(j).start()

    def gain_mp(d):
        return remote(dgain.at[0], dgrecv.at[d], vs.at[d], vr.at[d], {"mp": lax.rem(m + d, NM)})

    def gain_dp(d):
        return remote(dgz.at[0], dgzrecv.at[d], us.at[d], ur.at[d], {"dp": lax.rem(z + d, NZ)})

    for d in range(1, NM):
        gain_mp(d).start()

    def chunk_q(k):
        rows = pl.ds(pl.multiple_of(k * ZR, 16), ZR)
        return nt(ngt[rows, :], dpg[...])

    def chunk_o(k):
        rows = pl.ds(pl.multiple_of(k * 32, 32), 32)
        return nn(gpg[rows, :], atg[...])

    steps = (NZ - 1, 1, NZ - 2, 2, NZ - 1, 1, NZ - 2, 2)
    owners = (NZ - 3, 3, 4, 4, NZ - 1, 1, NZ - 2, 2)

    def peer(i):
        return {"dp": lax.rem(z + steps[i], NZ)}

    def tree_q(i):
        if i == 2 or i == 3:
            half = pl.ds(0, ZR // 2)
            return remote(sq.at[i, half], zq.at[i, half], qs.at[i], qr.at[i], peer(i))
        return remote(sq.at[i], zq.at[i], qs.at[i], qr.at[i], peer(i))

    def tree_o(i):
        if i == 2 or i == 3:
            half = pl.ds(0, 16)
            return remote(so.at[i, half], zo.at[i, half], os_.at[i], or_.at[i], peer(i))
        return remote(so.at[i], zo.at[i], os_.at[i], or_.at[i], peer(i))

    def whose(i):
        return lax.rem(z + owners[i], NZ)

    def leaf(i, chunk, buf, copy, rows):
        if i == 2:
            value = chunk(whose(2)).astype(BF16)
            buf[2, 0 : rows // 2] = value[0 : rows // 2]
            buf[3, 0 : rows // 2] = value[rows // 2 : rows]
            copy(2).start()
            copy(3).start()
        else:
            buf[i] = chunk(whose(i)).astype(BF16)
            copy(i).start()

    def branch(i, chunk, buf, got, copy, rows, hold):
        hold[...] = chunk(whose(i))
        copy(i - 6).wait_recv()
        hold[...] += got[i - 6].astype(F32)
        copy(i - 4).wait_recv()
        if i == 6:
            hold[0 : rows // 2] += got[2, 0 : rows // 2].astype(F32)
        else:
            hold[rows // 2 : rows] += got[3, 0 : rows // 2].astype(F32)
        buf[i] = hold[...].astype(BF16)
        copy(i).start()

    gather_finish(1)
    for d in range(1, NM):
        column_copy(1, d).wait_recv()
    for i in (2, 0, 1, 4, 5):
        leaf(i, chunk_o, so, tree_o, 32)

    gather_finish(0)
    for d in range(1, NM):
        column_copy(0, d).wait_recv()
    for i in (2, 0, 1):
        leaf(i, chunk_q, sq, tree_q, ZR)

    for i in (6, 7):
        branch(i, chunk_o, so, zo, tree_o, 32, ro)
    for i in (4, 5):
        leaf(i, chunk_q, sq, tree_q, ZR)

    sum_gain = dgain[0]
    for d in range(1, NM):
        gain_mp(d).wait_recv()
        sum_gain = sum_gain + dgrecv[d]
    dgz[0] = sum_gain
    for d in range(1, NZ):
        gain_dp(d).start()

    for i in (6, 7):
        branch(i, chunk_q, sq, zq, tree_q, ZR, rq.at[0:ZR])

    ro[...] = chunk_o(z)
    for i in (4, 5, 6, 7):
        tree_o(i).wait_recv()
        ro[...] += zo[i].astype(F32)
    out_o[:, 0, :] = ro[0:FR, :]

    rq[0:ZR, :] = chunk_q(z)
    for i in (4, 5, 6, 7):
        tree_q(i).wait_recv()
        rq[0:ZR, :] += zq[i].astype(F32)

    def piece(d):
        return remote(fin.at[lax.rem(m + d, NM)], finrecv.at[m], fs.at[d], fr.at[d], {"mp": lax.rem(m + d, NM)})

    for i in range(NM):
        if FR * i + 24 <= ZR:
            fin[i] = rq[FR * i : FR * i + 24, :]
        else:
            fin[i, 0:FR] = rq[FR * i : FR * i + FR, :]
            fin[i, FR:24] = jnp.zeros((24 - FR, 256), F32)
    for d in range(1, NM):
        piece(d).start()
    finrecv[m] = fin[m]

    sum_gain = dgz[0]
    for d in range(1, NZ):
        gain_dp(d).wait_recv()
        sum_gain = sum_gain + dgzrecv[d]
    out_gain[...] = sum_gain

    @pl.when(s < NS - 1)
    def _():
        for j in range(CHUNKS):
            hop_forward(j).wait_send()

    @pl.when(s > 0)
    def _():
        for j in range(CHUNKS):
            hop_back(j).wait_send()

    for i in range(NM - 1):
        for w in range(2):
            gather_copy(w, m, i, sibling).wait_send()
    for d in range(1, NM):
        for w in range(2):
            column_copy(w, d).wait_send()
        gain_mp(d).wait_send()
    for d in range(1, NZ):
        gain_dp(d).wait_send()
    for i in range(8):
        tree_q(i).wait_send()
        tree_o(i).wait_send()
    for j in range(CHUNKS):
        store_act(j).wait()
        store_gin(j).wait()

    for d in range(1, NM):
        source = lax.rem(m + NM - d, NM)
        remote(fin.at[source], finrecv.at[source], fs.at[d], fr.at[d], {"mp": source}).wait_recv()
    for i in range(NM):
        wide = min(256, 3 * HW - 256 * i)
        out_q[:, 0, 256 * i : 256 * i + wide] = finrecv[i, 0:FR, 0:wide]
    for d in range(1, NM):
        piece(d).wait_send()


def finish(act, gin, out_q, out_o, gain, act2, gin2, out_q2, out_o2, gain2, a, b, c, d, sem):
    there = ((act, a), (gin, b), (out_q, c), (out_o, d))
    back = ((a, act2), (b, gin2), (c, out_q2), (d, out_o2))
    reads = [pltpu.make_async_copy(x, y, sem.at[i]) for i, (x, y) in enumerate(there)]
    writes = [pltpu.make_async_copy(x, y, sem.at[4 + i]) for i, (x, y) in enumerate(back)]
    for r in reads:
        r.start()
    place = (lax.axis_index("dp") * NM + lax.axis_index("mp")) * FR
    rows = jnp.broadcast_to(gain[...], (8, VD))
    gain2[...] = pltpu.roll(rows, lax.rem(VD - place, VD), 1)[0:1, 0:FR]
    for r, w in zip(reads, writes):
        r.wait()
        w.start()
    for w in writes:
        w.wait()


def on_device(patches, windows, gain, w_qkv, w_out, cotangent):
    vmem = pl.BlockSpec(memory_space=pltpu.VMEM)
    hbm = pl.BlockSpec(memory_space=pl.ANY)
    dma = pltpu.SemaphoreType.DMA
    scratch = [
        pltpu.VMEM((VD, 3 * HW), BF16),
        pltpu.VMEM((HW, VD), BF16),
        pltpu.VMEM((1, ROWS), jnp.int32),
        pltpu.VMEM((1, VD), F32),
        pltpu.VMEM((CHUNKS, ROWS, CW), BF16),
        pltpu.VMEM((CHUNKS, ROWS, CW), BF16),
        pltpu.VMEM((CHUNKS, ROWS, CW), BF16),
        pltpu.VMEM((CHUNKS, ROWS, CW), BF16),
        pltpu.VMEM((ROWS, 3 * HW), F32),
        pltpu.VMEM((ROWS, HW), F32),
        pltpu.VMEM((ROWS, 3 * HW), BF16),
        pltpu.VMEM((HEADS, ROWS, ROWS), F32),
        pltpu.VMEM((HEADS, ROWS, ROWS), BF16),
        pltpu.VMEM((ROWS, HW), BF16),
        pltpu.VMEM((ROWS, HW), F32),
        pltpu.VMEM((ROWS, HW), F32),
        pltpu.VMEM((ROWS, HW), F32),
        pltpu.VMEM((ROWS, HW), BF16),
        pltpu.VMEM((ROWS, 3 * HW), BF16),
        pltpu.VMEM((CHUNKS, ROWS, CW), F32),
        pltpu.VMEM((ROWS, 1), F32),
        pltpu.VMEM((VD, NM * ROWS), BF16),
        pltpu.VMEM((NM * ROWS, HW), BF16),
        pltpu.VMEM((2048, ROWS), BF16),
        pltpu.VMEM((VD + 32, ROWS), F32),
        pltpu.VMEM((2048, ROWS), BF16),
        pltpu.VMEM((256, NM * ROWS), BF16),
        pltpu.VMEM((256, NM * ROWS), BF16),
        pltpu.VMEM((1, 1, VD), F32),
        pltpu.VMEM((NM, 1, VD), F32),
        pltpu.VMEM((1, 1, VD), F32),
        pltpu.VMEM((NZ, 1, VD), F32),
        pltpu.VMEM((ZR, 256), F32),
        pltpu.VMEM((32, HW), F32),
        pltpu.VMEM((8, ZR, 256), BF16),
        pltpu.VMEM((8, 32, HW), BF16),
        pltpu.VMEM((8, ZR, 256), BF16),
        pltpu.VMEM((8, 32, HW), BF16),
        pltpu.VMEM((NM, 24, 256), F32),
        pltpu.VMEM((NM, 24, 256), F32),
        dma((8,)), dma((CHUNKS,)), dma((2 * CHUNKS,)),
        dma((CHUNKS,)), dma((CHUNKS,)), dma((CHUNKS,)), dma((CHUNKS,)),
    ] + [dma((8,)) for _ in range(18)]
    shapes = (
        jax.ShapeDtypeStruct((ROWS, VD), BF16),
        jax.ShapeDtypeStruct((ROWS, VD), BF16),
        jax.ShapeDtypeStruct((FR, 1, 3 * HW), F32),
        jax.ShapeDtypeStruct((FR, 1, HW), F32),
        jax.ShapeDtypeStruct((1, VD), F32),
    )
    results = pl.pallas_call(
        kernel,
        out_shape=shapes,
        in_specs=[hbm] * 6,
        out_specs=(hbm, hbm, vmem, vmem, vmem),
        scratch_shapes=scratch,
        compiler_params=pltpu.CompilerParams(
            collective_id=0, has_side_effects=True, vmem_limit_bytes=60 * 1024 * 1024
        ),
    )(patches[0], cotangent[0], windows, gain, w_qkv[0], w_out[0])
    act, gin, out_q, out_o, own_gain = pl.pallas_call(
        finish,
        out_shape=shapes[:4] + (jax.ShapeDtypeStruct((1, FR), F32),),
        in_specs=[hbm] * 4 + [vmem],
        out_specs=(hbm,) * 4 + (vmem,),
        scratch_shapes=[pltpu.VMEM(x.shape, x.dtype) for x in shapes[:4]] + [dma((8,))],
        compiler_params=pltpu.CompilerParams(vmem_limit_bytes=60 * 1024 * 1024),
    )(*results)
    return (
        act[None, None],
        gin[None, None],
        out_q.transpose(1, 0, 2),
        out_o.transpose(1, 2, 0),
        own_gain,
    )


def solution(mesh):
    in_specs = (
        P(None, ("dp", "mp"), None),
        P(None, ("dp", "mp")),
        P("section", None),
        P("section", None, None),
        P("section", None, None),
        P(None, ("dp", "mp"), None),
    )
    out_specs = (
        P("section", None, ("dp", "mp"), None),
        P("section", None, ("dp", "mp"), None),
        P("section", ("dp", "mp"), None),
        P("section", None, ("dp", "mp")),
        P("section", ("dp", "mp")),
    )
    return jax.shard_map(
        on_device, mesh=mesh, in_specs=in_specs, out_specs=out_specs, check_vma=False
    )
```

```python
import jax
import jax.numpy as jnp
from jax import lax
from jax.experimental import pallas as pl
from jax.experimental.pallas import tpu as pltpu
from jax.sharding import PartitionSpec as P

HEAD = 80
HEADS = 8
ROWS = 128
VD = 1280
HW = 640
NM = 8
NZ = 8
NS = 4
CHUNKS = 5
CW = VD // CHUNKS
ZR = VD // NZ
FR = ZR // NM
SCALE = HEAD**-0.5
MESH = pl.DeviceIdType.MESH
F32 = jnp.float32
BF16 = jnp.bfloat16


def nt(a, b):
    return lax.dot_general(a, b, (((1,), (1,)), ((), ())), preferred_element_type=F32)


def nn(a, b):
    return lax.dot_general(a, b, (((1,), (0,)), ((), ())), preferred_element_type=F32)


def tn(a, b):
    return lax.dot_general(a, b, (((0,), (0,)), ((), ())), preferred_element_type=F32)


def tiles_of(h):
    return range(HEAD * h // 128, -(-(HEAD * h + HEAD) // 128))


def heads_of(t):
    return [h for h in range(HEADS) if t in tiles_of(h)]


PAIRS = [(t, h) for t in range(HW // 128) for h in heads_of(t)]


def pair_rows(t):
    first = PAIRS.index((t, heads_of(t)[0]))
    return slice(first * ROWS, (first + len(heads_of(t))) * ROWS)


def head_rows(t):
    heads = heads_of(t)
    return slice(heads[0] * ROWS, (heads[-1] + 1) * ROWS)


def gathered(stack, h):
    parts = []
    for t in tiles_of(h):
        i = PAIRS.index((t, h))
        parts.append(stack[i * ROWS : (i + 1) * ROWS, :])
    return parts[0] if len(parts) == 1 else jnp.concatenate(parts, axis=1)


def span(h):
    tiles = tiles_of(h)
    return tiles[0] * 128, tiles[-1] * 128 + 128


def kernel(
    patches, cot, win_hbm, gain_hbm, wq_hbm, wo_hbm,
    act, gin, out_q, out_o, out_gain,
    wq, wo, win, gain, hbuf, gbuf, hout, gout, pacc, dacc, packed, pt32, ptb, ptl, att, mk, qm, km, vm, dam, dsr, dsl,
    datt, dp, lifted, rs, wqt, oq, oo,
    ngt, atg, gt32, gperm, dpg, gpg, dgain, dgrecv, dgz, dgzrecv,
    rq, ro, sq, so, zq, zo, fin, finrecv,
    w_sem, in_sem, o_sem, hs, hr, gs, gr, ns, nr, as_, ar, ds, dr, ps, pr, vs, vr, us, ur, qs, qr, os_, or_, fs, fr,
):
    s = lax.axis_index("section")
    m = lax.axis_index("mp")
    z = lax.axis_index("dp")

    def cols_of(j):
        return pl.ds(j * CW, CW)

    def load_patches(j):
        return pltpu.make_async_copy(patches.at[:, cols_of(j)], hbuf.at[j], in_sem.at[j])

    def load_cot(j):
        return pltpu.make_async_copy(cot.at[:, cols_of(j)], gbuf.at[j], in_sem.at[j])

    def load_wq(j):
        return pltpu.make_async_copy(wq_hbm.at[cols_of(j)], wq.at[cols_of(j)], w_sem.at[j])

    load_wo = pltpu.make_async_copy(wo_hbm, wo, w_sem.at[5])
    load_gain = pltpu.make_async_copy(gain_hbm, gain, w_sem.at[6])
    load_win = pltpu.make_async_copy(win_hbm, win, w_sem.at[7])

    load_gain.start()

    @pl.when(s == 0)
    def _():
        for j in range(CHUNKS):
            load_patches(j).start()

    for j in range(CHUNKS):
        load_wq(j).start()
    load_win.start()
    load_wo.start()

    @pl.when(s == NS - 1)
    def _():
        for j in range(CHUNKS):
            load_cot(j).start()

    barrier = pltpu.get_barrier_semaphore()
    for d in range(1, NM):
        pl.semaphore_signal(barrier, inc=1, device_id={"mp": lax.rem(m + d, NM)}, device_id_type=MESH)
    for d in range(1, NZ):
        pl.semaphore_signal(barrier, inc=1, device_id={"dp": lax.rem(z + d, NZ)}, device_id_type=MESH)
    for d in (1, NS - 1):
        pl.semaphore_signal(barrier, inc=1, device_id={"section": lax.rem(s + d, NS)}, device_id_type=MESH)

    dp[:, 3 * HW : 2048] = jnp.zeros((ROWS, 2048 - 3 * HW), BF16)
    rq[ZR : ZR + 32, :] = jnp.zeros((32, 256), F32)
    for i, (t, h) in enumerate(PAIRS):
        cols = lax.broadcasted_iota(jnp.int32, (ROWS, 128), 1) + t * 128
        inside = (cols >= HEAD * h) & (cols < HEAD * h + HEAD)
        mk[i] = jnp.where(inside, 1.0, 0.0).astype(BF16)
    gt32[VD : VD + 32, :] = jnp.zeros((32, ROWS), F32)

    def remote(src, dst, ssem, rsem, where):
        return pltpu.make_async_remote_copy(
            src_ref=src, dst_ref=dst, send_sem=ssem, recv_sem=rsem, device_id=where, device_id_type=MESH
        )

    def hop_forward(j):
        return remote(hout.at[j], hbuf.at[j], hs.at[j], hr.at[j], {"section": lax.rem(s + 1, NS)})

    def hop_back(j):
        return remote(gout.at[j], gbuf.at[j], gs.at[j], gr.at[j], {"section": lax.rem(s + NS - 1, NS)})

    def mp_lanes(i):
        return pl.ds(pl.multiple_of(i * ROWS, ROWS), ROWS)

    def fold(x):
        return x[:, 0:128] + x[:, 128:256]

    load_gain.wait()
    @pl.when(s >= 2)
    def _():
        for j in range(CHUNKS):
            load_wq(j).wait()
            wqt[:, j * CW : (j + 1) * CW] = wq[j * CW : (j + 1) * CW, :].T

    squares = jnp.zeros((ROWS, 128), F32)
    for j in range(CHUNKS):

        @pl.when(s == 0)
        def _():
            load_patches(j).wait()

        @pl.when(s > 0)
        def _():
            hop_forward(j).wait_recv()

        @pl.when(s < 2)
        def _():
            load_wq(j).wait()

        wide = hbuf[j].astype(F32)
        squares = squares + fold(wide * wide)
        scaled = (wide * gain[:, j * CW : (j + 1) * CW]).astype(BF16)
        for i in range(3):
            part = nn(scaled, wq[j * CW : (j + 1) * CW, i * HW : (i + 1) * HW])
            if j == 0:
                pacc[:, i * HW : (i + 1) * HW] = part
            else:
                pacc[:, i * HW : (i + 1) * HW] += part
    spread = lax.rsqrt(jnp.sum(squares, axis=-1, keepdims=True) * (1.0 / VD) + 1e-6)
    rs[...] = spread
    packed[...] = (pacc[...] * spread).astype(BF16)
    load_win.wait()
    ids = jnp.broadcast_to(win[...].astype(F32), (ROWS, ROWS))
    same = ids.T == ids

    for i, (t, h) in enumerate(PAIRS):
        rows = slice(i * ROWS, (i + 1) * ROWS)
        km[rows, :] = packed[:, HW + t * 128 : HW + t * 128 + 128] * mk[i]
        vm[rows, :] = packed[:, 2 * HW + t * 128 : 2 * HW + t * 128 + 128] * mk[i]
    for h in range(HEADS):
        t0, t1 = span(h)
        scores = nt(gathered(km, h), packed[:, t0:t1]) * SCALE
        scores = jnp.where(same, scores, -1e30)
        top = jnp.max(scores, axis=0, keepdims=True)
        e = jnp.exp(scores - top)
        p = e / jnp.sum(e, axis=0, keepdims=True)
        pt32[h] = p
        ptb[h * ROWS : (h + 1) * ROWS, :] = p.astype(BF16)
    for t in range(HW // 128):
        att[:, t * 128 : t * 128 + 128] = tn(ptb[head_rows(t), :], vm[pair_rows(t), :]).astype(BF16)
    load_wo.wait()
    pl.semaphore_wait(barrier, (NM - 1) + (NZ - 1) + 2)

    def project(j):
        hout[j] = (hbuf[j].astype(F32) + nn(att[...], wo[:, j * CW : (j + 1) * CW])).astype(BF16)

    chip = m // 2
    core = lax.rem(m, 2)
    sibling = chip * 2 + 1 - core

    def gather_copy(which, slot, i, to):
        lanes = mp_lanes(slot)
        if which == 0:
            return remote(ngt.at[:, lanes], ngt.at[:, lanes], ns.at[i], nr.at[i], {"mp": to})
        return remote(atg.at[lanes, :], atg.at[lanes, :], as_.at[i], ar.at[i], {"mp": to})

    def across(d):
        return lax.rem(chip + d, NM // 2) * 2 + core

    def gather_start():
        for j in range(CHUNKS):
            wide = hbuf[j].astype(F32) * rs[...] * gain[:, j * CW : (j + 1) * CW]
            ngt[j * CW : (j + 1) * CW, mp_lanes(m)] = wide.astype(BF16).T
        atg[mp_lanes(m), :] = att[...]
        for w in range(2):
            for d in range(1, NM // 2):
                gather_copy(w, m, d, across(d)).start()
            gather_copy(w, m, 0, sibling).start()

    def gather_forward():
        for d in range(1, NM // 2):
            source = across(NM // 2 - d)
            for w in range(2):
                gather_copy(w, source, d, across(d)).wait_recv()
                gather_copy(w, source, NM // 2 - 1 + d, sibling).start()

    def gather_finish(w):
        gather_copy(w, sibling, 0, sibling).wait_recv()
        for d in range(1, NM // 2):
            source = lax.rem(chip + NM // 2 - d, NM // 2) * 2 + 1 - core
            gather_copy(w, source, NM // 2 - 1 + d, sibling).wait_recv()

    @pl.when(s < NS - 1)
    def _():
        for j in range(CHUNKS):
            project(j)
            hop_forward(j).start()

    gather_start()

    @pl.when(s < NS - 2)
    def _():
        gather_forward()

    def turn_weights():
        for j in range(CHUNKS):
            wqt[:, j * CW : (j + 1) * CW] = wq[j * CW : (j + 1) * CW, :].T

    @pl.when(s < 2)
    def _():
        turn_weights()

    for i, (t, h) in enumerate(PAIRS):
        qm[i * ROWS : (i + 1) * ROWS, :] = packed[:, t * 128 : t * 128 + 128] * mk[i]
    for h in range(HEADS):
        ptl[:, h * ROWS : (h + 1) * ROWS] = ptb[h * ROWS : (h + 1) * ROWS, :]

    def column_copy(which, d):
        to = lax.rem(m + d, NM)
        rows = pl.ds(pl.multiple_of(to * 256, 256), 256)
        lanes = mp_lanes(m)
        if which == 0:
            return remote(dp.at[:, rows], dpg.at[lanes, :], ds.at[d], dr.at[d], {"mp": to})
        return remote(gperm.at[rows], gpg.at[:, lanes], ps.at[d], pr.at[d], {"mp": to})

    def columns_q():
        for d in range(1, NM):
            column_copy(0, d).start()
        dpg[mp_lanes(m), :] = dp[:, pl.ds(pl.multiple_of(m * 256, 256), 256)]

    def turn_g(j):
        gt32[j * CW : (j + 1) * CW, :] = gbuf[j].astype(F32).T

    def columns_g():
        for i in range(NM):
            for j in range(NZ):
                first = FR * (NM * j + i)
                gperm[i * 256 + j * 32 : i * 256 + j * 32 + 32, :] = gt32[first : first + 32, :].astype(BF16)
        for d in range(1, NM):
            column_copy(1, d).start()
        gpg[:, mp_lanes(m)] = gperm[pl.ds(pl.multiple_of(m * 256, 256), 256), :]

    for j in range(CHUNKS):

        @pl.when(s == NS - 1)
        def _():
            load_cot(j).wait()

        @pl.when(s < NS - 1)
        def _():
            hop_back(j).wait_recv()

        part = nt(gbuf[j], wo[:, j * CW : (j + 1) * CW])
        if j == 0:
            dacc[...] = part
        else:
            dacc[...] += part

        @pl.when(s == 0)
        def _():
            turn_g(j)

    datt[...] = dacc[...].astype(BF16)

    @pl.when(s == 0)
    def _():
        columns_g()

    for i, (t, h) in enumerate(PAIRS):
        dam[i * ROWS : (i + 1) * ROWS, :] = datt[:, t * 128 : t * 128 + 128] * mk[i]
    for h in range(HEADS):
        t0, t1 = span(h)
        dprob = nt(gathered(vm, h), datt[:, t0:t1]).astype(BF16).astype(F32)
        p = pt32[h]
        dsc = p * (dprob - jnp.sum(p * dprob, axis=0, keepdims=True))
        dsc = (dsc * SCALE).astype(BF16)
        dsr[h * ROWS : (h + 1) * ROWS, :] = dsc
        dsl[:, h * ROWS : (h + 1) * ROWS] = dsc
    for t in range(HW // 128):
        c = t * 128
        dp[:, 2 * HW + c : 2 * HW + c + 128] = nn(ptl[:, head_rows(t)], dam[pair_rows(t), :]).astype(BF16)
    for t in range(HW // 128):
        c = t * 128
        dp[:, HW + c : HW + c + 128] = nn(dsl[:, head_rows(t)], qm[pair_rows(t), :]).astype(BF16)
        dp[:, c : c + 128] = tn(dsr[head_rows(t), :], km[pair_rows(t), :]).astype(BF16)

    @pl.when(s == 0)
    def _():
        columns_q()

    inner = jnp.zeros((ROWS, 128), F32)
    for j in range(CHUNKS):
        dn = nn(dp[:, 0 : 3 * HW], wqt[:, j * CW : (j + 1) * CW]).astype(BF16).astype(F32)
        wide = hbuf[j].astype(F32)
        up = dn * gain[:, j * CW : (j + 1) * CW]
        lifted[j] = up
        inner = inner + fold(up * wide)
        dgain[0, :, j * CW : (j + 1) * CW] = jnp.sum(dn * (wide * rs[...]), axis=0, keepdims=True)
    spread = rs[...]
    pull = jnp.sum(inner, axis=-1, keepdims=True) * (1.0 / VD) * (spread * spread * spread)
    for j in range(CHUNKS):
        back = gbuf[j].astype(F32) + spread * lifted[j] - hbuf[j].astype(F32) * pull
        gout[j] = back.astype(BF16)

        @pl.when(s > 0)
        def _():
            hop_back(j).start()

    def store_act(j):
        return pltpu.make_async_copy(hout.at[j], act.at[:, cols_of(j)], o_sem.at[j])

    def store_gin(j):
        return pltpu.make_async_copy(gout.at[j], gin.at[:, cols_of(j)], o_sem.at[CHUNKS + j])

    for j in range(CHUNKS):
        store_gin(j).start()

    @pl.when(s > 0)
    def _():
        columns_q()
        for j in range(CHUNKS):
            turn_g(j)
        columns_g()

    @pl.when(s == NS - 1)
    def _():
        for j in range(CHUNKS):
            project(j)

    @pl.when(s >= NS - 2)
    def _():
        gather_forward()

    for j in range(CHUNKS):
        store_act(j).start()

    def gain_mp(d):
        return remote(dgain.at[0], dgrecv.at[d], vs.at[d], vr.at[d], {"mp": lax.rem(m + d, NM)})

    def gain_dp(d):
        return remote(dgz.at[0], dgzrecv.at[d], us.at[d], ur.at[d], {"dp": lax.rem(z + d, NZ)})

    for d in range(1, NM):
        gain_mp(d).start()

    def chunk_q(k):
        rows = pl.ds(pl.multiple_of(k * ZR, 16), ZR)
        return nn(ngt[rows, :], dpg[...])

    def chunk_o(k):
        rows = pl.ds(pl.multiple_of(k * 32, 32), 32)
        return nn(gpg[rows, :], atg[...])

    steps = (NZ - 1, 1, NZ - 2, 2, NZ - 1, 1, NZ - 2, 2)
    owners = (NZ - 3, 3, 4, 4, NZ - 1, 1, NZ - 2, 2)

    def peer(i):
        return {"dp": lax.rem(z + steps[i], NZ)}

    def tree_q(i):
        if i == 2 or i == 3:
            half = pl.ds(0, ZR // 2)
            return remote(sq.at[i, half], zq.at[i, half], qs.at[i], qr.at[i], peer(i))
        return remote(sq.at[i], zq.at[i], qs.at[i], qr.at[i], peer(i))

    def tree_o(i):
        if i == 2 or i == 3:
            half = pl.ds(0, 16)
            return remote(so.at[i, half], zo.at[i, half], os_.at[i], or_.at[i], peer(i))
        return remote(so.at[i], zo.at[i], os_.at[i], or_.at[i], peer(i))

    def whose(i):
        return lax.rem(z + owners[i], NZ)

    def leaf(i, chunk, buf, copy, rows):
        if i == 2:
            value = chunk(whose(2)).astype(BF16)
            buf[2, 0 : rows // 2] = value[0 : rows // 2]
            buf[3, 0 : rows // 2] = value[rows // 2 : rows]
            copy(2).start()
            copy(3).start()
        else:
            buf[i] = chunk(whose(i)).astype(BF16)
            copy(i).start()

    def branch(i, chunk, buf, got, copy, rows, hold):
        hold[...] = chunk(whose(i))
        copy(i - 6).wait_recv()
        hold[...] += got[i - 6].astype(F32)
        copy(i - 4).wait_recv()
        if i == 6:
            hold[0 : rows // 2] += got[2, 0 : rows // 2].astype(F32)
        else:
            hold[rows // 2 : rows] += got[3, 0 : rows // 2].astype(F32)
        buf[i] = hold[...].astype(BF16)
        copy(i).start()

    gather_finish(1)
    for d in range(1, NM):
        column_copy(1, d).wait_recv()
    for i in (2, 0, 1, 4, 5):
        leaf(i, chunk_o, so, tree_o, 32)

    gather_finish(0)
    for d in range(1, NM):
        column_copy(0, d).wait_recv()
    for i in (2, 0, 1):
        leaf(i, chunk_q, sq, tree_q, ZR)

    for i in (6, 7):
        branch(i, chunk_o, so, zo, tree_o, 32, ro)
    for i in (4, 5):
        leaf(i, chunk_q, sq, tree_q, ZR)

    for i in (6, 7):
        branch(i, chunk_q, sq, zq, tree_q, ZR, rq.at[0:ZR])

    sum_gain = dgain[0]
    for d in range(1, NM):
        gain_mp(d).wait_recv()
        sum_gain = sum_gain + dgrecv[d]
    dgz[0] = sum_gain
    for d in range(1, NZ):
        gain_dp(d).start()

    ro[...] = chunk_o(z)
    for i in (4, 5, 6, 7):
        tree_o(i).wait_recv()
        ro[...] += zo[i].astype(F32)
    oo[:, 0, :] = ro[0:FR, :]
    store_o = pltpu.make_async_copy(oo, out_o, o_sem.at[2 * CHUNKS])
    store_o.start()

    rq[0:ZR, :] = chunk_q(z)
    for i in (4, 5, 6, 7):
        tree_q(i).wait_recv()
        rq[0:ZR, :] += zq[i].astype(F32)

    def piece(d):
        return remote(fin.at[lax.rem(m + d, NM)], finrecv.at[m], fs.at[d], fr.at[d], {"mp": lax.rem(m + d, NM)})

    for i in range(NM):
        fin[i] = rq[FR * i : FR * i + 32, :].astype(BF16)
    for d in range(1, NM):
        piece(d).start()
    finrecv[m] = fin[m]

    sum_gain = dgz[0]
    for d in range(1, NZ):
        gain_dp(d).wait_recv()
        sum_gain = sum_gain + dgzrecv[d]
    dgz[1] = sum_gain
    store_gain = pltpu.make_async_copy(dgz.at[1], out_gain, o_sem.at[2 * CHUNKS + 1])
    store_gain.start()

    @pl.when(s < NS - 1)
    def _():
        for j in range(CHUNKS):
            hop_forward(j).wait_send()

    @pl.when(s > 0)
    def _():
        for j in range(CHUNKS):
            hop_back(j).wait_send()

    for i in range(NM - 1):
        for w in range(2):
            gather_copy(w, m, i, sibling).wait_send()
    for d in range(1, NM):
        for w in range(2):
            column_copy(w, d).wait_send()
        gain_mp(d).wait_send()
    for d in range(1, NZ):
        gain_dp(d).wait_send()
    for i in range(8):
        tree_q(i).wait_send()
        tree_o(i).wait_send()
    for j in range(CHUNKS):
        store_act(j).wait()
        store_gin(j).wait()

    for d in range(1, NM):
        source = lax.rem(m + NM - d, NM)
        remote(fin.at[source], finrecv.at[source], fs.at[d], fr.at[d], {"mp": source}).wait_recv()
    for i in range(NM):
        wide = min(256, 3 * HW - 256 * i)
        oq[:, 0, 256 * i : 256 * i + wide] = finrecv[i, :, 0:wide].astype(F32)[0:FR]
    store_q = pltpu.make_async_copy(oq, out_q, o_sem.at[2 * CHUNKS + 2])
    store_q.start()
    for d in range(1, NM):
        piece(d).wait_send()
    store_o.wait()
    store_gain.wait()
    store_q.wait()


def finish(act, gin, out_q, out_o, gain, act2, gin2, out_q2, out_o2, gain2, a, b, c, d, e, f, sem):
    there = ((gain, e), (act, a), (gin, b), (out_q, c), (out_o, d))
    back = ((f, gain2), (a, act2), (b, gin2), (c, out_q2), (d, out_o2))
    reads = [pltpu.make_async_copy(x, y, sem.at[i]) for i, (x, y) in enumerate(there)]
    writes = [pltpu.make_async_copy(x, y, sem.at[5 + i]) for i, (x, y) in enumerate(back)]
    for r in reads:
        r.start()
    place = (lax.axis_index("dp") * NM + lax.axis_index("mp")) * FR
    for i, (r, w) in enumerate(zip(reads, writes)):
        r.wait()
        if i == 0:
            rows = jnp.broadcast_to(e[...], (8, VD))
            f[...] = pltpu.roll(rows, lax.rem(VD - place, VD), 1)[0:1, 0:FR]
        w.start()
    for w in writes:
        w.wait()


def on_device(patches, windows, gain, w_qkv, w_out, cotangent):
    hbm = pl.BlockSpec(memory_space=pl.ANY)
    dma = pltpu.SemaphoreType.DMA
    scratch = [
        pltpu.VMEM((VD, 3 * HW), BF16),
        pltpu.VMEM((HW, VD), BF16),
        pltpu.VMEM((1, ROWS), jnp.int32),
        pltpu.VMEM((1, VD), F32),
        pltpu.VMEM((CHUNKS, ROWS, CW), BF16),
        pltpu.VMEM((CHUNKS, ROWS, CW), BF16),
        pltpu.VMEM((CHUNKS, ROWS, CW), BF16),
        pltpu.VMEM((CHUNKS, ROWS, CW), BF16),
        pltpu.VMEM((ROWS, 3 * HW), F32),
        pltpu.VMEM((ROWS, HW), F32),
        pltpu.VMEM((ROWS, 3 * HW), BF16),
        pltpu.VMEM((HEADS, ROWS, ROWS), F32),
        pltpu.VMEM((HEADS * ROWS, ROWS), BF16),
        pltpu.VMEM((ROWS, HEADS * ROWS), BF16),
        pltpu.VMEM((ROWS, HW), BF16),
        pltpu.VMEM((len(PAIRS), ROWS, 128), BF16),
        pltpu.VMEM((len(PAIRS) * ROWS, 128), BF16),
        pltpu.VMEM((len(PAIRS) * ROWS, 128), BF16),
        pltpu.VMEM((len(PAIRS) * ROWS, 128), BF16),
        pltpu.VMEM((len(PAIRS) * ROWS, 128), BF16),
        pltpu.VMEM((HEADS * ROWS, ROWS), BF16),
        pltpu.VMEM((ROWS, HEADS * ROWS), BF16),
        pltpu.VMEM((ROWS, HW), BF16),
        pltpu.VMEM((ROWS, 2048), BF16),
        pltpu.VMEM((CHUNKS, ROWS, CW), F32),
        pltpu.VMEM((ROWS, 1), F32),
        pltpu.VMEM((3 * HW, VD), BF16),
        pltpu.VMEM((FR, 1, 3 * HW), F32),
        pltpu.VMEM((FR, 1, HW), F32),
        pltpu.VMEM((VD, NM * ROWS), BF16),
        pltpu.VMEM((NM * ROWS, HW), BF16),
        pltpu.VMEM((VD + 32, ROWS), F32),
        pltpu.VMEM((2048, ROWS), BF16),
        pltpu.VMEM((NM * ROWS, 256), BF16),
        pltpu.VMEM((256, NM * ROWS), BF16),
        pltpu.VMEM((1, 1, VD), F32),
        pltpu.VMEM((NM, 1, VD), F32),
        pltpu.VMEM((2, 1, VD), F32),
        pltpu.VMEM((NZ, 1, VD), F32),
        pltpu.VMEM((ZR + 32, 256), F32),
        pltpu.VMEM((32, HW), F32),
        pltpu.VMEM((8, ZR, 256), BF16),
        pltpu.VMEM((8, 32, HW), BF16),
        pltpu.VMEM((8, ZR, 256), BF16),
        pltpu.VMEM((8, 32, HW), BF16),
        pltpu.VMEM((NM, 32, 256), BF16),
        pltpu.VMEM((NM, 32, 256), BF16),
        dma((8,)), dma((CHUNKS,)), dma((2 * CHUNKS + 3,)),
        dma((CHUNKS,)), dma((CHUNKS,)), dma((CHUNKS,)), dma((CHUNKS,)),
    ] + [dma((8,)) for _ in range(18)]
    shapes = (
        jax.ShapeDtypeStruct((ROWS, VD), BF16),
        jax.ShapeDtypeStruct((ROWS, VD), BF16),
        jax.ShapeDtypeStruct((FR, 1, 3 * HW), F32),
        jax.ShapeDtypeStruct((FR, 1, HW), F32),
        jax.ShapeDtypeStruct((1, VD), F32),
    )
    results = pl.pallas_call(
        kernel,
        out_shape=shapes,
        in_specs=[hbm] * 6,
        out_specs=(hbm,) * 5,
        scratch_shapes=scratch,
        compiler_params=pltpu.CompilerParams(
            collective_id=0, has_side_effects=True, vmem_limit_bytes=60 * 1024 * 1024
        ),
    )(patches[0], cotangent[0], windows, gain, w_qkv[0], w_out[0])
    act, gin, out_q, out_o, own_gain = pl.pallas_call(
        finish,
        out_shape=shapes[:4] + (jax.ShapeDtypeStruct((1, FR), F32),),
        in_specs=[hbm] * 5,
        out_specs=(hbm,) * 5,
        scratch_shapes=[pltpu.VMEM(x.shape, x.dtype) for x in shapes] + [pltpu.VMEM((1, FR), F32), dma((10,))],
        compiler_params=pltpu.CompilerParams(vmem_limit_bytes=60 * 1024 * 1024),
    )(*results)
    return (
        act[None, None],
        gin[None, None],
        out_q.transpose(1, 0, 2),
        out_o.transpose(1, 2, 0),
        own_gain,
    )


def solution(mesh):
    in_specs = (
        P(None, ("dp", "mp"), None),
        P(None, ("dp", "mp")),
        P("section", None),
        P("section", None, None),
        P("section", None, None),
        P(None, ("dp", "mp"), None),
    )
    out_specs = (
        P("section", None, ("dp", "mp"), None),
        P("section", None, ("dp", "mp"), None),
        P("section", ("dp", "mp"), None),
        P("section", None, ("dp", "mp")),
        P("section", ("dp", "mp")),
    )
    return jax.shard_map(
        on_device, mesh=mesh, in_specs=in_specs, out_specs=out_specs, check_vma=False
    )
```

```python
import jax
import jax.numpy as jnp
from jax import lax
from jax.experimental import pallas as pl
from jax.experimental.pallas import tpu as pltpu
from jax.sharding import PartitionSpec as P

HEAD = 80
HEADS = 8
ROWS = 128
VD = 1280
HW = 640
NM = 8
NZ = 8
NS = 4
CHUNKS = 5
CW = VD // CHUNKS
FAR = CHUNKS - 1
SENT = (FAR,) + tuple(range(FAR))
HALF = ROWS // 2
ZR = VD // NZ
FR = ZR // NM
SCALE = HEAD**-0.5
MESH = pl.DeviceIdType.MESH
F32 = jnp.float32
BF16 = jnp.bfloat16


def nt(a, b):
    return lax.dot_general(a, b, (((1,), (1,)), ((), ())), preferred_element_type=F32)


def nn(a, b):
    return lax.dot_general(a, b, (((1,), (0,)), ((), ())), preferred_element_type=F32)


def tn(a, b):
    return lax.dot_general(a, b, (((0,), (0,)), ((), ())), preferred_element_type=F32)


def tiles_of(h):
    return range(HEAD * h // 128, -(-(HEAD * h + HEAD) // 128))


def heads_of(t):
    return [h for h in range(HEADS) if t in tiles_of(h)]


PAIRS = [(t, h) for t in range(HW // 128) for h in heads_of(t)]


def pair_rows(t):
    first = PAIRS.index((t, heads_of(t)[0]))
    return slice(first * ROWS, (first + len(heads_of(t))) * ROWS)


def head_rows(t):
    heads = heads_of(t)
    return slice(heads[0] * ROWS, (heads[-1] + 1) * ROWS)


def gathered(stack, h):
    parts = []
    for t in tiles_of(h):
        i = PAIRS.index((t, h))
        parts.append(stack[i * ROWS : (i + 1) * ROWS, :])
    return parts[0] if len(parts) == 1 else jnp.concatenate(parts, axis=1)


def span(h):
    tiles = tiles_of(h)
    return tiles[0] * 128, tiles[-1] * 128 + 128


def kernel(
    patches, cot, win_hbm, gain_hbm, wq_hbm, wo_hbm,
    act, gin, out_q, out_o, out_gain,
    wq, wo, win, gain, hbuf, gbuf, hout, gout, pacc, dacc, packed, pt32, ptb, ptl, att, mk, qm, km, vm, dam, dsr, dsl,
    datt, dp, lifted, rs, wqt, oq, oo, rbuf,
    ngt, atg, gt32, gp32, gperm, dpg, gpg, o32, opad, dgain, dgrecv, dgz, dgzrecv,
    rq, ro, sq, so, zq, zo, fin, finrecv,
    w_sem, in_sem, o_sem, hs, hr, gs, gr, ns, nr, as_, ar, ds, dr, ps, pr, vs, vr, us, ur, qs, qr, os_, or_, fs, fr, ls, lr, ts,
):
    s = lax.axis_index("section")
    m = lax.axis_index("mp")
    z = lax.axis_index("dp")

    def cols_of(j):
        return pl.ds(j * CW, CW)

    def load_patches(j):
        return pltpu.make_async_copy(patches.at[:, cols_of(j)], hbuf.at[j], in_sem.at[j])

    def load_cot(j):
        return pltpu.make_async_copy(cot.at[:, cols_of(j)], gbuf.at[j], in_sem.at[j])

    def load_wq(j):
        return pltpu.make_async_copy(wq_hbm.at[cols_of(j)], wq.at[cols_of(j)], w_sem.at[j])

    load_wo = pltpu.make_async_copy(wo_hbm, wo, w_sem.at[5])
    load_gain = pltpu.make_async_copy(gain_hbm, gain, w_sem.at[6])
    load_win = pltpu.make_async_copy(win_hbm, win, w_sem.at[7])

    load_gain.start()

    @pl.when(s == 0)
    def _():
        for j in range(CHUNKS):
            load_patches(j).start()

    for j in range(CHUNKS):
        load_wq(j).start()
    load_win.start()
    load_wo.start()

    @pl.when(s == NS - 1)
    def _():
        for j in range(CHUNKS):
            load_cot(j).start()

    barrier = pltpu.get_barrier_semaphore()
    for d in range(1, NM):
        pl.semaphore_signal(barrier, inc=1, device_id={"mp": lax.rem(m + d, NM)}, device_id_type=MESH)
    for d in range(1, NZ):
        pl.semaphore_signal(barrier, inc=1, device_id={"dp": lax.rem(z + d, NZ)}, device_id_type=MESH)
    for d in range(1, NS):
        pl.semaphore_signal(barrier, inc=1, device_id={"section": lax.rem(s + d, NS)}, device_id_type=MESH)

    dp[:, 3 * HW : 2048] = jnp.zeros((ROWS, 2048 - 3 * HW), BF16)
    rq[ZR : ZR + 32, :] = jnp.zeros((32, 256), F32)
    for i, (t, h) in enumerate(PAIRS):
        cols = lax.broadcasted_iota(jnp.int32, (ROWS, 128), 1) + t * 128
        inside = (cols >= HEAD * h) & (cols < HEAD * h + HEAD)
        mk[i] = jnp.where(inside, 1.0, 0.0).astype(BF16)
    o32[ZR : ZR + 16, :] = jnp.zeros((16, HW), F32)

    def remote(src, dst, ssem, rsem, where):
        return pltpu.make_async_remote_copy(
            src_ref=src, dst_ref=dst, send_sem=ssem, recv_sem=rsem, device_id=where, device_id_type=MESH
        )

    def hop_forward(j):
        return remote(hout.at[j], hbuf.at[j], hs.at[j], hr.at[j], {"section": lax.rem(s + 1, NS)})

    def hop_back(j):
        return remote(gout.at[j], gbuf.at[j], gs.at[j], gr.at[j], {"section": lax.rem(s + NS - 1, NS)})

    def half_rows(i):
        return pl.ds(i * HALF, HALF)

    def far_forward(i):
        slot = lax.rem(s, 2)
        to = {"section": lax.rem(s + 3 - lax.rem(s, 2), NS)}
        return remote(hout.at[FAR, half_rows(i)], rbuf.at[slot, i], ls.at[i], lr.at[slot * 2 + i], to)

    def far_back(i):
        slot = 3 - lax.rem(s, 2)
        to = {"section": lax.rem(s + 2 - lax.rem(s, 2), NS)}
        return remote(gout.at[FAR, half_rows(i)], rbuf.at[slot, i], ls.at[2 + i], lr.at[slot * 2 + i], to)

    def near_forward():
        half = half_rows(1)
        to = {"section": lax.rem(s + 1, NS)}
        return remote(hout.at[FAR, half], hbuf.at[FAR, half], hs.at[FAR], hr.at[FAR + 1], to)

    def near_back():
        half = half_rows(1)
        to = {"section": lax.rem(s + NS - 1, NS)}
        return remote(gout.at[FAR, half], gbuf.at[FAR, half], gs.at[FAR], gr.at[FAR + 1], to)

    def pass_on(slot, i):
        to = {"section": lax.rem(s + (2, 3, 2, 1)[slot], NS)}
        if slot < 2:
            return remote(rbuf.at[slot, i], hbuf.at[FAR, half_rows(i)], ts.at[slot * 2 + i], hr.at[FAR + i], to)
        return remote(rbuf.at[slot, i], gbuf.at[FAR, half_rows(i)], ts.at[slot * 2 + i], gr.at[FAR + i], to)

    def relay(slot):
        for i in range(1):
            remote(rbuf.at[slot, i], rbuf.at[slot, i], ts.at[slot * 2 + i], lr.at[slot * 2 + i], {"section": lax.rem(s + 1, NS)}).wait_recv()
            pass_on(slot, i).start()

    def forward_send(j):
        if j == FAR:
            far_forward(0).start()
        else:
            hop_forward(j).start()
            if j == FAR - 1:
                near_forward().start()

    def forward_arrived(j):
        if j == FAR:
            pass_on(0, 0).wait_recv()
            near_forward().wait_recv()
        else:
            hop_forward(j).wait_recv()

    def back_send(j):
        if j == FAR:
            far_back(0).start()
        else:
            hop_back(j).start()
            if j == FAR - 1:
                near_back().start()

    def back_arrived(j):
        if j == FAR:
            pass_on(2, 0).wait_recv()
            near_back().wait_recv()
        else:
            hop_back(j).wait_recv()

    def mp_lanes(i):
        return pl.ds(pl.multiple_of(i * ROWS, ROWS), ROWS)

    def fold(x):
        return x[:, 0:128] + x[:, 128:256]

    def column_copy(half, d):
        to = lax.rem(m + d, NM)
        cols = pl.ds(pl.multiple_of(to * 256 + half * 128, 128), 128)
        i = half * NM + d
        return remote(dp.at[:, cols], dpg.at[half, mp_lanes(m), :], ds.at[i], dr.at[i], {"mp": to})

    def g_copy(d):
        to = lax.rem(m + d, NM)
        rows = pl.ds(pl.multiple_of(to * ZR, 16), ZR)
        return remote(gperm.at[rows], gpg.at[:, mp_lanes(m)], ps.at[d], pr.at[d], {"mp": to})

    def columns_q():
        for half in range(2):
            for d in range(1, NM):
                column_copy(half, d).start()
        for half in range(2):
            cols = pl.ds(pl.multiple_of(m * 256 + half * 128, 128), 128)
            dpg[half, mp_lanes(m), :] = dp[:, cols]

    def turn_g(j):
        gt32[j * CW : (j + 1) * CW, :] = gbuf[j].astype(F32).T
        for first in range(0, VD, FR):
            if (first + FR - 1) // CW == j:
                i, k = first // FR % NM, first // FR // NM
                gp32[i * ZR + k * FR : i * ZR + k * FR + FR, :] = gt32[first : first + FR, :]

    def columns_g():
        gperm[...] = gp32[...].astype(BF16)
        for d in range(1, NM):
            g_copy(d).start()
        gpg[:, mp_lanes(m)] = gperm[pl.ds(pl.multiple_of(m * ZR, 16), ZR), :]

    def attend_back(j):
        part = nt(gbuf[j], wo[:, j * CW : (j + 1) * CW])
        if j == 0:
            dacc[...] = part
        else:
            dacc[...] += part

    @pl.when(s > 0)
    def _():
        load_wo.wait()
        pl.semaphore_wait(barrier, (NM - 1) + (NZ - 1) + (NS - 1))

    @pl.when(s == NS - 1)
    def _():
        for j in range(CHUNKS):
            load_cot(j).wait()
            attend_back(j)
            turn_g(j)
        columns_g()
        relay(0)
        relay(1)

    load_gain.wait()
    @pl.when(s >= 2)
    def _():
        for j in range(CHUNKS):
            load_wq(j).wait()
            wqt[:, j * CW : (j + 1) * CW] = wq[j * CW : (j + 1) * CW, :].T

    squares = jnp.zeros((ROWS, 128), F32)
    for j in range(CHUNKS):

        @pl.when(s == 0)
        def _():
            load_patches(j).wait()

        @pl.when(s > 0)
        def _():
            forward_arrived(j)

        @pl.when(s < 2)
        def _():
            load_wq(j).wait()

        wide = hbuf[j].astype(F32)
        squares = squares + fold(wide * wide)
        scaled = (wide * gain[:, j * CW : (j + 1) * CW]).astype(BF16)
        for i in range(3):
            part = nn(scaled, wq[j * CW : (j + 1) * CW, i * HW : (i + 1) * HW])
            if j == 0:
                pacc[:, i * HW : (i + 1) * HW] = part
            else:
                pacc[:, i * HW : (i + 1) * HW] += part
    spread = lax.rsqrt(jnp.sum(squares, axis=-1, keepdims=True) * (1.0 / VD) + 1e-6)
    rs[...] = spread
    packed[...] = (pacc[...] * spread).astype(BF16)
    load_win.wait()
    ids = jnp.broadcast_to(win[...].astype(F32), (ROWS, ROWS))
    same = ids.T == ids

    for i, (t, h) in enumerate(PAIRS):
        rows = slice(i * ROWS, (i + 1) * ROWS)
        km[rows, :] = packed[:, HW + t * 128 : HW + t * 128 + 128] * mk[i]
        vm[rows, :] = packed[:, 2 * HW + t * 128 : 2 * HW + t * 128 + 128] * mk[i]
    for h in range(HEADS):
        t0, t1 = span(h)
        scores = nt(gathered(km, h), packed[:, t0:t1]) * SCALE
        scores = jnp.where(same, scores, -1e30)
        top = jnp.max(scores, axis=0, keepdims=True)
        e = jnp.exp(scores - top)
        p = e / jnp.sum(e, axis=0, keepdims=True)
        pt32[h] = p
        ptb[h * ROWS : (h + 1) * ROWS, :] = p.astype(BF16)
    for t in range(HW // 128):
        att[:, t * 128 : t * 128 + 128] = tn(ptb[head_rows(t), :], vm[pair_rows(t), :]).astype(BF16)

    @pl.when(s == 0)
    def _():
        load_wo.wait()
        pl.semaphore_wait(barrier, (NM - 1) + (NZ - 1) + (NS - 1))

    def project(j):
        hout[j] = (hbuf[j].astype(F32) + nn(att[...], wo[:, j * CW : (j + 1) * CW])).astype(BF16)

    chip = m // 2
    core = lax.rem(m, 2)
    sibling = chip * 2 + 1 - core

    def gather_copy(which, slot, i, to):
        lanes = mp_lanes(slot)
        if which == 0:
            return remote(ngt.at[:, lanes], ngt.at[:, lanes], ns.at[i], nr.at[i], {"mp": to})
        return remote(atg.at[lanes, :], atg.at[lanes, :], as_.at[i], ar.at[i], {"mp": to})

    def across(d):
        return lax.rem(chip + d, NM // 2) * 2 + core

    def gather_start():
        for j in range(CHUNKS):
            wide = hbuf[j].astype(F32) * rs[...] * gain[:, j * CW : (j + 1) * CW]
            ngt[j * CW : (j + 1) * CW, mp_lanes(m)] = wide.astype(BF16).T
        atg[mp_lanes(m), :] = att[...]
        for w in range(2):
            for d in range(1, NM // 2):
                gather_copy(w, m, d, across(d)).start()
            gather_copy(w, m, 0, sibling).start()

    def gather_forward():
        for d in range(1, NM // 2):
            source = across(NM // 2 - d)
            for w in range(2):
                gather_copy(w, source, d, across(d)).wait_recv()
                gather_copy(w, source, NM // 2 - 1 + d, sibling).start()

    def gather_finish(w):
        gather_copy(w, sibling, 0, sibling).wait_recv()
        for d in range(1, NM // 2):
            source = lax.rem(chip + NM // 2 - d, NM // 2) * 2 + 1 - core
            gather_copy(w, source, NM // 2 - 1 + d, sibling).wait_recv()

    @pl.when(s < NS - 1)
    def _():
        for j in SENT:
            project(j)
            forward_send(j)

    gather_start()

    @pl.when(s == 0)
    def _():
        gather_forward()

    def turn_weights():
        for j in range(CHUNKS):
            wqt[:, j * CW : (j + 1) * CW] = wq[j * CW : (j + 1) * CW, :].T

    @pl.when(s < 2)
    def _():
        turn_weights()

    @pl.when(s == 1)
    def _():
        relay(0)
        gather_forward()

    @pl.when(s == 0)
    def _():
        relay(2)
        relay(3)

    for i, (t, h) in enumerate(PAIRS):
        qm[i * ROWS : (i + 1) * ROWS, :] = packed[:, t * 128 : t * 128 + 128] * mk[i]
    for h in range(HEADS):
        ptl[:, h * ROWS : (h + 1) * ROWS] = ptb[h * ROWS : (h + 1) * ROWS, :]

    for j in range(CHUNKS):

        @pl.when(s < NS - 1)
        def _():
            back_arrived(j)
            attend_back(j)

        @pl.when(s == 0)
        def _():
            turn_g(j)

    datt[...] = dacc[...].astype(BF16)

    for i, (t, h) in enumerate(PAIRS):
        dam[i * ROWS : (i + 1) * ROWS, :] = datt[:, t * 128 : t * 128 + 128] * mk[i]
    for h in range(HEADS):
        t0, t1 = span(h)
        dprob = nt(gathered(vm, h), datt[:, t0:t1]).astype(BF16).astype(F32)
        p = pt32[h]
        dsc = p * (dprob - jnp.sum(p * dprob, axis=0, keepdims=True))
        dsc = (dsc * SCALE).astype(BF16)
        dsr[h * ROWS : (h + 1) * ROWS, :] = dsc
        dsl[:, h * ROWS : (h + 1) * ROWS] = dsc
    for t in range(HW // 128):
        c = t * 128
        dp[:, 2 * HW + c : 2 * HW + c + 128] = nn(ptl[:, head_rows(t)], dam[pair_rows(t), :]).astype(BF16)
    for t in range(HW // 128):
        c = t * 128
        dp[:, HW + c : HW + c + 128] = nn(dsl[:, head_rows(t)], qm[pair_rows(t), :]).astype(BF16)
        dp[:, c : c + 128] = tn(dsr[head_rows(t), :], km[pair_rows(t), :]).astype(BF16)

    @pl.when(s == 0)
    def _():
        columns_q()
        columns_g()

    spread = rs[...]
    inner = jnp.zeros((ROWS, 128), F32)
    for t in range(3 * HW // 128):
        cols = slice(t * 128, t * 128 + 128)
        inner = inner + dp[:, cols].astype(F32) * pacc[:, cols]
    pull = jnp.sum(inner, axis=-1, keepdims=True) * (1.0 / VD) * (spread * spread * spread)
    for j in SENT:
        dn = nn(dp[:, 0 : 3 * HW], wqt[:, j * CW : (j + 1) * CW]).astype(BF16).astype(F32)
        up = dn * gain[:, j * CW : (j + 1) * CW]
        back = gbuf[j].astype(F32) + spread * up - hbuf[j].astype(F32) * pull
        gout[j] = back.astype(BF16)

        @pl.when(s > 0)
        def _():
            back_send(j)

        lifted[j] = dn

    def store_act(j):
        return pltpu.make_async_copy(hout.at[j], act.at[:, cols_of(j)], o_sem.at[j])

    def store_gin(j):
        return pltpu.make_async_copy(gout.at[j], gin.at[:, cols_of(j)], o_sem.at[CHUNKS + j])

    for j in range(CHUNKS):
        store_gin(j).start()

    @pl.when(s > 0)
    def _():
        columns_q()

    @pl.when((s > 0) & (s < NS - 1))
    def _():
        for j in range(CHUNKS):
            turn_g(j)
        columns_g()

    for j in range(CHUNKS):
        part = lifted[j] * (hbuf[j].astype(F32) * rs[...])
        dgain[0, :, j * CW : (j + 1) * CW] = jnp.sum(part, axis=0, keepdims=True)

    @pl.when(s == NS - 1)
    def _():
        for j in range(CHUNKS):
            project(j)

    @pl.when(s >= NS - 2)
    def _():
        gather_forward()

    @pl.when(s == 2)
    def _():
        relay(2)

    for j in range(CHUNKS):
        store_act(j).start()

    def gain_mp(d):
        return remote(dgain.at[0], dgrecv.at[d], vs.at[d], vr.at[d], {"mp": lax.rem(m + d, NM)})

    def gain_dp(d):
        return remote(dgz.at[0], dgzrecv.at[d], us.at[d], ur.at[d], {"dp": lax.rem(z + d, NZ)})

    for d in range(1, NM):
        gain_mp(d).start()

    def chunk_q(half):
        def chunk(k):
            rows = pl.ds(pl.multiple_of(k * ZR, 16), ZR)
            return nn(ngt[rows, :], dpg[half])

        return chunk

    def chunk_o(k):
        return opad[k]

    steps = (NZ - 1, 1, NZ - 2, 2, NZ - 1, 1, NZ - 2, 2)
    owners = (NZ - 3, 3, 4, 4, NZ - 1, 1, NZ - 2, 2)

    def peer(i):
        return {"dp": lax.rem(z + steps[i], NZ)}

    def tree_q(half):
        def copy(i):
            n = half * 8 + i
            if i == 2 or i == 3:
                top = pl.ds(0, ZR // 2)
                return remote(sq.at[half, i, top], zq.at[half, i, top], qs.at[n], qr.at[n], peer(i))
            return remote(sq.at[half, i], zq.at[half, i], qs.at[n], qr.at[n], peer(i))

        return copy

    def tree_o(i):
        if i == 2 or i == 3:
            half = pl.ds(0, 16)
            return remote(so.at[i, half], zo.at[i, half], os_.at[i], or_.at[i], peer(i))
        return remote(so.at[i], zo.at[i], os_.at[i], or_.at[i], peer(i))

    def whose(i):
        return lax.rem(z + owners[i], NZ)

    def leaf(i, chunk, buf, copy, rows):
        if i == 2:
            value = chunk(whose(2)).astype(BF16)
            buf[2, 0 : rows // 2] = value[0 : rows // 2]
            buf[3, 0 : rows // 2] = value[rows // 2 : rows]
            copy(2).start()
            copy(3).start()
        else:
            buf[i] = chunk(whose(i)).astype(BF16)
            copy(i).start()

    def branch(i, chunk, buf, got, copy, rows, hold):
        hold[...] = chunk(whose(i))
        copy(i - 6).wait_recv()
        hold[...] += got[i - 6].astype(F32)
        copy(i - 4).wait_recv()
        if i == 6:
            hold[0 : rows // 2] += got[2, 0 : rows // 2].astype(F32)
        else:
            hold[rows // 2 : rows] += got[3, 0 : rows // 2].astype(F32)
        buf[i] = hold[...].astype(BF16)
        copy(i).start()

    def leaf_q(half, i):
        leaf(i, chunk_q(half), sq.at[half], tree_q(half), ZR)

    def sum_of(half):
        return rq.at[0:ZR, half * 128 : half * 128 + 128]

    def branch_q(half, i):
        branch(i, chunk_q(half), sq.at[half], zq.at[half], tree_q(half), ZR, sum_of(half))

    gather_finish(0)
    for half in range(2):
        for d in range(1, NM):
            column_copy(half, d).wait_recv()
        for i in (2, 0, 1):
            leaf_q(half, i)
    for i in (4, 5):
        leaf_q(0, i)
    for i in (6, 7):
        branch_q(0, i)

    gather_finish(1)
    for d in range(1, NM):
        g_copy(d).wait_recv()
    o32[0:ZR, :] = nn(gpg[...], atg[...])
    for k in range(NZ):
        opad[k] = o32[FR * k : FR * k + 32, :]
    for i in (2, 0, 1):
        leaf(i, chunk_o, so, tree_o, 32)
    for i in (4, 5):
        leaf_q(1, i)
    for i in (6, 7):
        branch_q(1, i)
    for i in (4, 5):
        leaf(i, chunk_o, so, tree_o, 32)
    for i in (6, 7):
        branch(i, chunk_o, so, zo, tree_o, 32, ro)

    sum_gain = dgain[0]
    for d in range(1, NM):
        gain_mp(d).wait_recv()
        sum_gain = sum_gain + dgrecv[d]
    dgz[0] = sum_gain
    for d in range(1, NZ):
        gain_dp(d).start()

    for half in range(2):
        hold = sum_of(half)
        hold[...] = chunk_q(half)(z)
        for i in (4, 5, 6, 7):
            tree_q(half)(i).wait_recv()
            hold[...] += zq[half, i].astype(F32)

    def piece(d):
        return remote(fin.at[lax.rem(m + d, NM)], finrecv.at[m], fs.at[d], fr.at[d], {"mp": lax.rem(m + d, NM)})

    for i in range(NM):
        fin[i] = rq[FR * i : FR * i + 32, :].astype(BF16)
    for d in range(1, NM):
        piece(d).start()
    finrecv[m] = fin[m]

    ro[...] = chunk_o(z)
    for i in (4, 5, 6, 7):
        tree_o(i).wait_recv()
        ro[...] += zo[i].astype(F32)
    oo[:, 0, :] = ro[0:FR, :]
    store_o = pltpu.make_async_copy(oo, out_o, o_sem.at[2 * CHUNKS])
    store_o.start()

    sum_gain = dgz[0]
    for d in range(1, NZ):
        gain_dp(d).wait_recv()
        sum_gain = sum_gain + dgzrecv[d]
    dgz[1] = sum_gain
    store_gain = pltpu.make_async_copy(dgz.at[1], out_gain, o_sem.at[2 * CHUNKS + 1])
    store_gain.start()

    @pl.when(s < NS - 1)
    def _():
        for j in range(FAR):
            hop_forward(j).wait_send()
        far_forward(0).wait_send()
        near_forward().wait_send()

    @pl.when(s > 0)
    def _():
        for j in range(FAR):
            hop_back(j).wait_send()
        far_back(0).wait_send()
        near_back().wait_send()

    for where, slots in ((0, (2, 3)), (1, (0,)), (2, (2,)), (3, (0, 1))):

        @pl.when(s == where)
        def _():
            for slot in slots:
                pass_on(slot, 0).wait_send()

    for i in range(NM - 1):
        for w in range(2):
            gather_copy(w, m, i, sibling).wait_send()
    for d in range(1, NM):
        for half in range(2):
            column_copy(half, d).wait_send()
        g_copy(d).wait_send()
        gain_mp(d).wait_send()
    for d in range(1, NZ):
        gain_dp(d).wait_send()
    for i in range(8):
        tree_q(0)(i).wait_send()
        tree_q(1)(i).wait_send()
        tree_o(i).wait_send()
    for j in range(CHUNKS):
        store_act(j).wait()
        store_gin(j).wait()

    for d in range(1, NM):
        source = lax.rem(m + NM - d, NM)
        remote(fin.at[source], finrecv.at[source], fs.at[d], fr.at[d], {"mp": source}).wait_recv()
    for i in range(NM):
        wide = min(256, 3 * HW - 256 * i)
        oq[:, 0, 256 * i : 256 * i + wide] = finrecv[i, :, 0:wide].astype(F32)[0:FR]
    store_q = pltpu.make_async_copy(oq, out_q, o_sem.at[2 * CHUNKS + 2])
    store_q.start()
    for d in range(1, NM):
        piece(d).wait_send()
    store_o.wait()
    store_gain.wait()
    store_q.wait()


def finish(act, gin, out_q, out_o, gain, act2, gin2, out_q2, out_o2, gain2, a, b, c, d, e, f, sem):
    there = ((gain, e), (act, a), (gin, b), (out_q, c), (out_o, d))
    back = ((f, gain2), (a, act2), (b, gin2), (c, out_q2), (d, out_o2))
    reads = [pltpu.make_async_copy(x, y, sem.at[i]) for i, (x, y) in enumerate(there)]
    writes = [pltpu.make_async_copy(x, y, sem.at[5 + i]) for i, (x, y) in enumerate(back)]
    for r in reads:
        r.start()
    place = (lax.axis_index("dp") * NM + lax.axis_index("mp")) * FR
    for i, (r, w) in enumerate(zip(reads, writes)):
        r.wait()
        if i == 0:
            rows = jnp.broadcast_to(e[...], (8, VD))
            f[...] = pltpu.roll(rows, lax.rem(VD - place, VD), 1)[0:1, 0:FR]
        w.start()
    for w in writes:
        w.wait()


def on_device(patches, windows, gain, w_qkv, w_out, cotangent):
    hbm = pl.BlockSpec(memory_space=pl.ANY)
    dma = pltpu.SemaphoreType.DMA
    scratch = [
        pltpu.VMEM((VD, 3 * HW), BF16),
        pltpu.VMEM((HW, VD), BF16),
        pltpu.VMEM((1, ROWS), jnp.int32),
        pltpu.VMEM((1, VD), F32),
        pltpu.VMEM((CHUNKS, ROWS, CW), BF16),
        pltpu.VMEM((CHUNKS, ROWS, CW), BF16),
        pltpu.VMEM((CHUNKS, ROWS, CW), BF16),
        pltpu.VMEM((CHUNKS, ROWS, CW), BF16),
        pltpu.VMEM((ROWS, 3 * HW), F32),
        pltpu.VMEM((ROWS, HW), F32),
        pltpu.VMEM((ROWS, 3 * HW), BF16),
        pltpu.VMEM((HEADS, ROWS, ROWS), F32),
        pltpu.VMEM((HEADS * ROWS, ROWS), BF16),
        pltpu.VMEM((ROWS, HEADS * ROWS), BF16),
        pltpu.VMEM((ROWS, HW), BF16),
        pltpu.VMEM((len(PAIRS), ROWS, 128), BF16),
        pltpu.VMEM((len(PAIRS) * ROWS, 128), BF16),
        pltpu.VMEM((len(PAIRS) * ROWS, 128), BF16),
        pltpu.VMEM((len(PAIRS) * ROWS, 128), BF16),
        pltpu.VMEM((len(PAIRS) * ROWS, 128), BF16),
        pltpu.VMEM((HEADS * ROWS, ROWS), BF16),
        pltpu.VMEM((ROWS, HEADS * ROWS), BF16),
        pltpu.VMEM((ROWS, HW), BF16),
        pltpu.VMEM((ROWS, 2048), BF16),
        pltpu.VMEM((CHUNKS, ROWS, CW), F32),
        pltpu.VMEM((ROWS, 1), F32),
        pltpu.VMEM((3 * HW, VD), BF16),
        pltpu.VMEM((FR, 1, 3 * HW), F32),
        pltpu.VMEM((FR, 1, HW), F32),
        pltpu.VMEM((4, 2, HALF, CW), BF16),
        pltpu.VMEM((VD, NM * ROWS), BF16),
        pltpu.VMEM((NM * ROWS, HW), BF16),
        pltpu.VMEM((VD, ROWS), F32),
        pltpu.VMEM((VD, ROWS), F32),
        pltpu.VMEM((VD, ROWS), BF16),
        pltpu.VMEM((2, NM * ROWS, 128), BF16),
        pltpu.VMEM((ZR, NM * ROWS), BF16),
        pltpu.VMEM((ZR + 16, HW), F32),
        pltpu.VMEM((NZ, 32, HW), F32),
        pltpu.VMEM((1, 1, VD), F32),
        pltpu.VMEM((NM, 1, VD), F32),
        pltpu.VMEM((2, 1, VD), F32),
        pltpu.VMEM((NZ, 1, VD), F32),
        pltpu.VMEM((ZR + 32, 256), F32),
        pltpu.VMEM((32, HW), F32),
        pltpu.VMEM((2, 8, ZR, 128), BF16),
        pltpu.VMEM((8, 32, HW), BF16),
        pltpu.VMEM((2, 8, ZR, 128), BF16),
        pltpu.VMEM((8, 32, HW), BF16),
        pltpu.VMEM((NM, 32, 256), BF16),
        pltpu.VMEM((NM, 32, 256), BF16),
        dma((8,)), dma((CHUNKS,)), dma((2 * CHUNKS + 3,)),
        dma((8,)), dma((8,)), dma((8,)), dma((8,)),
    ] + [dma((16,)) for _ in range(21)]
    shapes = (
        jax.ShapeDtypeStruct((ROWS, VD), BF16),
        jax.ShapeDtypeStruct((ROWS, VD), BF16),
        jax.ShapeDtypeStruct((FR, 1, 3 * HW), F32),
        jax.ShapeDtypeStruct((FR, 1, HW), F32),
        jax.ShapeDtypeStruct((1, VD), F32),
    )
    results = pl.pallas_call(
        kernel,
        out_shape=shapes,
        in_specs=[hbm] * 6,
        out_specs=(hbm,) * 5,
        scratch_shapes=scratch,
        compiler_params=pltpu.CompilerParams(
            collective_id=0, has_side_effects=True, vmem_limit_bytes=60 * 1024 * 1024
        ),
    )(patches[0], cotangent[0], windows, gain, w_qkv[0], w_out[0])
    act, gin, out_q, out_o, own_gain = pl.pallas_call(
        finish,
        out_shape=shapes[:4] + (jax.ShapeDtypeStruct((1, FR), F32),),
        in_specs=[hbm] * 5,
        out_specs=(hbm,) * 5,
        scratch_shapes=[pltpu.VMEM(x.shape, x.dtype) for x in shapes] + [pltpu.VMEM((1, FR), F32), dma((10,))],
        compiler_params=pltpu.CompilerParams(vmem_limit_bytes=60 * 1024 * 1024),
    )(*results)
    return (
        act[None, None],
        gin[None, None],
        out_q.transpose(1, 0, 2),
        out_o.transpose(1, 2, 0),
        own_gain,
    )


def solution(mesh):
    in_specs = (
        P(None, ("dp", "mp"), None),
        P(None, ("dp", "mp")),
        P("section", None),
        P("section", None, None),
        P("section", None, None),
        P(None, ("dp", "mp"), None),
    )
    out_specs = (
        P("section", None, ("dp", "mp"), None),
        P("section", None, ("dp", "mp"), None),
        P("section", ("dp", "mp"), None),
        P("section", None, ("dp", "mp")),
        P("section", ("dp", "mp")),
    )
    return jax.shard_map(
        on_device, mesh=mesh, in_specs=in_specs, out_specs=out_specs, check_vma=False
    )
```

```python
import jax
import jax.numpy as jnp
from jax import lax
from jax.experimental import pallas as pl
from jax.experimental.pallas import tpu as pltpu
from jax.sharding import PartitionSpec as P

HEAD = 80
HEADS = 8
ROWS = 128
VD = 1280
HW = 640
NM = 8
NZ = 8
NS = 4
CHUNKS = 5
CW = VD // CHUNKS
FAR = CHUNKS - 1
SENT = (FAR,) + tuple(range(FAR))
HALF = ROWS // 2
ZR = VD // NZ
FR = ZR // NM
SCALE = HEAD**-0.5
MESH = pl.DeviceIdType.MESH
F32 = jnp.float32
BF16 = jnp.bfloat16


def nt(a, b):
    return lax.dot_general(a, b, (((1,), (1,)), ((), ())), preferred_element_type=F32)


def nn(a, b):
    return lax.dot_general(a, b, (((1,), (0,)), ((), ())), preferred_element_type=F32)


def tn(a, b):
    return lax.dot_general(a, b, (((0,), (0,)), ((), ())), preferred_element_type=F32)


def tiles_of(h):
    return range(HEAD * h // 128, -(-(HEAD * h + HEAD) // 128))


def heads_of(t):
    return [h for h in range(HEADS) if t in tiles_of(h)]


PAIRS = [(t, h) for t in range(HW // 128) for h in heads_of(t)]


def pair_rows(t):
    first = PAIRS.index((t, heads_of(t)[0]))
    return slice(first * ROWS, (first + len(heads_of(t))) * ROWS)


def head_rows(t):
    heads = heads_of(t)
    return slice(heads[0] * ROWS, (heads[-1] + 1) * ROWS)


def gathered(stack, h):
    parts = []
    for t in tiles_of(h):
        i = PAIRS.index((t, h))
        parts.append(stack[i * ROWS : (i + 1) * ROWS, :])
    return parts[0] if len(parts) == 1 else jnp.concatenate(parts, axis=1)


def span(h):
    tiles = tiles_of(h)
    return tiles[0] * 128, tiles[-1] * 128 + 128


def kernel(
    patches, cot, win_hbm, gain_hbm, wq_hbm, wo_hbm,
    act, gin, out_q, out_o, out_gain,
    wq, wo, win, gain, hbuf, gbuf, hout, gout, pacc, dacc, packed, pt32, ptb, ptl, att, mk, qm, km, vm, dam, dsr, dsl,
    datt, dp, lifted, rs, wqt, oq, oo, rbuf,
    ngt, atg, gt32, gp32, gperm, dpg, gpg, o32, opad, dgain, dgrecv, dgz, dgzrecv,
    rq, ro, sq, so, zq, zo, fin, finrecv,
    w_sem, in_sem, o_sem, hs, hr, gs, gr, ns, nr, as_, ar, ds, dr, ps, pr, vs, vr, us, ur, qs, qr, os_, or_, fs, fr, ls, lr, ts,
):
    s = lax.axis_index("section")
    m = lax.axis_index("mp")
    z = lax.axis_index("dp")

    def cols_of(j):
        return pl.ds(j * CW, CW)

    def load_patches(j):
        return pltpu.make_async_copy(patches.at[:, cols_of(j)], hbuf.at[j], in_sem.at[j])

    def load_cot(j):
        return pltpu.make_async_copy(cot.at[:, cols_of(j)], gbuf.at[j], in_sem.at[j])

    def load_wq(j):
        return pltpu.make_async_copy(wq_hbm.at[cols_of(j)], wq.at[cols_of(j)], w_sem.at[j])

    load_wo = pltpu.make_async_copy(wo_hbm, wo, w_sem.at[5])
    load_gain = pltpu.make_async_copy(gain_hbm, gain, w_sem.at[6])
    load_win = pltpu.make_async_copy(win_hbm, win, w_sem.at[7])

    load_gain.start()

    @pl.when(s == 0)
    def _():
        for j in range(CHUNKS):
            load_patches(j).start()

    for j in range(CHUNKS):
        load_wq(j).start()
    load_win.start()
    load_wo.start()

    @pl.when(s == NS - 1)
    def _():
        for j in range(CHUNKS):
            load_cot(j).start()

    barrier = pltpu.get_barrier_semaphore()
    for d in range(1, NM):
        pl.semaphore_signal(barrier, inc=1, device_id={"mp": lax.rem(m + d, NM)}, device_id_type=MESH)
    for d in range(1, NZ):
        pl.semaphore_signal(barrier, inc=1, device_id={"dp": lax.rem(z + d, NZ)}, device_id_type=MESH)
    for d in range(1, NS):
        pl.semaphore_signal(barrier, inc=1, device_id={"section": lax.rem(s + d, NS)}, device_id_type=MESH)

    dp[:, 3 * HW : 2048] = jnp.zeros((ROWS, 2048 - 3 * HW), BF16)
    rq[ZR : ZR + 32, :] = jnp.zeros((32, 256), F32)
    for i, (t, h) in enumerate(PAIRS):
        cols = lax.broadcasted_iota(jnp.int32, (ROWS, 128), 1) + t * 128
        inside = (cols >= HEAD * h) & (cols < HEAD * h + HEAD)
        mk[i] = jnp.where(inside, 1.0, 0.0).astype(BF16)
    opad[:, :, HW : HW + 256] = jnp.zeros((NZ, 16, 256), F32)

    def remote(src, dst, ssem, rsem, where):
        return pltpu.make_async_remote_copy(
            src_ref=src, dst_ref=dst, send_sem=ssem, recv_sem=rsem, device_id=where, device_id_type=MESH
        )

    def hop_forward(j):
        return remote(hout.at[j], hbuf.at[j], hs.at[j], hr.at[j], {"section": lax.rem(s + 1, NS)})

    def hop_back(j):
        return remote(gout.at[j], gbuf.at[j], gs.at[j], gr.at[j], {"section": lax.rem(s + NS - 1, NS)})

    def half_rows(i):
        return pl.ds(i * HALF, HALF)

    def far_forward(i):
        slot = lax.rem(s, 2)
        to = {"section": lax.rem(s + 3 - lax.rem(s, 2), NS)}
        return remote(hout.at[FAR, half_rows(i)], rbuf.at[slot, i], ls.at[i], lr.at[slot * 2 + i], to)

    def far_back(i):
        slot = 3 - lax.rem(s, 2)
        to = {"section": lax.rem(s + 2 - lax.rem(s, 2), NS)}
        return remote(gout.at[FAR, half_rows(i)], rbuf.at[slot, i], ls.at[2 + i], lr.at[slot * 2 + i], to)

    def near_forward():
        half = half_rows(1)
        to = {"section": lax.rem(s + 1, NS)}
        return remote(hout.at[FAR, half], hbuf.at[FAR, half], hs.at[FAR], hr.at[FAR + 1], to)

    def near_back():
        half = half_rows(1)
        to = {"section": lax.rem(s + NS - 1, NS)}
        return remote(gout.at[FAR, half], gbuf.at[FAR, half], gs.at[FAR], gr.at[FAR + 1], to)

    def pass_on(slot, i):
        to = {"section": lax.rem(s + (2, 3, 2, 1)[slot], NS)}
        if slot < 2:
            return remote(rbuf.at[slot, i], hbuf.at[FAR, half_rows(i)], ts.at[slot * 2 + i], hr.at[FAR + i], to)
        return remote(rbuf.at[slot, i], gbuf.at[FAR, half_rows(i)], ts.at[slot * 2 + i], gr.at[FAR + i], to)

    def relay(slot):
        for i in range(1):
            remote(rbuf.at[slot, i], rbuf.at[slot, i], ts.at[slot * 2 + i], lr.at[slot * 2 + i], {"section": lax.rem(s + 1, NS)}).wait_recv()
            pass_on(slot, i).start()

    def forward_send(j):
        if j == FAR:
            far_forward(0).start()
        else:
            hop_forward(j).start()
            if j == FAR - 1:
                near_forward().start()

    def forward_arrived(j):
        if j == FAR:
            pass_on(0, 0).wait_recv()
            near_forward().wait_recv()
        else:
            hop_forward(j).wait_recv()

    def back_send(j):
        if j == FAR:
            far_back(0).start()
        else:
            hop_back(j).start()
            if j == FAR - 1:
                near_back().start()

    def back_arrived(j):
        if j == FAR:
            pass_on(2, 0).wait_recv()
            near_back().wait_recv()
        else:
            hop_back(j).wait_recv()

    def mp_lanes(i):
        return pl.ds(pl.multiple_of(i * ROWS, ROWS), ROWS)

    def fold(x):
        return x[:, 0:128] + x[:, 128:256]

    def column_copy(half, d):
        to = lax.rem(m + d, NM)
        cols = pl.ds(pl.multiple_of(to * 256 + half * 128, 128), 128)
        i = half * NM + d
        return remote(dp.at[:, cols], dpg.at[half, mp_lanes(m), :], ds.at[i], dr.at[i], {"mp": to})

    def g_copy(d):
        to = lax.rem(m + d, NM)
        rows = pl.ds(pl.multiple_of(to * ZR, 16), ZR)
        return remote(gperm.at[rows], gpg.at[:, mp_lanes(m)], ps.at[d], pr.at[d], {"mp": to})

    def columns_q():
        for half in range(2):
            for d in range(1, NM):
                column_copy(half, d).start()
        for half in range(2):
            cols = pl.ds(pl.multiple_of(m * 256 + half * 128, 128), 128)
            dpg[half, mp_lanes(m), :] = dp[:, cols]

    def turn_g(j):
        gt32[j * CW : (j + 1) * CW, :] = gbuf[j].astype(F32).T
        for first in range(0, VD, FR):
            if (first + FR - 1) // CW == j:
                i, k = first // FR % NM, first // FR // NM
                gp32[i * ZR + k * FR : i * ZR + k * FR + FR, :] = gt32[first : first + FR, :]

    def columns_g():
        gperm[...] = gp32[...].astype(BF16)
        for d in range(1, NM):
            g_copy(d).start()
        gpg[:, mp_lanes(m)] = gperm[pl.ds(pl.multiple_of(m * ZR, 16), ZR), :]

    def attend_back(j):
        part = nt(gbuf[j], wo[:, j * CW : (j + 1) * CW])
        if j == 0:
            dacc[...] = part
        else:
            dacc[...] += part

    @pl.when(s > 0)
    def _():
        load_wo.wait()
        pl.semaphore_wait(barrier, (NM - 1) + (NZ - 1) + (NS - 1))

    @pl.when(s == NS - 1)
    def _():
        for j in range(CHUNKS):
            load_cot(j).wait()
            attend_back(j)
            turn_g(j)
        columns_g()
        relay(0)
        relay(1)

    load_gain.wait()
    @pl.when(s >= 2)
    def _():
        for j in range(CHUNKS):
            load_wq(j).wait()
            wqt[:, j * CW : (j + 1) * CW] = wq[j * CW : (j + 1) * CW, :].T

    squares = jnp.zeros((ROWS, 128), F32)
    for j in range(CHUNKS):

        @pl.when(s == 0)
        def _():
            load_patches(j).wait()

        @pl.when(s > 0)
        def _():
            forward_arrived(j)

        @pl.when(s < 2)
        def _():
            load_wq(j).wait()

        wide = hbuf[j].astype(F32)
        squares = squares + fold(wide * wide)
        scaled = (wide * gain[:, j * CW : (j + 1) * CW]).astype(BF16)
        for i in range(3):
            part = nn(scaled, wq[j * CW : (j + 1) * CW, i * HW : (i + 1) * HW])
            if j == 0:
                pacc[:, i * HW : (i + 1) * HW] = part
            else:
                pacc[:, i * HW : (i + 1) * HW] += part
    spread = lax.rsqrt(jnp.sum(squares, axis=-1, keepdims=True) * (1.0 / VD) + 1e-6)
    rs[...] = spread
    packed[...] = (pacc[...] * spread).astype(BF16)
    load_win.wait()
    ids = jnp.broadcast_to(win[...].astype(F32), (ROWS, ROWS))
    same = ids.T == ids

    for i, (t, h) in enumerate(PAIRS):
        rows = slice(i * ROWS, (i + 1) * ROWS)
        km[rows, :] = packed[:, HW + t * 128 : HW + t * 128 + 128] * mk[i]
        vm[rows, :] = packed[:, 2 * HW + t * 128 : 2 * HW + t * 128 + 128] * mk[i]
    for h in range(HEADS):
        t0, t1 = span(h)
        scores = nt(gathered(km, h), packed[:, t0:t1]) * SCALE
        scores = jnp.where(same, scores, -1e30)
        top = jnp.max(scores, axis=0, keepdims=True)
        e = jnp.exp(scores - top)
        p = e / jnp.sum(e, axis=0, keepdims=True)
        pt32[h] = p
        ptb[h * ROWS : (h + 1) * ROWS, :] = p.astype(BF16)
    for t in range(HW // 128):
        att[:, t * 128 : t * 128 + 128] = tn(ptb[head_rows(t), :], vm[pair_rows(t), :]).astype(BF16)

    @pl.when(s == 0)
    def _():
        load_wo.wait()
        pl.semaphore_wait(barrier, (NM - 1) + (NZ - 1) + (NS - 1))

    def project(j):
        hout[j] = (hbuf[j].astype(F32) + nn(att[...], wo[:, j * CW : (j + 1) * CW])).astype(BF16)

    chip = m // 2
    core = lax.rem(m, 2)
    sibling = chip * 2 + 1 - core

    def gather_copy(which, slot, i, to):
        lanes = mp_lanes(slot)
        if which == 0:
            return remote(ngt.at[:, lanes], ngt.at[:, lanes], ns.at[i], nr.at[i], {"mp": to})
        return remote(atg.at[lanes, :], atg.at[lanes, :], as_.at[i], ar.at[i], {"mp": to})

    def across(d):
        return lax.rem(chip + d, NM // 2) * 2 + core

    def gather_start():
        for j in range(CHUNKS):
            wide = hbuf[j].astype(F32) * rs[...] * gain[:, j * CW : (j + 1) * CW]
            ngt[j * CW : (j + 1) * CW, mp_lanes(m)] = wide.astype(BF16).T
        atg[mp_lanes(m), :] = att[...]
        for w in range(2):
            for d in range(1, NM // 2):
                gather_copy(w, m, d, across(d)).start()
            gather_copy(w, m, 0, sibling).start()

    def gather_forward():
        for d in range(1, NM // 2):
            source = across(NM // 2 - d)
            for w in range(2):
                gather_copy(w, source, d, across(d)).wait_recv()
                gather_copy(w, source, NM // 2 - 1 + d, sibling).start()

    def gather_finish(w):
        gather_copy(w, sibling, 0, sibling).wait_recv()
        for d in range(1, NM // 2):
            source = lax.rem(chip + NM // 2 - d, NM // 2) * 2 + 1 - core
            gather_copy(w, source, NM // 2 - 1 + d, sibling).wait_recv()

    @pl.when(s < NS - 1)
    def _():
        for j in SENT:
            project(j)
            forward_send(j)

    gather_start()

    @pl.when(s == 0)
    def _():
        gather_forward()

    def turn_weights():
        for j in range(CHUNKS):
            wqt[:, j * CW : (j + 1) * CW] = wq[j * CW : (j + 1) * CW, :].T

    @pl.when(s < 2)
    def _():
        turn_weights()

    @pl.when(s == 1)
    def _():
        relay(0)
        gather_forward()

    @pl.when(s == 0)
    def _():
        relay(2)
        relay(3)

    for i, (t, h) in enumerate(PAIRS):
        qm[i * ROWS : (i + 1) * ROWS, :] = packed[:, t * 128 : t * 128 + 128] * mk[i]
    for h in range(HEADS):
        ptl[:, h * ROWS : (h + 1) * ROWS] = ptb[h * ROWS : (h + 1) * ROWS, :]

    for j in range(CHUNKS):

        @pl.when(s < NS - 1)
        def _():
            back_arrived(j)
            attend_back(j)

        @pl.when(s == 0)
        def _():
            turn_g(j)

    datt[...] = dacc[...].astype(BF16)

    for i, (t, h) in enumerate(PAIRS):
        dam[i * ROWS : (i + 1) * ROWS, :] = datt[:, t * 128 : t * 128 + 128] * mk[i]
    for h in range(HEADS):
        t0, t1 = span(h)
        dprob = nt(gathered(vm, h), datt[:, t0:t1]).astype(BF16).astype(F32)
        p = pt32[h]
        dsc = p * (dprob - jnp.sum(p * dprob, axis=0, keepdims=True))
        dsc = (dsc * SCALE).astype(BF16)
        dsr[h * ROWS : (h + 1) * ROWS, :] = dsc
        dsl[:, h * ROWS : (h + 1) * ROWS] = dsc
    for t in range(HW // 128):
        c = t * 128
        dp[:, 2 * HW + c : 2 * HW + c + 128] = nn(ptl[:, head_rows(t)], dam[pair_rows(t), :]).astype(BF16)
    for t in range(HW // 128):
        c = t * 128
        dp[:, HW + c : HW + c + 128] = nn(dsl[:, head_rows(t)], qm[pair_rows(t), :]).astype(BF16)
        dp[:, c : c + 128] = tn(dsr[head_rows(t), :], km[pair_rows(t), :]).astype(BF16)

    @pl.when(s == 0)
    def _():
        columns_q()
        columns_g()

    spread = rs[...]
    inner = jnp.zeros((ROWS, 128), F32)
    for t in range(3 * HW // 128):
        cols = slice(t * 128, t * 128 + 128)
        inner = inner + dp[:, cols].astype(F32) * pacc[:, cols]
    pull = jnp.sum(inner, axis=-1, keepdims=True) * (1.0 / VD) * (spread * spread * spread)
    for j in SENT:
        dn = nn(dp[:, 0 : 3 * HW], wqt[:, j * CW : (j + 1) * CW]).astype(BF16).astype(F32)
        up = dn * gain[:, j * CW : (j + 1) * CW]
        back = gbuf[j].astype(F32) + spread * up - hbuf[j].astype(F32) * pull
        gout[j] = back.astype(BF16)

        @pl.when(s > 0)
        def _():
            back_send(j)

        lifted[j] = dn

    def store_act(j):
        return pltpu.make_async_copy(hout.at[j], act.at[:, cols_of(j)], o_sem.at[j])

    def store_gin(j):
        return pltpu.make_async_copy(gout.at[j], gin.at[:, cols_of(j)], o_sem.at[CHUNKS + j])

    for j in range(CHUNKS):
        store_gin(j).start()

    @pl.when(s > 0)
    def _():
        columns_q()

    @pl.when((s > 0) & (s < NS - 1))
    def _():
        for j in range(CHUNKS):
            turn_g(j)
        columns_g()

    for j in range(CHUNKS):
        part = lifted[j] * (hbuf[j].astype(F32) * rs[...])
        dgain[0, :, j * CW : (j + 1) * CW] = jnp.sum(part, axis=0, keepdims=True)

    @pl.when(s == NS - 1)
    def _():
        for j in range(CHUNKS):
            project(j)

    @pl.when(s >= NS - 2)
    def _():
        gather_forward()

    @pl.when(s == 2)
    def _():
        relay(2)

    for j in range(CHUNKS):
        store_act(j).start()

    def gain_mp(d):
        return remote(dgain.at[0], dgrecv.at[d], vs.at[d], vr.at[d], {"mp": lax.rem(m + d, NM)})

    def gain_dp(d):
        return remote(dgz.at[0], dgzrecv.at[d], us.at[d], ur.at[d], {"dp": lax.rem(z + d, NZ)})

    for d in range(1, NM):
        gain_mp(d).start()

    def chunk_q(half):
        def chunk(k):
            rows = pl.ds(pl.multiple_of(k * ZR, 16), ZR)
            return nn(ngt[rows, :], dpg[half])

        return chunk

    def chunk_o(k):
        return opad[k]

    steps = (NZ - 1, 1, NZ - 2, 2, NZ - 1, 1, NZ - 2, 2)
    owners = (NZ - 3, 3, 4, 4, NZ - 1, 1, NZ - 2, 2)

    def peer(i):
        return {"dp": lax.rem(z + steps[i], NZ)}

    def tree_q(half):
        def copy(i):
            n = half * 8 + i
            if i == 2 or i == 3:
                top = pl.ds(0, ZR // 2)
                return remote(sq.at[half, i, top], zq.at[half, i, top], qs.at[n], qr.at[n], peer(i))
            return remote(sq.at[half, i], zq.at[half, i], qs.at[n], qr.at[n], peer(i))

        return copy

    def tree_o(i):
        to = {"dp": lax.rem(z + NZ - 2 + 4 * core, NZ)} if i == 2 else peer(i)
        return remote(so.at[i], zo.at[i], os_.at[i], or_.at[i], to)

    def whose(i):
        return lax.rem(z + owners[i], NZ)

    def leaf_o(i):
        so[i] = chunk_o(whose(i)).astype(BF16)
        tree_o(i).start()

    def branch_o(i):
        ro[...] = chunk_o(whose(i))
        tree_o(i - 6).wait_recv()
        ro[...] += zo[i - 6].astype(F32)

        @pl.when(core == i - 6)
        def _():
            tree_o(2).wait_recv()
            ro[...] += zo[2].astype(F32)

        so[i] = ro[...].astype(BF16)
        tree_o(i).start()

    def leaf_q(half, i):
        copy, buf = tree_q(half), sq.at[half]
        if i == 2:
            value = chunk_q(half)(whose(2)).astype(BF16)
            buf[2, 0 : ZR // 2] = value[0 : ZR // 2]
            buf[3, 0 : ZR // 2] = value[ZR // 2 : ZR]
            copy(2).start()
            copy(3).start()
        else:
            buf[i] = chunk_q(half)(whose(i)).astype(BF16)
            copy(i).start()

    def sum_of(half):
        return rq.at[0:ZR, half * 128 : half * 128 + 128]

    def branch_q(half, i):
        hold, copy = sum_of(half), tree_q(half)
        hold[...] = chunk_q(half)(whose(i))
        copy(i - 6).wait_recv()
        hold[...] += zq[half, i - 6].astype(F32)
        copy(i - 4).wait_recv()
        top = 0 if i == 6 else ZR // 2
        hold[top : top + ZR // 2] += zq[half, i - 4, 0 : ZR // 2].astype(F32)
        sq[half, i] = hold[...].astype(BF16)
        copy(i).start()

    gather_finish(0)
    for half in range(2):
        for d in range(1, NM):
            column_copy(half, d).wait_recv()
        for i in (2, 0, 1):
            leaf_q(half, i)
    for i in (4, 5):
        leaf_q(0, i)
    for i in (6, 7):
        branch_q(0, i)

    gather_finish(1)
    for d in range(1, NM):
        g_copy(d).wait_recv()
    o32[0:ZR, :] = nn(gpg[...], atg[...])
    for k in range(NZ):
        opad[k, :, 0:HW] = o32[FR * k : FR * k + 16, :]
        for t in range(HW // 128):
            row, col = 4 * (t % 4), HW + t // 4 * 128
            opad[k, row : row + 4, col : col + 128] = o32[FR * k + 16 : FR * k + FR, t * 128 : t * 128 + 128]
    for i in (2, 0, 1):
        leaf_o(i)
    for i in (4, 5):
        leaf_q(1, i)
    for i in (6, 7):
        branch_q(1, i)
    for i in (4, 5):
        leaf_o(i)
    for i in (6, 7):
        branch_o(i)

    def piece(half, to, slot, d):
        i = half * NM + d
        return remote(fin.at[half, to], finrecv.at[half, slot], fs.at[i], fr.at[i], {"mp": to})

    for half in range(2):
        hold = sum_of(half)
        hold[...] = chunk_q(half)(z)
        for i in (4, 5, 6, 7):
            tree_q(half)(i).wait_recv()
            hold[...] += zq[half, i].astype(F32)
        cols = slice(half * 128, half * 128 + 128)
        for i in range(NM):
            fin[half, i] = rq[FR * i : FR * i + 32, cols].astype(BF16)
        for d in range(1, NM):
            piece(half, lax.rem(m + d, NM), m, d).start()
        finrecv[half, m] = fin[half, m]

    sum_gain = dgain[0]
    for d in range(1, NM):
        gain_mp(d).wait_recv()
        sum_gain = sum_gain + dgrecv[d]
    dgz[0] = sum_gain
    for d in range(1, NZ):
        gain_dp(d).start()

    ro[...] = chunk_o(z)
    for i in (4, 5, 6, 7):
        tree_o(i).wait_recv()
        ro[...] += zo[i].astype(F32)
    oo[0:16, 0, :] = ro[:, 0:HW]
    for t in range(HW // 128):
        row, col = 4 * (t % 4), HW + t // 4 * 128
        oo[16:FR, 0, t * 128 : t * 128 + 128] = ro[row : row + 4, col : col + 128]
    store_o = pltpu.make_async_copy(oo, out_o, o_sem.at[2 * CHUNKS])
    store_o.start()

    sum_gain = dgz[0]
    for d in range(1, NZ):
        gain_dp(d).wait_recv()
        sum_gain = sum_gain + dgzrecv[d]
    dgz[1] = sum_gain
    store_gain = pltpu.make_async_copy(dgz.at[1], out_gain, o_sem.at[2 * CHUNKS + 1])
    store_gain.start()

    @pl.when(s < NS - 1)
    def _():
        for j in range(FAR):
            hop_forward(j).wait_send()
        far_forward(0).wait_send()
        near_forward().wait_send()

    @pl.when(s > 0)
    def _():
        for j in range(FAR):
            hop_back(j).wait_send()
        far_back(0).wait_send()
        near_back().wait_send()

    for where, slots in ((0, (2, 3)), (1, (0,)), (2, (2,)), (3, (0, 1))):

        @pl.when(s == where)
        def _():
            for slot in slots:
                pass_on(slot, 0).wait_send()

    for i in range(NM - 1):
        for w in range(2):
            gather_copy(w, m, i, sibling).wait_send()
    for d in range(1, NM):
        for half in range(2):
            column_copy(half, d).wait_send()
        g_copy(d).wait_send()
        gain_mp(d).wait_send()
    for d in range(1, NZ):
        gain_dp(d).wait_send()
    for i in range(8):
        tree_q(0)(i).wait_send()
        tree_q(1)(i).wait_send()
        if i != 3:
            tree_o(i).wait_send()
    for j in range(CHUNKS):
        store_act(j).wait()
        store_gin(j).wait()

    for half in range(2):
        for d in range(1, NM):
            source = lax.rem(m + NM - d, NM)
            piece(half, source, source, d).wait_recv()
        for i in range(NM):
            first = 256 * i + 128 * half
            if first < 3 * HW:
                oq[:, 0, first : first + 128] = finrecv[half, i].astype(F32)[0:FR]
    store_q = pltpu.make_async_copy(oq, out_q, o_sem.at[2 * CHUNKS + 2])
    store_q.start()
    for half in range(2):
        for d in range(1, NM):
            piece(half, lax.rem(m + d, NM), m, d).wait_send()
    store_o.wait()
    store_gain.wait()
    store_q.wait()


def finish(act, gin, out_q, out_o, gain, act2, gin2, out_q2, out_o2, gain2, a, b, c, d, e, f, sem):
    there = ((gain, e), (act, a), (gin, b), (out_q, c), (out_o, d))
    back = ((f, gain2), (a, act2), (b, gin2), (c, out_q2), (d, out_o2))
    reads = [pltpu.make_async_copy(x, y, sem.at[i]) for i, (x, y) in enumerate(there)]
    writes = [pltpu.make_async_copy(x, y, sem.at[5 + i]) for i, (x, y) in enumerate(back)]
    for r in reads:
        r.start()
    place = (lax.axis_index("dp") * NM + lax.axis_index("mp")) * FR
    for i, (r, w) in enumerate(zip(reads, writes)):
        r.wait()
        if i == 0:
            rows = jnp.broadcast_to(e[...], (8, VD))
            f[...] = pltpu.roll(rows, lax.rem(VD - place, VD), 1)[0:1, 0:FR]
        w.start()
    for w in writes:
        w.wait()


def on_device(patches, windows, gain, w_qkv, w_out, cotangent):
    hbm = pl.BlockSpec(memory_space=pl.ANY)
    dma = pltpu.SemaphoreType.DMA
    scratch = [
        pltpu.VMEM((VD, 3 * HW), BF16),
        pltpu.VMEM((HW, VD), BF16),
        pltpu.VMEM((1, ROWS), jnp.int32),
        pltpu.VMEM((1, VD), F32),
        pltpu.VMEM((CHUNKS, ROWS, CW), BF16),
        pltpu.VMEM((CHUNKS, ROWS, CW), BF16),
        pltpu.VMEM((CHUNKS, ROWS, CW), BF16),
        pltpu.VMEM((CHUNKS, ROWS, CW), BF16),
        pltpu.VMEM((ROWS, 3 * HW), F32),
        pltpu.VMEM((ROWS, HW), F32),
        pltpu.VMEM((ROWS, 3 * HW), BF16),
        pltpu.VMEM((HEADS, ROWS, ROWS), F32),
        pltpu.VMEM((HEADS * ROWS, ROWS), BF16),
        pltpu.VMEM((ROWS, HEADS * ROWS), BF16),
        pltpu.VMEM((ROWS, HW), BF16),
        pltpu.VMEM((len(PAIRS), ROWS, 128), BF16),
        pltpu.VMEM((len(PAIRS) * ROWS, 128), BF16),
        pltpu.VMEM((len(PAIRS) * ROWS, 128), BF16),
        pltpu.VMEM((len(PAIRS) * ROWS, 128), BF16),
        pltpu.VMEM((len(PAIRS) * ROWS, 128), BF16),
        pltpu.VMEM((HEADS * ROWS, ROWS), BF16),
        pltpu.VMEM((ROWS, HEADS * ROWS), BF16),
        pltpu.VMEM((ROWS, HW), BF16),
        pltpu.VMEM((ROWS, 2048), BF16),
        pltpu.VMEM((CHUNKS, ROWS, CW), F32),
        pltpu.VMEM((ROWS, 1), F32),
        pltpu.VMEM((3 * HW, VD), BF16),
        pltpu.VMEM((FR, 1, 3 * HW), F32),
        pltpu.VMEM((FR, 1, HW), F32),
        pltpu.VMEM((4, 2, HALF, CW), BF16),
        pltpu.VMEM((VD, NM * ROWS), BF16),
        pltpu.VMEM((NM * ROWS, HW), BF16),
        pltpu.VMEM((VD, ROWS), F32),
        pltpu.VMEM((VD, ROWS), F32),
        pltpu.VMEM((VD, ROWS), BF16),
        pltpu.VMEM((2, NM * ROWS, 128), BF16),
        pltpu.VMEM((ZR, NM * ROWS), BF16),
        pltpu.VMEM((ZR, HW), F32),
        pltpu.VMEM((NZ, 16, HW + 256), F32),
        pltpu.VMEM((1, 1, VD), F32),
        pltpu.VMEM((NM, 1, VD), F32),
        pltpu.VMEM((2, 1, VD), F32),
        pltpu.VMEM((NZ, 1, VD), F32),
        pltpu.VMEM((ZR + 32, 256), F32),
        pltpu.VMEM((16, HW + 256), F32),
        pltpu.VMEM((2, 8, ZR, 128), BF16),
        pltpu.VMEM((8, 16, HW + 256), BF16),
        pltpu.VMEM((2, 8, ZR, 128), BF16),
        pltpu.VMEM((8, 16, HW + 256), BF16),
        pltpu.VMEM((2, NM, 32, 128), BF16),
        pltpu.VMEM((2, NM, 32, 128), BF16),
        dma((8,)), dma((CHUNKS,)), dma((2 * CHUNKS + 3,)),
        dma((8,)), dma((8,)), dma((8,)), dma((8,)),
    ] + [dma((16,)) for _ in range(21)]
    shapes = (
        jax.ShapeDtypeStruct((ROWS, VD), BF16),
        jax.ShapeDtypeStruct((ROWS, VD), BF16),
        jax.ShapeDtypeStruct((FR, 1, 3 * HW), F32),
        jax.ShapeDtypeStruct((FR, 1, HW), F32),
        jax.ShapeDtypeStruct((1, VD), F32),
    )
    results = pl.pallas_call(
        kernel,
        out_shape=shapes,
        in_specs=[hbm] * 6,
        out_specs=(hbm,) * 5,
        scratch_shapes=scratch,
        compiler_params=pltpu.CompilerParams(
            collective_id=0, has_side_effects=True, vmem_limit_bytes=60 * 1024 * 1024
        ),
    )(patches[0], cotangent[0], windows, gain, w_qkv[0], w_out[0])
    act, gin, out_q, out_o, own_gain = pl.pallas_call(
        finish,
        out_shape=shapes[:4] + (jax.ShapeDtypeStruct((1, FR), F32),),
        in_specs=[hbm] * 5,
        out_specs=(hbm,) * 5,
        scratch_shapes=[pltpu.VMEM(x.shape, x.dtype) for x in shapes] + [pltpu.VMEM((1, FR), F32), dma((10,))],
        compiler_params=pltpu.CompilerParams(vmem_limit_bytes=60 * 1024 * 1024),
    )(*results)
    return (
        act[None, None],
        gin[None, None],
        out_q.transpose(1, 0, 2),
        out_o.transpose(1, 2, 0),
        own_gain,
    )


def solution(mesh):
    in_specs = (
        P(None, ("dp", "mp"), None),
        P(None, ("dp", "mp")),
        P("section", None),
        P("section", None, None),
        P("section", None, None),
        P(None, ("dp", "mp"), None),
    )
    out_specs = (
        P("section", None, ("dp", "mp"), None),
        P("section", None, ("dp", "mp"), None),
        P("section", ("dp", "mp"), None),
        P("section", None, ("dp", "mp")),
        P("section", ("dp", "mp")),
    )
    return jax.shard_map(
        on_device, mesh=mesh, in_specs=in_specs, out_specs=out_specs, check_vma=False
    )
```

```python
import jax
import jax.numpy as jnp
from jax import lax
from jax.experimental import pallas as pl
from jax.experimental.pallas import tpu as pltpu
from jax.sharding import PartitionSpec as P

HEAD = 80
HEADS = 8
ROWS = 128
VD = 1280
HW = 640
NM = 8
NZ = 8
NS = 4
CHUNKS = 5
CW = VD // CHUNKS
FAR = CHUNKS - 1
SENT = (FAR,) + tuple(range(FAR))
HALF = ROWS // 2
ZR = VD // NZ
FR = ZR // NM
SCALE = HEAD**-0.5
MESH = pl.DeviceIdType.MESH
F32 = jnp.float32
BF16 = jnp.bfloat16


def nt(a, b):
    return lax.dot_general(a, b, (((1,), (1,)), ((), ())), preferred_element_type=F32)


def nn(a, b):
    return lax.dot_general(a, b, (((1,), (0,)), ((), ())), preferred_element_type=F32)


def tn(a, b):
    return lax.dot_general(a, b, (((0,), (0,)), ((), ())), preferred_element_type=F32)


def tiles_of(h):
    return range(HEAD * h // 128, -(-(HEAD * h + HEAD) // 128))


def heads_of(t):
    return [h for h in range(HEADS) if t in tiles_of(h)]


PAIRS = [(t, h) for t in range(HW // 128) for h in heads_of(t)]


def pair_rows(t):
    first = PAIRS.index((t, heads_of(t)[0]))
    return slice(first * ROWS, (first + len(heads_of(t))) * ROWS)


def head_rows(t):
    heads = heads_of(t)
    return slice(heads[0] * ROWS, (heads[-1] + 1) * ROWS)


def gathered(stack, h):
    parts = []
    for t in tiles_of(h):
        i = PAIRS.index((t, h))
        parts.append(stack[i * ROWS : (i + 1) * ROWS, :])
    return parts[0] if len(parts) == 1 else jnp.concatenate(parts, axis=1)


def span(h):
    tiles = tiles_of(h)
    return tiles[0] * 128, tiles[-1] * 128 + 128


def kernel(
    patches, cot, win_hbm, gain_hbm, wq_hbm, wo_hbm,
    act, gin, out_q, out_o, out_gain,
    wq, wo, win, gain, hbuf, gbuf, hout, gout, pacc, dacc, packed, pt32, ptb, ptl, att, mk, qm, km, vm, dam, dsr, dsl,
    datt, dp, lifted, rs, wqt, oq, oo, rbuf,
    ngt, atg, gt32, gp32, gperm, dpg, gpg, o32, opad, dgain, dgrecv, dgz, dgzrecv,
    rq, ro, sq, so, zq, zo, fin, finrecv,
    w_sem, in_sem, o_sem, hs, hr, gs, gr, ns, nr, as_, ar, ds, dr, ps, pr, vs, vr, us, ur, qs, qr, os_, or_, fs, fr, ls, lr, ts,
):
    s = lax.axis_index("section")
    m = lax.axis_index("mp")
    z = lax.axis_index("dp")

    def cols_of(j):
        return pl.ds(j * CW, CW)

    def load_patches(j):
        return pltpu.make_async_copy(patches.at[:, cols_of(j)], hbuf.at[j], in_sem.at[j])

    def load_cot(j):
        return pltpu.make_async_copy(cot.at[:, cols_of(j)], gbuf.at[j], in_sem.at[j])

    def load_wq(j):
        return pltpu.make_async_copy(wq_hbm.at[cols_of(j)], wq.at[cols_of(j)], w_sem.at[j])

    load_wo = pltpu.make_async_copy(wo_hbm, wo, w_sem.at[5])
    load_gain = pltpu.make_async_copy(gain_hbm, gain, w_sem.at[6])
    load_win = pltpu.make_async_copy(win_hbm, win, w_sem.at[7])

    load_gain.start()

    @pl.when(s == 0)
    def _():
        for j in range(CHUNKS):
            load_patches(j).start()

    for j in range(CHUNKS):
        load_wq(j).start()
    load_win.start()
    load_wo.start()

    @pl.when(s == NS - 1)
    def _():
        for j in range(CHUNKS):
            load_cot(j).start()

    barrier = pltpu.get_barrier_semaphore()
    for d in range(1, NM):
        pl.semaphore_signal(barrier, inc=1, device_id={"mp": lax.rem(m + d, NM)}, device_id_type=MESH)
    for d in range(1, NZ):
        pl.semaphore_signal(barrier, inc=1, device_id={"dp": lax.rem(z + d, NZ)}, device_id_type=MESH)
    for d in range(1, NS):
        pl.semaphore_signal(barrier, inc=1, device_id={"section": lax.rem(s + d, NS)}, device_id_type=MESH)

    dp[:, 3 * HW : 2048] = jnp.zeros((ROWS, 2048 - 3 * HW), BF16)
    rq[ZR : ZR + 32, :] = jnp.zeros((32, 256), F32)
    for i, (t, h) in enumerate(PAIRS):
        cols = lax.broadcasted_iota(jnp.int32, (ROWS, 128), 1) + t * 128
        inside = (cols >= HEAD * h) & (cols < HEAD * h + HEAD)
        mk[i] = jnp.where(inside, 1.0, 0.0).astype(BF16)
    opad[:, :, HW : HW + 256] = jnp.zeros((NZ, 16, 256), F32)

    def remote(src, dst, ssem, rsem, where):
        return pltpu.make_async_remote_copy(
            src_ref=src, dst_ref=dst, send_sem=ssem, recv_sem=rsem, device_id=where, device_id_type=MESH
        )

    def hop_forward(j):
        return remote(hout.at[j], hbuf.at[j], hs.at[j], hr.at[j], {"section": lax.rem(s + 1, NS)})

    def hop_back(j):
        return remote(gout.at[j], gbuf.at[j], gs.at[j], gr.at[j], {"section": lax.rem(s + NS - 1, NS)})

    def half_rows(i):
        return pl.ds(i * HALF, HALF)

    def far_forward(i):
        slot = lax.rem(s, 2)
        to = {"section": lax.rem(s + 3 - lax.rem(s, 2), NS)}
        return remote(hout.at[FAR, half_rows(i)], rbuf.at[slot, i], ls.at[i], lr.at[slot * 2 + i], to)

    def far_back(i):
        slot = 3 - lax.rem(s, 2)
        to = {"section": lax.rem(s + 2 - lax.rem(s, 2), NS)}
        return remote(gout.at[FAR, half_rows(i)], rbuf.at[slot, i], ls.at[2 + i], lr.at[slot * 2 + i], to)

    def near_forward():
        half = half_rows(1)
        to = {"section": lax.rem(s + 1, NS)}
        return remote(hout.at[FAR, half], hbuf.at[FAR, half], hs.at[FAR], hr.at[FAR + 1], to)

    def near_back():
        half = half_rows(1)
        to = {"section": lax.rem(s + NS - 1, NS)}
        return remote(gout.at[FAR, half], gbuf.at[FAR, half], gs.at[FAR], gr.at[FAR + 1], to)

    def last_back():
        half = half_rows(0)
        return remote(gout.at[FAR, half], gbuf.at[FAR, half], ls.at[2], gr.at[FAR], {"section": lax.rem(s + NS - 1, NS)})

    def pass_on(slot, i):
        to = {"section": lax.rem(s + (2, 3, 2, 1)[slot], NS)}
        if slot < 2:
            return remote(rbuf.at[slot, i], hbuf.at[FAR, half_rows(i)], ts.at[slot * 2 + i], hr.at[FAR + i], to)
        return remote(rbuf.at[slot, i], gbuf.at[FAR, half_rows(i)], ts.at[slot * 2 + i], gr.at[FAR + i], to)

    def relay(slot):
        for i in range(1):
            remote(rbuf.at[slot, i], rbuf.at[slot, i], ts.at[slot * 2 + i], lr.at[slot * 2 + i], {"section": lax.rem(s + 1, NS)}).wait_recv()
            pass_on(slot, i).start()

    def forward_send(j):
        if j == FAR:
            far_forward(0).start()
        else:
            hop_forward(j).start()
            if j == FAR - 1:
                near_forward().start()

    def forward_arrived(j):
        if j == FAR:
            pass_on(0, 0).wait_recv()
            near_forward().wait_recv()
        else:
            hop_forward(j).wait_recv()

    def back_send(j):
        if j == FAR:

            @pl.when(s > 1)
            def _():
                far_back(0).start()

            @pl.when(s == 1)
            def _():
                last_back().start()
        else:
            hop_back(j).start()
            if j == FAR - 1:
                near_back().start()

    def back_arrived(j):
        if j == FAR:
            pass_on(2, 0).wait_recv()
            near_back().wait_recv()
        else:
            hop_back(j).wait_recv()

    def mp_lanes(i):
        return pl.ds(pl.multiple_of(i * ROWS, ROWS), ROWS)

    def fold(x):
        return x[:, 0:128] + x[:, 128:256]

    def column_copy(half, d):
        to = lax.rem(m + d, NM)
        cols = pl.ds(pl.multiple_of(to * 256 + half * 128, 128), 128)
        i = half * NM + d
        return remote(dp.at[:, cols], dpg.at[half, mp_lanes(m), :], ds.at[i], dr.at[i], {"mp": to})

    def g_copy(d):
        to = lax.rem(m + d, NM)
        rows = pl.ds(pl.multiple_of(to * ZR, 16), ZR)
        return remote(gperm.at[rows], gpg.at[:, mp_lanes(m)], ps.at[d], pr.at[d], {"mp": to})

    def columns_q():
        for half in range(2):
            for d in range(1, NM):
                column_copy(half, d).start()
        for half in range(2):
            cols = pl.ds(pl.multiple_of(m * 256 + half * 128, 128), 128)
            dpg[half, mp_lanes(m), :] = dp[:, cols]

    def turn_g(j):
        gt32[j * CW : (j + 1) * CW, :] = gbuf[j].astype(F32).T
        for first in range(0, VD, FR):
            if (first + FR - 1) // CW == j:
                i, k = first // FR % NM, first // FR // NM
                gp32[i * ZR + k * FR : i * ZR + k * FR + FR, :] = gt32[first : first + FR, :]

    def columns_g():
        gperm[...] = gp32[...].astype(BF16)
        for d in range(1, NM):
            g_copy(d).start()
        gpg[:, mp_lanes(m)] = gperm[pl.ds(pl.multiple_of(m * ZR, 16), ZR), :]

    def attend_back(j):
        part = nt(gbuf[j], wo[:, j * CW : (j + 1) * CW])
        if j == 0:
            dacc[...] = part
        else:
            dacc[...] += part

    @pl.when(s > 0)
    def _():
        load_wo.wait()
        pl.semaphore_wait(barrier, (NM - 1) + (NZ - 1) + (NS - 1))

    @pl.when(s == NS - 1)
    def _():
        for j in range(CHUNKS):
            load_cot(j).wait()
            attend_back(j)
            turn_g(j)
        columns_g()
        relay(0)
        relay(1)

    load_gain.wait()
    @pl.when(s >= 2)
    def _():
        for j in range(CHUNKS):
            load_wq(j).wait()
            wqt[:, j * CW : (j + 1) * CW] = wq[j * CW : (j + 1) * CW, :].T

    squares = jnp.zeros((ROWS, 128), F32)
    for j in range(CHUNKS):

        @pl.when(s == 0)
        def _():
            load_patches(j).wait()

        @pl.when(s > 0)
        def _():
            forward_arrived(j)

        @pl.when(s < 2)
        def _():
            load_wq(j).wait()

        wide = hbuf[j].astype(F32)
        squares = squares + fold(wide * wide)
        scaled = (wide * gain[:, j * CW : (j + 1) * CW]).astype(BF16)
        for i in range(3):
            part = nn(scaled, wq[j * CW : (j + 1) * CW, i * HW : (i + 1) * HW])
            if j == 0:
                pacc[:, i * HW : (i + 1) * HW] = part
            else:
                pacc[:, i * HW : (i + 1) * HW] += part
    spread = lax.rsqrt(jnp.sum(squares, axis=-1, keepdims=True) * (1.0 / VD) + 1e-6)
    rs[...] = spread
    packed[...] = (pacc[...] * spread).astype(BF16)
    load_win.wait()
    ids = jnp.broadcast_to(win[...].astype(F32), (ROWS, ROWS))
    same = ids.T == ids

    for i, (t, h) in enumerate(PAIRS):
        rows = slice(i * ROWS, (i + 1) * ROWS)
        km[rows, :] = packed[:, HW + t * 128 : HW + t * 128 + 128] * mk[i]
        vm[rows, :] = packed[:, 2 * HW + t * 128 : 2 * HW + t * 128 + 128] * mk[i]
    for h in range(HEADS):
        t0, t1 = span(h)
        scores = nt(gathered(km, h), packed[:, t0:t1]) * SCALE
        scores = jnp.where(same, scores, -1e30)
        top = jnp.max(scores, axis=0, keepdims=True)
        e = jnp.exp(scores - top)
        p = e / jnp.sum(e, axis=0, keepdims=True)
        pt32[h] = p
        ptb[h * ROWS : (h + 1) * ROWS, :] = p.astype(BF16)
    for t in range(HW // 128):
        att[:, t * 128 : t * 128 + 128] = tn(ptb[head_rows(t), :], vm[pair_rows(t), :]).astype(BF16)

    @pl.when(s == 0)
    def _():
        load_wo.wait()
        pl.semaphore_wait(barrier, (NM - 1) + (NZ - 1) + (NS - 1))

    def project(j):
        hout[j] = (hbuf[j].astype(F32) + nn(att[...], wo[:, j * CW : (j + 1) * CW])).astype(BF16)

    chip = m // 2
    core = lax.rem(m, 2)
    sibling = chip * 2 + 1 - core

    def gather_copy(which, slot, i, to):
        lanes = mp_lanes(slot)
        if which == 0:
            return remote(ngt.at[:, lanes], ngt.at[:, lanes], ns.at[i], nr.at[i], {"mp": to})
        return remote(atg.at[lanes, :], atg.at[lanes, :], as_.at[i], ar.at[i], {"mp": to})

    def across(d):
        return lax.rem(chip + d, NM // 2) * 2 + core

    def gather_start():
        for j in range(CHUNKS):
            wide = hbuf[j].astype(F32) * rs[...] * gain[:, j * CW : (j + 1) * CW]
            ngt[j * CW : (j + 1) * CW, mp_lanes(m)] = wide.astype(BF16).T
        atg[mp_lanes(m), :] = att[...]
        for w in range(2):
            for d in range(1, NM // 2):
                gather_copy(w, m, d, across(d)).start()
            gather_copy(w, m, 0, sibling).start()

    def gather_forward():
        for d in range(1, NM // 2):
            source = across(NM // 2 - d)
            for w in range(2):
                gather_copy(w, source, d, across(d)).wait_recv()
                gather_copy(w, source, NM // 2 - 1 + d, sibling).start()

    def gather_finish(w):
        gather_copy(w, sibling, 0, sibling).wait_recv()
        for d in range(1, NM // 2):
            source = lax.rem(chip + NM // 2 - d, NM // 2) * 2 + 1 - core
            gather_copy(w, source, NM // 2 - 1 + d, sibling).wait_recv()

    @pl.when(s < NS - 1)
    def _():
        for j in SENT:
            project(j)
            forward_send(j)

    gather_start()

    @pl.when(s == 0)
    def _():
        gather_forward()

    def turn_weights():
        for j in range(CHUNKS):
            wqt[:, j * CW : (j + 1) * CW] = wq[j * CW : (j + 1) * CW, :].T

    @pl.when(s < 2)
    def _():
        turn_weights()

    @pl.when(s == 1)
    def _():
        relay(0)
        gather_forward()

    @pl.when(s == 0)
    def _():
        relay(2)
        relay(3)

    for i, (t, h) in enumerate(PAIRS):
        qm[i * ROWS : (i + 1) * ROWS, :] = packed[:, t * 128 : t * 128 + 128] * mk[i]
    for h in range(HEADS):
        ptl[:, h * ROWS : (h + 1) * ROWS] = ptb[h * ROWS : (h + 1) * ROWS, :]

    for j in range(CHUNKS):

        @pl.when(s < NS - 1)
        def _():
            back_arrived(j)
            attend_back(j)

        if j != FAR:

            @pl.when(s == 0)
            def _():
                turn_g(j)

    datt[...] = dacc[...].astype(BF16)

    for i, (t, h) in enumerate(PAIRS):
        dam[i * ROWS : (i + 1) * ROWS, :] = datt[:, t * 128 : t * 128 + 128] * mk[i]
    for h in range(HEADS):
        t0, t1 = span(h)
        dprob = nt(gathered(vm, h), datt[:, t0:t1]).astype(BF16).astype(F32)
        p = pt32[h]
        dsc = p * (dprob - jnp.sum(p * dprob, axis=0, keepdims=True))
        dsc = (dsc * SCALE).astype(BF16)
        dsr[h * ROWS : (h + 1) * ROWS, :] = dsc
        dsl[:, h * ROWS : (h + 1) * ROWS] = dsc
    for t in range(HW // 128):
        c = t * 128
        dp[:, 2 * HW + c : 2 * HW + c + 128] = nn(ptl[:, head_rows(t)], dam[pair_rows(t), :]).astype(BF16)
    for t in range(HW // 128):
        c = t * 128
        dp[:, HW + c : HW + c + 128] = nn(dsl[:, head_rows(t)], qm[pair_rows(t), :]).astype(BF16)
        dp[:, c : c + 128] = tn(dsr[head_rows(t), :], km[pair_rows(t), :]).astype(BF16)

    @pl.when(s == 0)
    def _():
        columns_q()
        turn_g(FAR)
        columns_g()

    spread = rs[...]
    inner = jnp.zeros((ROWS, 128), F32)
    for t in range(3 * HW // 128):
        cols = slice(t * 128, t * 128 + 128)
        inner = inner + dp[:, cols].astype(F32) * pacc[:, cols]
    pull = jnp.sum(inner, axis=-1, keepdims=True) * (1.0 / VD) * (spread * spread * spread)
    for j in SENT:
        dn = nn(dp[:, 0 : 3 * HW], wqt[:, j * CW : (j + 1) * CW]).astype(BF16).astype(F32)
        up = dn * gain[:, j * CW : (j + 1) * CW]
        back = gbuf[j].astype(F32) + spread * up - hbuf[j].astype(F32) * pull
        gout[j] = back.astype(BF16)

        @pl.when(s > 0)
        def _():
            back_send(j)

        lifted[j] = dn

    def store_act(j):
        return pltpu.make_async_copy(hout.at[j], act.at[:, cols_of(j)], o_sem.at[j])

    def store_gin(j):
        return pltpu.make_async_copy(gout.at[j], gin.at[:, cols_of(j)], o_sem.at[CHUNKS + j])

    for j in range(CHUNKS):
        store_gin(j).start()

    @pl.when(s > 0)
    def _():
        columns_q()

    @pl.when((s > 0) & (s < NS - 1))
    def _():
        for j in range(CHUNKS):
            turn_g(j)
        columns_g()

    for j in range(CHUNKS):
        part = lifted[j] * (hbuf[j].astype(F32) * rs[...])
        dgain[0, :, j * CW : (j + 1) * CW] = jnp.sum(part, axis=0, keepdims=True)

    @pl.when(s == NS - 1)
    def _():
        for j in range(CHUNKS):
            project(j)

    @pl.when(s >= NS - 2)
    def _():
        gather_forward()

    for j in range(CHUNKS):
        store_act(j).start()

    def gain_mp(d):
        return remote(dgain.at[0], dgrecv.at[d], vs.at[d], vr.at[d], {"mp": lax.rem(m + d, NM)})

    def gain_dp(d):
        return remote(dgz.at[0], dgzrecv.at[d], us.at[d], ur.at[d], {"dp": lax.rem(z + d, NZ)})

    for d in range(1, NM):
        gain_mp(d).start()

    def chunk_q(half):
        def chunk(k):
            rows = pl.ds(pl.multiple_of(k * ZR, 16), ZR)
            return nn(ngt[rows, :], dpg[half])

        return chunk

    def chunk_o(k):
        return opad[k]

    steps = (NZ - 1, 1, NZ - 2, 2, NZ - 1, 1, NZ - 2, 2)
    owners = (NZ - 3, 3, 4, 4, NZ - 1, 1, NZ - 2, 2)

    def peer(i):
        return {"dp": lax.rem(z + steps[i], NZ)}

    def tree_q(half):
        def copy(i):
            n = half * 8 + i
            if i == 2 or i == 3:
                top = pl.ds(0, ZR // 2)
                return remote(sq.at[half, i, top], zq.at[half, i, top], qs.at[n], qr.at[n], peer(i))
            return remote(sq.at[half, i], zq.at[half, i], qs.at[n], qr.at[n], peer(i))

        return copy

    def tree_o(i):
        to = {"dp": lax.rem(z + NZ - 2 + 4 * core, NZ)} if i == 2 else peer(i)
        return remote(so.at[i], zo.at[i], os_.at[i], or_.at[i], to)

    def whose(i):
        return lax.rem(z + owners[i], NZ)

    def leaf_o(i):
        so[i] = chunk_o(whose(i)).astype(BF16)
        tree_o(i).start()

    def branch_o(i):
        ro[...] = chunk_o(whose(i))
        tree_o(i - 6).wait_recv()
        ro[...] += zo[i - 6].astype(F32)

        @pl.when(core == i - 6)
        def _():
            tree_o(2).wait_recv()
            ro[...] += zo[2].astype(F32)

        so[i] = ro[...].astype(BF16)
        tree_o(i).start()

    def leaf_q(half, i):
        copy, buf = tree_q(half), sq.at[half]
        if i == 2:
            value = chunk_q(half)(whose(2)).astype(BF16)
            buf[2, 0 : ZR // 2] = value[0 : ZR // 2]
            buf[3, 0 : ZR // 2] = value[ZR // 2 : ZR]
            copy(2).start()
            copy(3).start()
        else:
            buf[i] = chunk_q(half)(whose(i)).astype(BF16)
            copy(i).start()

    def sum_of(half):
        return rq.at[0:ZR, half * 128 : half * 128 + 128]

    def branch_q(half, i):
        hold, copy = sum_of(half), tree_q(half)
        hold[...] = chunk_q(half)(whose(i))
        copy(i - 6).wait_recv()
        hold[...] += zq[half, i - 6].astype(F32)
        copy(i - 4).wait_recv()
        top = 0 if i == 6 else ZR // 2
        hold[top : top + ZR // 2] += zq[half, i - 4, 0 : ZR // 2].astype(F32)
        sq[half, i] = hold[...].astype(BF16)
        copy(i).start()

    gather_finish(0)
    for half in range(2):
        for d in range(1, NM):
            column_copy(half, d).wait_recv()
        for i in (2, 0, 1):
            leaf_q(half, i)
    for i in (4, 5):
        leaf_q(0, i)
    for i in (6, 7):
        branch_q(0, i)

    gather_finish(1)
    for d in range(1, NM):
        g_copy(d).wait_recv()
    o32[0:ZR, :] = nn(gpg[...], atg[...])
    for k in range(NZ):
        opad[k, :, 0:HW] = o32[FR * k : FR * k + 16, :]
        for t in range(HW // 128):
            row, col = 4 * (t % 4), HW + t // 4 * 128
            opad[k, row : row + 4, col : col + 128] = o32[FR * k + 16 : FR * k + FR, t * 128 : t * 128 + 128]
    for i in (2, 0, 1):
        leaf_o(i)
    for i in (4, 5):
        leaf_q(1, i)
    for i in (6, 7):
        branch_q(1, i)
    for i in (4, 5):
        leaf_o(i)
    for i in (6, 7):
        branch_o(i)

    def piece(half, to, slot, d):
        i = half * NM + d
        return remote(fin.at[half, to], finrecv.at[half, slot], fs.at[i], fr.at[i], {"mp": to})

    for half in range(2):
        hold = sum_of(half)
        hold[...] = chunk_q(half)(z)
        for i in (4, 5, 6, 7):
            tree_q(half)(i).wait_recv()
            hold[...] += zq[half, i].astype(F32)
        cols = slice(half * 128, half * 128 + 128)
        for i in range(NM):
            fin[half, i] = rq[FR * i : FR * i + 32, cols].astype(BF16)
        for d in range(1, NM):
            piece(half, lax.rem(m + d, NM), m, d).start()
        finrecv[half, m] = fin[half, m]

    sum_gain = dgain[0]
    for d in range(1, NM):
        gain_mp(d).wait_recv()
        sum_gain = sum_gain + dgrecv[d]
    dgz[0] = sum_gain
    for d in range(1, NZ):
        gain_dp(d).start()

    ro[...] = chunk_o(z)
    for i in (4, 5, 6, 7):
        tree_o(i).wait_recv()
        ro[...] += zo[i].astype(F32)
    oo[0:16, 0, :] = ro[:, 0:HW]
    for t in range(HW // 128):
        row, col = 4 * (t % 4), HW + t // 4 * 128
        oo[16:FR, 0, t * 128 : t * 128 + 128] = ro[row : row + 4, col : col + 128]
    store_o = pltpu.make_async_copy(oo, out_o, o_sem.at[2 * CHUNKS])
    store_o.start()

    sum_gain = dgz[0]
    for d in range(1, NZ):
        gain_dp(d).wait_recv()
        sum_gain = sum_gain + dgzrecv[d]
    dgz[1] = sum_gain
    store_gain = pltpu.make_async_copy(dgz.at[1], out_gain, o_sem.at[2 * CHUNKS + 1])
    store_gain.start()

    @pl.when(s < NS - 1)
    def _():
        for j in range(FAR):
            hop_forward(j).wait_send()
        far_forward(0).wait_send()
        near_forward().wait_send()

    @pl.when(s > 0)
    def _():
        for j in range(FAR):
            hop_back(j).wait_send()
        last_back().wait_send()
        near_back().wait_send()

    for where, slots in ((0, (2, 3)), (1, (0,)), (3, (0, 1))):

        @pl.when(s == where)
        def _():
            for slot in slots:
                pass_on(slot, 0).wait_send()

    for i in range(NM - 1):
        for w in range(2):
            gather_copy(w, m, i, sibling).wait_send()
    for d in range(1, NM):
        for half in range(2):
            column_copy(half, d).wait_send()
        g_copy(d).wait_send()
        gain_mp(d).wait_send()
    for d in range(1, NZ):
        gain_dp(d).wait_send()
    for i in range(8):
        tree_q(0)(i).wait_send()
        tree_q(1)(i).wait_send()
        if i != 3:
            tree_o(i).wait_send()
    for j in range(CHUNKS):
        store_act(j).wait()
        store_gin(j).wait()

    for half in range(2):
        for d in range(1, NM):
            source = lax.rem(m + NM - d, NM)
            piece(half, source, source, d).wait_recv()
        for i in range(NM):
            first = 256 * i + 128 * half
            if first < 3 * HW:
                oq[:, 0, first : first + 128] = finrecv[half, i].astype(F32)[0:FR]
    store_q = pltpu.make_async_copy(oq, out_q, o_sem.at[2 * CHUNKS + 2])
    store_q.start()
    for half in range(2):
        for d in range(1, NM):
            piece(half, lax.rem(m + d, NM), m, d).wait_send()
    store_o.wait()
    store_gain.wait()
    store_q.wait()


def finish(act, gin, out_q, out_o, gain, act2, gin2, out_q2, out_o2, gain2, a, b, c, d, e, f, sem):
    there = ((gain, e), (act, a), (gin, b), (out_q, c), (out_o, d))
    back = ((f, gain2), (a, act2), (b, gin2), (c, out_q2), (d, out_o2))
    reads = [pltpu.make_async_copy(x, y, sem.at[i]) for i, (x, y) in enumerate(there)]
    writes = [pltpu.make_async_copy(x, y, sem.at[5 + i]) for i, (x, y) in enumerate(back)]
    for r in reads:
        r.start()
    place = (lax.axis_index("dp") * NM + lax.axis_index("mp")) * FR
    for i, (r, w) in enumerate(zip(reads, writes)):
        r.wait()
        if i == 0:
            rows = jnp.broadcast_to(e[...], (8, VD))
            f[...] = pltpu.roll(rows, lax.rem(VD - place, VD), 1)[0:1, 0:FR]
        w.start()
    for w in writes:
        w.wait()


def on_device(patches, windows, gain, w_qkv, w_out, cotangent):
    hbm = pl.BlockSpec(memory_space=pl.ANY)
    dma = pltpu.SemaphoreType.DMA
    scratch = [
        pltpu.VMEM((VD, 3 * HW), BF16),
        pltpu.VMEM((HW, VD), BF16),
        pltpu.VMEM((1, ROWS), jnp.int32),
        pltpu.VMEM((1, VD), F32),
        pltpu.VMEM((CHUNKS, ROWS, CW), BF16),
        pltpu.VMEM((CHUNKS, ROWS, CW), BF16),
        pltpu.VMEM((CHUNKS, ROWS, CW), BF16),
        pltpu.VMEM((CHUNKS, ROWS, CW), BF16),
        pltpu.VMEM((ROWS, 3 * HW), F32),
        pltpu.VMEM((ROWS, HW), F32),
        pltpu.VMEM((ROWS, 3 * HW), BF16),
        pltpu.VMEM((HEADS, ROWS, ROWS), F32),
        pltpu.VMEM((HEADS * ROWS, ROWS), BF16),
        pltpu.VMEM((ROWS, HEADS * ROWS), BF16),
        pltpu.VMEM((ROWS, HW), BF16),
        pltpu.VMEM((len(PAIRS), ROWS, 128), BF16),
        pltpu.VMEM((len(PAIRS) * ROWS, 128), BF16),
        pltpu.VMEM((len(PAIRS) * ROWS, 128), BF16),
        pltpu.VMEM((len(PAIRS) * ROWS, 128), BF16),
        pltpu.VMEM((len(PAIRS) * ROWS, 128), BF16),
        pltpu.VMEM((HEADS * ROWS, ROWS), BF16),
        pltpu.VMEM((ROWS, HEADS * ROWS), BF16),
        pltpu.VMEM((ROWS, HW), BF16),
        pltpu.VMEM((ROWS, 2048), BF16),
        pltpu.VMEM((CHUNKS, ROWS, CW), F32),
        pltpu.VMEM((ROWS, 1), F32),
        pltpu.VMEM((3 * HW, VD), BF16),
        pltpu.VMEM((FR, 1, 3 * HW), F32),
        pltpu.VMEM((FR, 1, HW), F32),
        pltpu.VMEM((4, 2, HALF, CW), BF16),
        pltpu.VMEM((VD, NM * ROWS), BF16),
        pltpu.VMEM((NM * ROWS, HW), BF16),
        pltpu.VMEM((VD, ROWS), F32),
        pltpu.VMEM((VD, ROWS), F32),
        pltpu.VMEM((VD, ROWS), BF16),
        pltpu.VMEM((2, NM * ROWS, 128), BF16),
        pltpu.VMEM((ZR, NM * ROWS), BF16),
        pltpu.VMEM((ZR, HW), F32),
        pltpu.VMEM((NZ, 16, HW + 256), F32),
        pltpu.VMEM((1, 1, VD), F32),
        pltpu.VMEM((NM, 1, VD), F32),
        pltpu.VMEM((2, 1, VD), F32),
        pltpu.VMEM((NZ, 1, VD), F32),
        pltpu.VMEM((ZR + 32, 256), F32),
        pltpu.VMEM((16, HW + 256), F32),
        pltpu.VMEM((2, 8, ZR, 128), BF16),
        pltpu.VMEM((8, 16, HW + 256), BF16),
        pltpu.VMEM((2, 8, ZR, 128), BF16),
        pltpu.VMEM((8, 16, HW + 256), BF16),
        pltpu.VMEM((2, NM, 32, 128), BF16),
        pltpu.VMEM((2, NM, 32, 128), BF16),
        dma((8,)), dma((CHUNKS,)), dma((2 * CHUNKS + 3,)),
        dma((8,)), dma((8,)), dma((8,)), dma((8,)),
    ] + [dma((16,)) for _ in range(21)]
    shapes = (
        jax.ShapeDtypeStruct((ROWS, VD), BF16),
        jax.ShapeDtypeStruct((ROWS, VD), BF16),
        jax.ShapeDtypeStruct((FR, 1, 3 * HW), F32),
        jax.ShapeDtypeStruct((FR, 1, HW), F32),
        jax.ShapeDtypeStruct((1, VD), F32),
    )
    results = pl.pallas_call(
        kernel,
        out_shape=shapes,
        in_specs=[hbm] * 6,
        out_specs=(hbm,) * 5,
        scratch_shapes=scratch,
        compiler_params=pltpu.CompilerParams(
            collective_id=0, has_side_effects=True, vmem_limit_bytes=60 * 1024 * 1024
        ),
    )(patches[0], cotangent[0], windows, gain, w_qkv[0], w_out[0])
    act, gin, out_q, out_o, own_gain = pl.pallas_call(
        finish,
        out_shape=shapes[:4] + (jax.ShapeDtypeStruct((1, FR), F32),),
        in_specs=[hbm] * 5,
        out_specs=(hbm,) * 5,
        scratch_shapes=[pltpu.VMEM(x.shape, x.dtype) for x in shapes] + [pltpu.VMEM((1, FR), F32), dma((10,))],
        compiler_params=pltpu.CompilerParams(vmem_limit_bytes=60 * 1024 * 1024),
    )(*results)
    return (
        act[None, None],
        gin[None, None],
        out_q.transpose(1, 0, 2),
        out_o.transpose(1, 2, 0),
        own_gain,
    )


def solution(mesh):
    in_specs = (
        P(None, ("dp", "mp"), None),
        P(None, ("dp", "mp")),
        P("section", None),
        P("section", None, None),
        P("section", None, None),
        P(None, ("dp", "mp"), None),
    )
    out_specs = (
        P("section", None, ("dp", "mp"), None),
        P("section", None, ("dp", "mp"), None),
        P("section", ("dp", "mp"), None),
        P("section", None, ("dp", "mp")),
        P("section", ("dp", "mp")),
    )
    return jax.shard_map(
        on_device, mesh=mesh, in_specs=in_specs, out_specs=out_specs, check_vma=False
    )
```

```python
import jax
import jax.numpy as jnp
from jax import lax
from jax.experimental import pallas as pl
from jax.experimental.pallas import tpu as pltpu
from jax.sharding import PartitionSpec as P

HEAD = 80
HEADS = 8
ROWS = 128
VD = 1280
HW = 640
NM = 8
NZ = 8
NS = 4
CHUNKS = 5
CW = VD // CHUNKS
FAR = CHUNKS - 1
SENT = (FAR,) + tuple(range(FAR))
HALF = ROWS // 2
ZR = VD // NZ
FR = ZR // NM
SCALE = HEAD**-0.5
MESH = pl.DeviceIdType.MESH
F32 = jnp.float32
BF16 = jnp.bfloat16


def nt(a, b):
    return lax.dot_general(a, b, (((1,), (1,)), ((), ())), preferred_element_type=F32)


def nn(a, b):
    return lax.dot_general(a, b, (((1,), (0,)), ((), ())), preferred_element_type=F32)


def tn(a, b):
    return lax.dot_general(a, b, (((0,), (0,)), ((), ())), preferred_element_type=F32)


def tiles_of(h):
    return range(HEAD * h // 128, -(-(HEAD * h + HEAD) // 128))


def heads_of(t):
    return [h for h in range(HEADS) if t in tiles_of(h)]


PAIRS = [(t, h) for t in range(HW // 128) for h in heads_of(t)]


def pair_rows(t):
    first = PAIRS.index((t, heads_of(t)[0]))
    return slice(first * ROWS, (first + len(heads_of(t))) * ROWS)


def head_rows(t):
    heads = heads_of(t)
    return slice(heads[0] * ROWS, (heads[-1] + 1) * ROWS)


def gathered(stack, h):
    parts = []
    for t in tiles_of(h):
        i = PAIRS.index((t, h))
        parts.append(stack[i * ROWS : (i + 1) * ROWS, :])
    return parts[0] if len(parts) == 1 else jnp.concatenate(parts, axis=1)


def span(h):
    tiles = tiles_of(h)
    return tiles[0] * 128, tiles[-1] * 128 + 128


def kernel(
    patches, cot, win_hbm, gain_hbm, wq_hbm, wo_hbm,
    act, gin, out_q, out_o, out_gain,
    wq, wo, win, gain, hbuf, gbuf, hout, gout, pacc, dacc, packed, pt32, ptb, ptl, att, mk, qm, km, vm, dam, dsr, dsl,
    datt, dp, lifted, rs, wqt, oq, oo, rbuf,
    ngt, atg, gt32, gp32, gperm, dpg, gpg, o32, opad, dgain, dgrecv, dgz, dgzrecv,
    rq, ro, sq, so, zq, zo, fin, finrecv,
    w_sem, in_sem, o_sem, hs, hr, gs, gr, ns, nr, as_, ar, ds, dr, ps, pr, vs, vr, us, ur, qs, qr, os_, or_, fs, fr, ls, lr, ts,
):
    s = lax.axis_index("section")
    m = lax.axis_index("mp")
    z = lax.axis_index("dp")

    def cols_of(j):
        return pl.ds(j * CW, CW)

    def load_patches(j):
        return pltpu.make_async_copy(patches.at[:, cols_of(j)], hbuf.at[j], in_sem.at[j])

    def load_cot(j):
        return pltpu.make_async_copy(cot.at[:, cols_of(j)], gbuf.at[j], in_sem.at[j])

    def load_wq(j):
        return pltpu.make_async_copy(wq_hbm.at[cols_of(j)], wq.at[cols_of(j)], w_sem.at[j])

    load_wo = pltpu.make_async_copy(wo_hbm, wo, w_sem.at[5])
    load_gain = pltpu.make_async_copy(gain_hbm, gain, w_sem.at[6])
    load_win = pltpu.make_async_copy(win_hbm, win, w_sem.at[7])

    load_gain.start()

    @pl.when(s == 0)
    def _():
        for j in range(CHUNKS):
            load_patches(j).start()

    for j in range(CHUNKS):
        load_wq(j).start()
    load_win.start()
    load_wo.start()

    @pl.when(s == NS - 1)
    def _():
        for j in range(CHUNKS):
            load_cot(j).start()

    barrier = pltpu.get_barrier_semaphore()
    for d in range(1, NM):
        pl.semaphore_signal(barrier, inc=1, device_id={"mp": lax.rem(m + d, NM)}, device_id_type=MESH)
    for d in range(1, NZ):
        pl.semaphore_signal(barrier, inc=1, device_id={"dp": lax.rem(z + d, NZ)}, device_id_type=MESH)
    for d in range(1, NS):
        pl.semaphore_signal(barrier, inc=1, device_id={"section": lax.rem(s + d, NS)}, device_id_type=MESH)

    dp[:, 3 * HW : 2048] = jnp.zeros((ROWS, 2048 - 3 * HW), BF16)
    rq[ZR : ZR + 32, :] = jnp.zeros((32, 256), F32)
    for i, (t, h) in enumerate(PAIRS):
        cols = lax.broadcasted_iota(jnp.int32, (ROWS, 128), 1) + t * 128
        inside = (cols >= HEAD * h) & (cols < HEAD * h + HEAD)
        mk[i] = jnp.where(inside, 1.0, 0.0).astype(BF16)
    opad[:, :, HW : HW + 256] = jnp.zeros((NZ, 16, 256), F32)

    def remote(src, dst, ssem, rsem, where):
        return pltpu.make_async_remote_copy(
            src_ref=src, dst_ref=dst, send_sem=ssem, recv_sem=rsem, device_id=where, device_id_type=MESH
        )

    def hop_forward(j):
        return remote(hout.at[j], hbuf.at[j], hs.at[j], hr.at[j], {"section": lax.rem(s + 1, NS)})

    def hop_back(j):
        return remote(gout.at[j], gbuf.at[j], gs.at[j], gr.at[j], {"section": lax.rem(s + NS - 1, NS)})

    def half_rows(i):
        return pl.ds(i * HALF, HALF)

    def far_forward(i):
        slot = lax.rem(s, 2)
        to = {"section": lax.rem(s + 3 - lax.rem(s, 2), NS)}
        return remote(hout.at[FAR, half_rows(i)], rbuf.at[slot, i], ls.at[i], lr.at[slot * 2 + i], to)

    def far_back(i):
        slot = 3 - lax.rem(s, 2)
        to = {"section": lax.rem(s + 2 - lax.rem(s, 2), NS)}
        return remote(gout.at[FAR, half_rows(i)], rbuf.at[slot, i], ls.at[2 + i], lr.at[slot * 2 + i], to)

    def near_forward():
        half = half_rows(1)
        to = {"section": lax.rem(s + 1, NS)}
        return remote(hout.at[FAR, half], hbuf.at[FAR, half], hs.at[FAR], hr.at[FAR + 1], to)

    def near_back():
        half = half_rows(1)
        to = {"section": lax.rem(s + NS - 1, NS)}
        return remote(gout.at[FAR, half], gbuf.at[FAR, half], gs.at[FAR], gr.at[FAR + 1], to)

    def last_back():
        half = half_rows(0)
        return remote(gout.at[FAR, half], gbuf.at[FAR, half], ls.at[2], gr.at[FAR], {"section": lax.rem(s + NS - 1, NS)})

    def pass_on(slot, i):
        to = {"section": lax.rem(s + (2, 3, 2, 1)[slot], NS)}
        if slot < 2:
            return remote(rbuf.at[slot, i], hbuf.at[FAR, half_rows(i)], ts.at[slot * 2 + i], hr.at[FAR + i], to)
        return remote(rbuf.at[slot, i], gbuf.at[FAR, half_rows(i)], ts.at[slot * 2 + i], gr.at[FAR + i], to)

    def relay(slot):
        for i in range(1):
            remote(rbuf.at[slot, i], rbuf.at[slot, i], ts.at[slot * 2 + i], lr.at[slot * 2 + i], {"section": lax.rem(s + 1, NS)}).wait_recv()
            pass_on(slot, i).start()

    def forward_send(j):
        if j == FAR:
            far_forward(0).start()
        else:
            hop_forward(j).start()
            if j == FAR - 1:
                near_forward().start()

    def forward_arrived(j):
        if j == FAR:
            pass_on(0, 0).wait_recv()
            near_forward().wait_recv()
        else:
            hop_forward(j).wait_recv()

    def back_send(j):
        if j == FAR:

            @pl.when(s > 1)
            def _():
                far_back(0).start()

            @pl.when(s == 1)
            def _():
                last_back().start()
        else:
            hop_back(j).start()
            if j == FAR - 1:
                near_back().start()

    def back_arrived(j):
        if j == FAR:
            pass_on(2, 0).wait_recv()
            near_back().wait_recv()
        else:
            hop_back(j).wait_recv()

    def mp_lanes(i):
        return pl.ds(pl.multiple_of(i * ROWS, ROWS), ROWS)

    def fold(x):
        return x[:, 0:128] + x[:, 128:256]

    def column_copy(half, d):
        to = lax.rem(m + d, NM)
        cols = pl.ds(pl.multiple_of(to * 256 + half * 128, 128), 128)
        i = half * NM + d
        return remote(dp.at[:, cols], dpg.at[half, mp_lanes(m), :], ds.at[i], dr.at[i], {"mp": to})

    def g_copy(d):
        to = lax.rem(m + d, NM)
        rows = pl.ds(pl.multiple_of(to * ZR, 16), ZR)
        return remote(gperm.at[rows], gpg.at[:, mp_lanes(m)], ps.at[d], pr.at[d], {"mp": to})

    def columns_q():
        for half in range(2):
            for d in range(1, NM):
                column_copy(half, d).start()
        for half in range(2):
            cols = pl.ds(pl.multiple_of(m * 256 + half * 128, 128), 128)
            dpg[half, mp_lanes(m), :] = dp[:, cols]

    def turn_g(j):
        gt32[j * CW : (j + 1) * CW, :] = gbuf[j].astype(F32).T
        for first in range(0, VD, FR):
            if (first + FR - 1) // CW == j:
                i, k = first // FR % NM, first // FR // NM
                gp32[i * ZR + k * FR : i * ZR + k * FR + FR, :] = gt32[first : first + FR, :]

    def columns_g():
        gperm[...] = gp32[...].astype(BF16)
        for d in range(1, NM):
            g_copy(d).start()
        gpg[:, mp_lanes(m)] = gperm[pl.ds(pl.multiple_of(m * ZR, 16), ZR), :]

    def attend_back(j):
        part = nt(gbuf[j], wo[:, j * CW : (j + 1) * CW])
        if j == 0:
            dacc[...] = part
        else:
            dacc[...] += part

    @pl.when(s > 0)
    def _():
        load_wo.wait()
        pl.semaphore_wait(barrier, (NM - 1) + (NZ - 1) + (NS - 1))

    @pl.when(s == NS - 1)
    def _():
        for j in range(CHUNKS):
            load_cot(j).wait()
            attend_back(j)
            turn_g(j)
        columns_g()
        relay(0)
        relay(1)

    load_gain.wait()
    @pl.when(s >= 2)
    def _():
        for j in range(CHUNKS):
            load_wq(j).wait()
            wqt[:, j * CW : (j + 1) * CW] = wq[j * CW : (j + 1) * CW, :].T

    squares = jnp.zeros((ROWS, 128), F32)
    for j in range(CHUNKS):

        @pl.when(s == 0)
        def _():
            load_patches(j).wait()

        @pl.when(s > 0)
        def _():
            forward_arrived(j)

        @pl.when(s < 2)
        def _():
            load_wq(j).wait()

        wide = hbuf[j].astype(F32)
        squares = squares + fold(wide * wide)
        scaled = (wide * gain[:, j * CW : (j + 1) * CW]).astype(BF16)
        for i in range(3):
            part = nn(scaled, wq[j * CW : (j + 1) * CW, i * HW : (i + 1) * HW])
            if j == 0:
                pacc[:, i * HW : (i + 1) * HW] = part
            else:
                pacc[:, i * HW : (i + 1) * HW] += part
    spread = lax.rsqrt(jnp.sum(squares, axis=-1, keepdims=True) * (1.0 / VD) + 1e-6)
    rs[...] = spread
    packed[...] = (pacc[...] * spread).astype(BF16)
    load_win.wait()
    ids = jnp.broadcast_to(win[...].astype(F32), (ROWS, ROWS))
    same = ids.T == ids

    for i, (t, h) in enumerate(PAIRS):
        rows = slice(i * ROWS, (i + 1) * ROWS)
        km[rows, :] = packed[:, HW + t * 128 : HW + t * 128 + 128] * mk[i]
        vm[rows, :] = packed[:, 2 * HW + t * 128 : 2 * HW + t * 128 + 128] * mk[i]
    for h in range(HEADS):
        t0, t1 = span(h)
        scores = nt(gathered(km, h), packed[:, t0:t1]) * SCALE
        scores = jnp.where(same, scores, -1e30)
        top = jnp.max(scores, axis=0, keepdims=True)
        e = jnp.exp(scores - top)
        p = e / jnp.sum(e, axis=0, keepdims=True)
        pt32[h] = p
        ptb[h * ROWS : (h + 1) * ROWS, :] = p.astype(BF16)
    for t in range(HW // 128):
        att[:, t * 128 : t * 128 + 128] = tn(ptb[head_rows(t), :], vm[pair_rows(t), :]).astype(BF16)

    @pl.when(s == 0)
    def _():
        load_wo.wait()
        pl.semaphore_wait(barrier, (NM - 1) + (NZ - 1) + (NS - 1))

    def project(j):
        hout[j] = (hbuf[j].astype(F32) + nn(att[...], wo[:, j * CW : (j + 1) * CW])).astype(BF16)

    chip = m // 2
    core = lax.rem(m, 2)
    sibling = chip * 2 + 1 - core

    def gather_copy(which, slot, i, to):
        lanes = mp_lanes(slot)
        if which == 0:
            return remote(ngt.at[:, lanes], ngt.at[:, lanes], ns.at[i], nr.at[i], {"mp": to})
        return remote(atg.at[lanes, :], atg.at[lanes, :], as_.at[i], ar.at[i], {"mp": to})

    def across(d):
        return lax.rem(chip + d, NM // 2) * 2 + core

    def gather_start():
        for j in range(CHUNKS):
            wide = hbuf[j].astype(F32) * rs[...] * gain[:, j * CW : (j + 1) * CW]
            ngt[j * CW : (j + 1) * CW, mp_lanes(m)] = wide.astype(BF16).T
        atg[mp_lanes(m), :] = att[...]
        for w in range(2):
            for d in range(1, NM // 2):
                gather_copy(w, m, d, across(d)).start()
            gather_copy(w, m, 0, sibling).start()

    def gather_forward():
        for d in range(1, NM // 2):
            source = across(NM // 2 - d)
            for w in range(2):
                gather_copy(w, source, d, across(d)).wait_recv()
                gather_copy(w, source, NM // 2 - 1 + d, sibling).start()

    def gather_finish(w):
        gather_copy(w, sibling, 0, sibling).wait_recv()
        for d in range(1, NM // 2):
            source = lax.rem(chip + NM // 2 - d, NM // 2) * 2 + 1 - core
            gather_copy(w, source, NM // 2 - 1 + d, sibling).wait_recv()

    @pl.when(s < NS - 1)
    def _():
        for j in SENT:
            project(j)
            forward_send(j)

    gather_start()

    @pl.when(s == 0)
    def _():
        gather_forward()

    def turn_weights():
        for j in range(CHUNKS):
            wqt[:, j * CW : (j + 1) * CW] = wq[j * CW : (j + 1) * CW, :].T

    @pl.when(s < 2)
    def _():
        turn_weights()

    @pl.when(s == 1)
    def _():
        relay(0)
        gather_forward()

    @pl.when(s == 0)
    def _():
        relay(2)
        relay(3)

    for i, (t, h) in enumerate(PAIRS):
        qm[i * ROWS : (i + 1) * ROWS, :] = packed[:, t * 128 : t * 128 + 128] * mk[i]
    for h in range(HEADS):
        ptl[:, h * ROWS : (h + 1) * ROWS] = ptb[h * ROWS : (h + 1) * ROWS, :]

    for j in range(CHUNKS):

        @pl.when(s < NS - 1)
        def _():
            back_arrived(j)
            attend_back(j)

        if j != FAR:

            @pl.when(s == 0)
            def _():
                turn_g(j)

    datt[...] = dacc[...].astype(BF16)

    for i, (t, h) in enumerate(PAIRS):
        dam[i * ROWS : (i + 1) * ROWS, :] = datt[:, t * 128 : t * 128 + 128] * mk[i]
    for h in range(HEADS):
        t0, t1 = span(h)
        dprob = nt(gathered(vm, h), datt[:, t0:t1]).astype(BF16).astype(F32)
        p = pt32[h]
        dsc = p * (dprob - jnp.sum(p * dprob, axis=0, keepdims=True))
        dsc = (dsc * SCALE).astype(BF16)
        dsr[h * ROWS : (h + 1) * ROWS, :] = dsc
        dsl[:, h * ROWS : (h + 1) * ROWS] = dsc
    for t in range(HW // 128):
        c = t * 128
        dp[:, 2 * HW + c : 2 * HW + c + 128] = nn(ptl[:, head_rows(t)], dam[pair_rows(t), :]).astype(BF16)
    for t in range(HW // 128):
        c = t * 128
        dp[:, HW + c : HW + c + 128] = nn(dsl[:, head_rows(t)], qm[pair_rows(t), :]).astype(BF16)
        dp[:, c : c + 128] = tn(dsr[head_rows(t), :], km[pair_rows(t), :]).astype(BF16)

    @pl.when(s == 0)
    def _():
        columns_q()
        turn_g(FAR)
        columns_g()

    spread = rs[...]
    inner = jnp.zeros((ROWS, 128), F32)
    for t in range(3 * HW // 128):
        cols = slice(t * 128, t * 128 + 128)
        inner = inner + dp[:, cols].astype(F32) * pacc[:, cols]
    pull = jnp.sum(inner, axis=-1, keepdims=True) * (1.0 / VD) * (spread * spread * spread)
    for j in SENT:
        dn = nn(dp[:, 0 : 3 * HW], wqt[:, j * CW : (j + 1) * CW]).astype(BF16).astype(F32)
        up = dn * gain[:, j * CW : (j + 1) * CW]
        back = gbuf[j].astype(F32) + spread * up - hbuf[j].astype(F32) * pull
        gout[j] = back.astype(BF16)

        @pl.when(s > 0)
        def _():
            back_send(j)

        lifted[j] = dn

    def store_act(j):
        return pltpu.make_async_copy(hout.at[j], act.at[:, cols_of(j)], o_sem.at[j])

    def store_gin(j):
        return pltpu.make_async_copy(gout.at[j], gin.at[:, cols_of(j)], o_sem.at[CHUNKS + j])

    for j in range(CHUNKS):
        store_gin(j).start()

    @pl.when(s > 0)
    def _():
        columns_q()

    @pl.when((s > 0) & (s < NS - 1))
    def _():
        for j in range(CHUNKS):
            turn_g(j)
        columns_g()

    for j in range(CHUNKS):
        part = lifted[j] * (hbuf[j].astype(F32) * rs[...])
        dgain[0, :, j * CW : (j + 1) * CW] = jnp.sum(part, axis=0, keepdims=True)

    @pl.when(s == NS - 1)
    def _():
        for j in range(CHUNKS):
            project(j)

    @pl.when(s >= NS - 2)
    def _():
        gather_forward()

    for j in range(CHUNKS):
        store_act(j).start()

    def gain_mp(d):
        return remote(dgain.at[0], dgrecv.at[d], vs.at[d], vr.at[d], {"mp": lax.rem(m + d, NM)})

    def gain_dp(d):
        return remote(dgz.at[0], dgzrecv.at[d], us.at[d], ur.at[d], {"dp": lax.rem(z + d, NZ)})

    for d in range(1, NM):
        gain_mp(d).start()

    def chunk_q(half):
        def chunk(k):
            rows = pl.ds(pl.multiple_of(k * ZR, 16), ZR)
            return nn(ngt[rows, :], dpg[half])

        return chunk

    def chunk_o(k):
        return opad[k]

    steps = (NZ - 1, 1, NZ - 2, 2, NZ - 1, 1, NZ - 2, 2)
    owners = (NZ - 3, 3, 4, 4, NZ - 1, 1, NZ - 2, 2)

    def peer(i):
        return {"dp": lax.rem(z + steps[i], NZ)}

    def tree_q(half):
        def copy(i):
            n = half * 8 + i
            if i == 2 or i == 3:
                top = pl.ds(0, ZR // 2)
                return remote(sq.at[half, i, top], zq.at[half, i, top], qs.at[n], qr.at[n], peer(i))
            return remote(sq.at[half, i], zq.at[half, i], qs.at[n], qr.at[n], peer(i))

        return copy

    def tree_o(i):
        to = {"dp": lax.rem(z + NZ - 2 + 4 * core, NZ)} if i == 2 else peer(i)
        return remote(so.at[i], zo.at[i], os_.at[i], or_.at[i], to)

    def whose(i):
        return lax.rem(z + owners[i], NZ)

    def leaf_o(i):
        so[i] = chunk_o(whose(i)).astype(BF16)
        tree_o(i).start()

    def branch_o(i):
        ro[...] = chunk_o(whose(i))
        tree_o(i - 6).wait_recv()
        ro[...] += zo[i - 6].astype(F32)

        @pl.when(core == i - 6)
        def _():
            tree_o(2).wait_recv()
            ro[...] += zo[2].astype(F32)

        so[i] = ro[...].astype(BF16)
        tree_o(i).start()

    def leaf_q(half, i):
        copy, buf = tree_q(half), sq.at[half]
        if i == 2:
            value = chunk_q(half)(whose(2)).astype(BF16)
            buf[2, 0 : ZR // 2] = value[0 : ZR // 2]
            buf[3, 0 : ZR // 2] = value[ZR // 2 : ZR]
            copy(2).start()
            copy(3).start()
        else:
            buf[i] = chunk_q(half)(whose(i)).astype(BF16)
            copy(i).start()

    def sum_of(half):
        return rq.at[0:ZR, half * 128 : half * 128 + 128]

    def branch_q(half, i):
        hold, copy = sum_of(half), tree_q(half)
        hold[...] = chunk_q(half)(whose(i))
        copy(i - 6).wait_recv()
        hold[...] += zq[half, i - 6].astype(F32)
        copy(i - 4).wait_recv()
        top = 0 if i == 6 else ZR // 2
        hold[top : top + ZR // 2] += zq[half, i - 4, 0 : ZR // 2].astype(F32)
        sq[half, i] = hold[...].astype(BF16)
        copy(i).start()

    gather_finish(0)
    for half in range(2):
        for d in range(1, NM):
            column_copy(half, d).wait_recv()
        for i in (2, 0, 1):
            leaf_q(half, i)
    for i in (4, 5):
        leaf_q(0, i)
    for i in (6, 7):
        branch_q(0, i)

    gather_finish(1)
    for d in range(1, NM):
        g_copy(d).wait_recv()
    o32[0:ZR, :] = nn(gpg[...], atg[...])
    for k in range(NZ):
        opad[k, :, 0:HW] = o32[FR * k : FR * k + 16, :]
        for t in range(HW // 128):
            row, col = 4 * (t % 4), HW + t // 4 * 128
            opad[k, row : row + 4, col : col + 128] = o32[FR * k + 16 : FR * k + FR, t * 128 : t * 128 + 128]
    for i in (2, 0, 1):
        leaf_o(i)
    for i in (4, 5):
        leaf_q(1, i)
    for i in (6, 7):
        branch_q(1, i)
    for i in (4, 5):
        leaf_o(i)
    def piece(half, to, slot, d):
        i = half * NM + d
        return remote(fin.at[half, to], finrecv.at[half, slot], fs.at[i], fr.at[i], {"mp": to})

    def settle(half):
        hold = sum_of(half)
        for i in (4, 5, 6, 7):
            tree_q(half)(i).wait_recv()
            hold[...] += zq[half, i].astype(F32)
        cols = slice(half * 128, half * 128 + 128)
        for i in range(NM):
            fin[half, i] = rq[FR * i : FR * i + 32, cols].astype(BF16)
        for d in range(1, NM):
            piece(half, lax.rem(m + d, NM), m, d).start()
        finrecv[half, m] = fin[half, m]

    for half in range(2):
        sum_of(half)[...] = chunk_q(half)(z)
    settle(0)
    for i in (6, 7):
        branch_o(i)
    settle(1)

    sum_gain = dgain[0]
    for d in range(1, NM):
        gain_mp(d).wait_recv()
        sum_gain = sum_gain + dgrecv[d]
    dgz[0] = sum_gain
    for d in range(1, NZ):
        gain_dp(d).start()

    ro[...] = chunk_o(z)
    for i in (4, 5, 6, 7):
        tree_o(i).wait_recv()
        ro[...] += zo[i].astype(F32)
    oo[0:16, 0, :] = ro[:, 0:HW]
    for t in range(HW // 128):
        row, col = 4 * (t % 4), HW + t // 4 * 128
        oo[16:FR, 0, t * 128 : t * 128 + 128] = ro[row : row + 4, col : col + 128]
    store_o = pltpu.make_async_copy(oo, out_o, o_sem.at[2 * CHUNKS])
    store_o.start()

    sum_gain = dgz[0]
    for d in range(1, NZ):
        gain_dp(d).wait_recv()
        sum_gain = sum_gain + dgzrecv[d]
    dgz[1] = sum_gain
    store_gain = pltpu.make_async_copy(dgz.at[1], out_gain, o_sem.at[2 * CHUNKS + 1])
    store_gain.start()

    @pl.when(s < NS - 1)
    def _():
        for j in range(FAR):
            hop_forward(j).wait_send()
        far_forward(0).wait_send()
        near_forward().wait_send()

    @pl.when(s > 0)
    def _():
        for j in range(FAR):
            hop_back(j).wait_send()
        last_back().wait_send()
        near_back().wait_send()

    for where, slots in ((0, (2, 3)), (1, (0,)), (3, (0, 1))):

        @pl.when(s == where)
        def _():
            for slot in slots:
                pass_on(slot, 0).wait_send()

    for i in range(NM - 1):
        for w in range(2):
            gather_copy(w, m, i, sibling).wait_send()
    for d in range(1, NM):
        for half in range(2):
            column_copy(half, d).wait_send()
        g_copy(d).wait_send()
        gain_mp(d).wait_send()
    for d in range(1, NZ):
        gain_dp(d).wait_send()
    for i in range(8):
        tree_q(0)(i).wait_send()
        tree_q(1)(i).wait_send()
        if i != 3:
            tree_o(i).wait_send()
    for j in range(CHUNKS):
        store_act(j).wait()
        store_gin(j).wait()

    for half in range(2):
        for d in range(1, NM):
            source = lax.rem(m + NM - d, NM)
            piece(half, source, source, d).wait_recv()
        for i in range(NM):
            first = 256 * i + 128 * half
            if first < 3 * HW:
                oq[:, 0, first : first + 128] = finrecv[half, i].astype(F32)[0:FR]
    store_q = pltpu.make_async_copy(oq, out_q, o_sem.at[2 * CHUNKS + 2])
    store_q.start()
    for half in range(2):
        for d in range(1, NM):
            piece(half, lax.rem(m + d, NM), m, d).wait_send()
    store_o.wait()
    store_gain.wait()
    store_q.wait()


def finish(act, gin, out_q, out_o, gain, act2, gin2, out_q2, out_o2, gain2, a, b, c, d, e, f, sem):
    there = ((gain, e), (act, a), (gin, b), (out_q, c), (out_o, d))
    back = ((f, gain2), (a, act2), (b, gin2), (c, out_q2), (d, out_o2))
    reads = [pltpu.make_async_copy(x, y, sem.at[i]) for i, (x, y) in enumerate(there)]
    writes = [pltpu.make_async_copy(x, y, sem.at[5 + i]) for i, (x, y) in enumerate(back)]
    for r in reads:
        r.start()
    place = (lax.axis_index("dp") * NM + lax.axis_index("mp")) * FR
    for i, (r, w) in enumerate(zip(reads, writes)):
        r.wait()
        if i == 0:
            rows = jnp.broadcast_to(e[...], (8, VD))
            f[...] = pltpu.roll(rows, lax.rem(VD - place, VD), 1)[0:1, 0:FR]
        w.start()
    for w in writes:
        w.wait()


def on_device(patches, windows, gain, w_qkv, w_out, cotangent):
    hbm = pl.BlockSpec(memory_space=pl.ANY)
    dma = pltpu.SemaphoreType.DMA
    scratch = [
        pltpu.VMEM((VD, 3 * HW), BF16),
        pltpu.VMEM((HW, VD), BF16),
        pltpu.VMEM((1, ROWS), jnp.int32),
        pltpu.VMEM((1, VD), F32),
        pltpu.VMEM((CHUNKS, ROWS, CW), BF16),
        pltpu.VMEM((CHUNKS, ROWS, CW), BF16),
        pltpu.VMEM((CHUNKS, ROWS, CW), BF16),
        pltpu.VMEM((CHUNKS, ROWS, CW), BF16),
        pltpu.VMEM((ROWS, 3 * HW), F32),
        pltpu.VMEM((ROWS, HW), F32),
        pltpu.VMEM((ROWS, 3 * HW), BF16),
        pltpu.VMEM((HEADS, ROWS, ROWS), F32),
        pltpu.VMEM((HEADS * ROWS, ROWS), BF16),
        pltpu.VMEM((ROWS, HEADS * ROWS), BF16),
        pltpu.VMEM((ROWS, HW), BF16),
        pltpu.VMEM((len(PAIRS), ROWS, 128), BF16),
        pltpu.VMEM((len(PAIRS) * ROWS, 128), BF16),
        pltpu.VMEM((len(PAIRS) * ROWS, 128), BF16),
        pltpu.VMEM((len(PAIRS) * ROWS, 128), BF16),
        pltpu.VMEM((len(PAIRS) * ROWS, 128), BF16),
        pltpu.VMEM((HEADS * ROWS, ROWS), BF16),
        pltpu.VMEM((ROWS, HEADS * ROWS), BF16),
        pltpu.VMEM((ROWS, HW), BF16),
        pltpu.VMEM((ROWS, 2048), BF16),
        pltpu.VMEM((CHUNKS, ROWS, CW), F32),
        pltpu.VMEM((ROWS, 1), F32),
        pltpu.VMEM((3 * HW, VD), BF16),
        pltpu.VMEM((FR, 1, 3 * HW), F32),
        pltpu.VMEM((FR, 1, HW), F32),
        pltpu.VMEM((4, 2, HALF, CW), BF16),
        pltpu.VMEM((VD, NM * ROWS), BF16),
        pltpu.VMEM((NM * ROWS, HW), BF16),
        pltpu.VMEM((VD, ROWS), F32),
        pltpu.VMEM((VD, ROWS), F32),
        pltpu.VMEM((VD, ROWS), BF16),
        pltpu.VMEM((2, NM * ROWS, 128), BF16),
        pltpu.VMEM((ZR, NM * ROWS), BF16),
        pltpu.VMEM((ZR, HW), F32),
        pltpu.VMEM((NZ, 16, HW + 256), F32),
        pltpu.VMEM((1, 1, VD), F32),
        pltpu.VMEM((NM, 1, VD), F32),
        pltpu.VMEM((2, 1, VD), F32),
        pltpu.VMEM((NZ, 1, VD), F32),
        pltpu.VMEM((ZR + 32, 256), F32),
        pltpu.VMEM((16, HW + 256), F32),
        pltpu.VMEM((2, 8, ZR, 128), BF16),
        pltpu.VMEM((8, 16, HW + 256), BF16),
        pltpu.VMEM((2, 8, ZR, 128), BF16),
        pltpu.VMEM((8, 16, HW + 256), BF16),
        pltpu.VMEM((2, NM, 32, 128), BF16),
        pltpu.VMEM((2, NM, 32, 128), BF16),
        dma((8,)), dma((CHUNKS,)), dma((2 * CHUNKS + 3,)),
        dma((8,)), dma((8,)), dma((8,)), dma((8,)),
    ] + [dma((16,)) for _ in range(21)]
    shapes = (
        jax.ShapeDtypeStruct((ROWS, VD), BF16),
        jax.ShapeDtypeStruct((ROWS, VD), BF16),
        jax.ShapeDtypeStruct((FR, 1, 3 * HW), F32),
        jax.ShapeDtypeStruct((FR, 1, HW), F32),
        jax.ShapeDtypeStruct((1, VD), F32),
    )
    results = pl.pallas_call(
        kernel,
        out_shape=shapes,
        in_specs=[hbm] * 6,
        out_specs=(hbm,) * 5,
        scratch_shapes=scratch,
        compiler_params=pltpu.CompilerParams(
            collective_id=0, has_side_effects=True, vmem_limit_bytes=60 * 1024 * 1024
        ),
    )(patches[0], cotangent[0], windows, gain, w_qkv[0], w_out[0])
    act, gin, out_q, out_o, own_gain = pl.pallas_call(
        finish,
        out_shape=shapes[:4] + (jax.ShapeDtypeStruct((1, FR), F32),),
        in_specs=[hbm] * 5,
        out_specs=(hbm,) * 5,
        scratch_shapes=[pltpu.VMEM(x.shape, x.dtype) for x in shapes] + [pltpu.VMEM((1, FR), F32), dma((10,))],
        compiler_params=pltpu.CompilerParams(vmem_limit_bytes=60 * 1024 * 1024),
    )(*results)
    return (
        act[None, None],
        gin[None, None],
        out_q.transpose(1, 0, 2),
        out_o.transpose(1, 2, 0),
        own_gain,
    )


def solution(mesh):
    in_specs = (
        P(None, ("dp", "mp"), None),
        P(None, ("dp", "mp")),
        P("section", None),
        P("section", None, None),
        P("section", None, None),
        P(None, ("dp", "mp"), None),
    )
    out_specs = (
        P("section", None, ("dp", "mp"), None),
        P("section", None, ("dp", "mp"), None),
        P("section", ("dp", "mp"), None),
        P("section", None, ("dp", "mp")),
        P("section", ("dp", "mp")),
    )
    return jax.shard_map(
        on_device, mesh=mesh, in_specs=in_specs, out_specs=out_specs, check_vma=False
    )
```

```python
import jax
import jax.numpy as jnp
from jax import lax
from jax.experimental import pallas as pl
from jax.experimental.pallas import tpu as pltpu
from jax.sharding import PartitionSpec as P

HEAD = 80
HEADS = 8
ROWS = 128
VD = 1280
HW = 640
NM = 8
NZ = 8
NS = 4
CHUNKS = 5
CW = VD // CHUNKS
FAR = CHUNKS - 1
SENT = (FAR,) + tuple(range(FAR))
HALF = ROWS // 2
ZR = VD // NZ
FR = ZR // NM
SCALE = HEAD**-0.5
MESH = pl.DeviceIdType.MESH
F32 = jnp.float32
BF16 = jnp.bfloat16


def nt(a, b):
    return lax.dot_general(a, b, (((1,), (1,)), ((), ())), preferred_element_type=F32)


def nn(a, b):
    return lax.dot_general(a, b, (((1,), (0,)), ((), ())), preferred_element_type=F32)


def tn(a, b):
    return lax.dot_general(a, b, (((0,), (0,)), ((), ())), preferred_element_type=F32)


def tiles_of(h):
    return range(HEAD * h // 128, -(-(HEAD * h + HEAD) // 128))


def heads_of(t):
    return [h for h in range(HEADS) if t in tiles_of(h)]


PAIRS = [(t, h) for t in range(HW // 128) for h in heads_of(t)]


def pair_rows(t):
    first = PAIRS.index((t, heads_of(t)[0]))
    return slice(first * ROWS, (first + len(heads_of(t))) * ROWS)


def head_rows(t):
    heads = heads_of(t)
    return slice(heads[0] * ROWS, (heads[-1] + 1) * ROWS)


def gathered(stack, h):
    parts = []
    for t in tiles_of(h):
        i = PAIRS.index((t, h))
        parts.append(stack[i * ROWS : (i + 1) * ROWS, :])
    return parts[0] if len(parts) == 1 else jnp.concatenate(parts, axis=1)


def span(h):
    tiles = tiles_of(h)
    return tiles[0] * 128, tiles[-1] * 128 + 128


def kernel(
    patches, cot, win_hbm, gain_hbm, wq_hbm, wo_hbm,
    act, gin, out_q, out_o, out_gain,
    wq, wo, win, gain, hbuf, gbuf, hout, gout, pacc, dacc, packed, pt32, ptb, ptl, att, mk, qm, km, vm, dam, dsr, dsl,
    datt, dp, lifted, rs, wqt, oq, oo, rbuf,
    ngt, atg, gt32, gp32, gperm, dpg, gpg, o32, opad, dgain, dgrecv, dgz, dgzrecv,
    rq, ro, sq, so, zq, zo, fin, finrecv,
    w_sem, in_sem, o_sem, hs, hr, gs, gr, ns, nr, as_, ar, ds, dr, ps, pr, vs, vr, us, ur, qs, qr, os_, or_, fs, fr, ls, lr, ts,
):
    s = lax.axis_index("section")
    m = lax.axis_index("mp")
    z = lax.axis_index("dp")

    def cols_of(j):
        return pl.ds(j * CW, CW)

    def load_patches(j):
        return pltpu.make_async_copy(patches.at[:, cols_of(j)], hbuf.at[j], in_sem.at[j])

    def load_cot(j):
        return pltpu.make_async_copy(cot.at[:, cols_of(j)], gbuf.at[j], in_sem.at[j])

    def load_wq(j):
        return pltpu.make_async_copy(wq_hbm.at[cols_of(j)], wq.at[cols_of(j)], w_sem.at[j])

    load_wo = pltpu.make_async_copy(wo_hbm, wo, w_sem.at[5])
    load_gain = pltpu.make_async_copy(gain_hbm, gain, w_sem.at[6])
    load_win = pltpu.make_async_copy(win_hbm, win, w_sem.at[7])

    load_gain.start()

    @pl.when(s == 0)
    def _():
        for j in range(CHUNKS):
            load_patches(j).start()

    for j in range(CHUNKS):
        load_wq(j).start()
    load_win.start()
    load_wo.start()

    @pl.when(s == NS - 1)
    def _():
        for j in range(CHUNKS):
            load_cot(j).start()

    barrier = pltpu.get_barrier_semaphore()
    for d in range(1, NM):
        pl.semaphore_signal(barrier, inc=1, device_id={"mp": lax.rem(m + d, NM)}, device_id_type=MESH)
    for d in range(1, NZ):
        pl.semaphore_signal(barrier, inc=1, device_id={"dp": lax.rem(z + d, NZ)}, device_id_type=MESH)
    for d in range(1, NS):
        pl.semaphore_signal(barrier, inc=1, device_id={"section": lax.rem(s + d, NS)}, device_id_type=MESH)

    dp[:, 3 * HW : 2048] = jnp.zeros((ROWS, 2048 - 3 * HW), BF16)
    rq[ZR : ZR + 32, :] = jnp.zeros((32, 256), F32)
    for i, (t, h) in enumerate(PAIRS):
        cols = lax.broadcasted_iota(jnp.int32, (ROWS, 128), 1) + t * 128
        inside = (cols >= HEAD * h) & (cols < HEAD * h + HEAD)
        mk[i] = jnp.where(inside, 1.0, 0.0).astype(BF16)
    opad[:, :, HW : HW + 256] = jnp.zeros((NZ, 16, 256), F32)

    def remote(src, dst, ssem, rsem, where):
        return pltpu.make_async_remote_copy(
            src_ref=src, dst_ref=dst, send_sem=ssem, recv_sem=rsem, device_id=where, device_id_type=MESH
        )

    def hop_forward(j):
        return remote(hout.at[j], hbuf.at[j], hs.at[j], hr.at[j], {"section": lax.rem(s + 1, NS)})

    def hop_back(j):
        return remote(gout.at[j], gbuf.at[j], gs.at[j], gr.at[j], {"section": lax.rem(s + NS - 1, NS)})

    def half_rows(i):
        return pl.ds(i * HALF, HALF)

    def far_forward(i):
        slot = lax.rem(s, 2)
        to = {"section": lax.rem(s + 3 - lax.rem(s, 2), NS)}
        return remote(hout.at[FAR, half_rows(i)], rbuf.at[slot, i], ls.at[i], lr.at[slot * 2 + i], to)

    def far_back(i):
        slot = 3 - lax.rem(s, 2)
        to = {"section": lax.rem(s + 2 - lax.rem(s, 2), NS)}
        return remote(gout.at[FAR, half_rows(i)], rbuf.at[slot, i], ls.at[2 + i], lr.at[slot * 2 + i], to)

    def near_forward():
        half = half_rows(1)
        to = {"section": lax.rem(s + 1, NS)}
        return remote(hout.at[FAR, half], hbuf.at[FAR, half], hs.at[FAR], hr.at[FAR + 1], to)

    def near_back():
        half = half_rows(1)
        to = {"section": lax.rem(s + NS - 1, NS)}
        return remote(gout.at[FAR, half], gbuf.at[FAR, half], gs.at[FAR], gr.at[FAR + 1], to)

    def last_back():
        half = half_rows(0)
        return remote(gout.at[FAR, half], gbuf.at[FAR, half], ls.at[2], gr.at[FAR], {"section": lax.rem(s + NS - 1, NS)})

    def pass_on(slot, i):
        to = {"section": lax.rem(s + (2, 3, 2, 1)[slot], NS)}
        if slot < 2:
            return remote(rbuf.at[slot, i], hbuf.at[FAR, half_rows(i)], ts.at[slot * 2 + i], hr.at[FAR + i], to)
        return remote(rbuf.at[slot, i], gbuf.at[FAR, half_rows(i)], ts.at[slot * 2 + i], gr.at[FAR + i], to)

    def relay(slot):
        for i in range(1):
            remote(rbuf.at[slot, i], rbuf.at[slot, i], ts.at[slot * 2 + i], lr.at[slot * 2 + i], {"section": lax.rem(s + 1, NS)}).wait_recv()
            pass_on(slot, i).start()

    def forward_send(j):
        if j == FAR:
            far_forward(0).start()
        else:
            hop_forward(j).start()
            if j == FAR - 1:
                near_forward().start()

    def forward_arrived(j):
        if j == FAR:
            pass_on(0, 0).wait_recv()
            near_forward().wait_recv()
        else:
            hop_forward(j).wait_recv()

    def back_send(j):
        if j == FAR:

            @pl.when(s > 1)
            def _():
                far_back(0).start()

            @pl.when(s == 1)
            def _():
                last_back().start()
        else:
            hop_back(j).start()
            if j == FAR - 1:
                near_back().start()

    def back_arrived(j):
        if j == FAR:
            pass_on(2, 0).wait_recv()
            near_back().wait_recv()
        else:
            hop_back(j).wait_recv()

    def mp_lanes(i):
        return pl.ds(pl.multiple_of(i * ROWS, ROWS), ROWS)

    def fold(x):
        return x[:, 0:128] + x[:, 128:256]

    def column_copy(half, d):
        to = lax.rem(m + d, NM)
        cols = pl.ds(pl.multiple_of(to * 256 + half * 128, 128), 128)
        i = half * NM + d
        return remote(dp.at[:, cols], dpg.at[half, mp_lanes(m), :], ds.at[i], dr.at[i], {"mp": to})

    def g_copy(d):
        to = lax.rem(m + d, NM)
        rows = pl.ds(pl.multiple_of(to * ZR, 16), ZR)
        return remote(gperm.at[rows], gpg.at[:, mp_lanes(m)], ps.at[d], pr.at[d], {"mp": to})

    def columns_q():
        for half in range(2):
            for d in range(1, NM):
                column_copy(half, d).start()
        for half in range(2):
            cols = pl.ds(pl.multiple_of(m * 256 + half * 128, 128), 128)
            dpg[half, mp_lanes(m), :] = dp[:, cols]

    def turn_g(j):
        gt32[j * CW : (j + 1) * CW, :] = gbuf[j].astype(F32).T
        for first in range(0, VD, FR):
            if (first + FR - 1) // CW == j:
                i, k = first // FR % NM, first // FR // NM
                gp32[i * ZR + k * FR : i * ZR + k * FR + FR, :] = gt32[first : first + FR, :]

    def columns_g():
        gperm[...] = gp32[...].astype(BF16)
        for d in range(1, NM):
            g_copy(d).start()
        gpg[:, mp_lanes(m)] = gperm[pl.ds(pl.multiple_of(m * ZR, 16), ZR), :]

    def attend_back(j):
        part = nt(gbuf[j], wo[:, j * CW : (j + 1) * CW])
        if j == 0:
            dacc[...] = part
        else:
            dacc[...] += part

    @pl.when(s > 0)
    def _():
        load_wo.wait()
        pl.semaphore_wait(barrier, (NM - 1) + (NZ - 1) + (NS - 1))

    @pl.when(s == NS - 1)
    def _():
        for j in range(CHUNKS):
            load_cot(j).wait()
            attend_back(j)
            turn_g(j)
        columns_g()
        relay(0)
        relay(1)

    load_gain.wait()
    @pl.when(s >= 2)
    def _():
        for j in range(CHUNKS):
            load_wq(j).wait()
            wqt[:, j * CW : (j + 1) * CW] = wq[j * CW : (j + 1) * CW, :].T

    squares = jnp.zeros((ROWS, 128), F32)
    for j in range(CHUNKS):

        @pl.when(s == 0)
        def _():
            load_patches(j).wait()

        @pl.when(s > 0)
        def _():
            forward_arrived(j)

        @pl.when(s < 2)
        def _():
            load_wq(j).wait()

        wide = hbuf[j].astype(F32)
        squares = squares + fold(wide * wide)
        scaled = (wide * gain[:, j * CW : (j + 1) * CW]).astype(BF16)
        for i in range(3):
            part = nn(scaled, wq[j * CW : (j + 1) * CW, i * HW : (i + 1) * HW])
            if j == 0:
                pacc[:, i * HW : (i + 1) * HW] = part
            else:
                pacc[:, i * HW : (i + 1) * HW] += part
    spread = lax.rsqrt(jnp.sum(squares, axis=-1, keepdims=True) * (1.0 / VD) + 1e-6)
    rs[...] = spread
    packed[...] = (pacc[...] * spread).astype(BF16)
    load_win.wait()
    ids = jnp.broadcast_to(win[...].astype(F32), (ROWS, ROWS))
    same = ids.T == ids

    for i, (t, h) in enumerate(PAIRS):
        rows = slice(i * ROWS, (i + 1) * ROWS)
        km[rows, :] = packed[:, HW + t * 128 : HW + t * 128 + 128] * mk[i]
        vm[rows, :] = packed[:, 2 * HW + t * 128 : 2 * HW + t * 128 + 128] * mk[i]
    for h in range(HEADS):
        t0, t1 = span(h)
        scores = nt(gathered(km, h), packed[:, t0:t1]) * SCALE
        scores = jnp.where(same, scores, -1e30)
        top = jnp.max(scores, axis=0, keepdims=True)
        e = jnp.exp(scores - top)
        p = e / jnp.sum(e, axis=0, keepdims=True)
        pt32[h] = p
        ptb[h * ROWS : (h + 1) * ROWS, :] = p.astype(BF16)
    for t in range(HW // 128):
        att[:, t * 128 : t * 128 + 128] = tn(ptb[head_rows(t), :], vm[pair_rows(t), :]).astype(BF16)

    @pl.when(s == 0)
    def _():
        load_wo.wait()
        pl.semaphore_wait(barrier, (NM - 1) + (NZ - 1) + (NS - 1))

    def project(j):
        hout[j] = (hbuf[j].astype(F32) + nn(att[...], wo[:, j * CW : (j + 1) * CW])).astype(BF16)

    chip = m // 2
    core = lax.rem(m, 2)
    sibling = chip * 2 + 1 - core

    def gather_copy(which, slot, i, to):
        lanes = mp_lanes(slot)
        if which == 0:
            return remote(ngt.at[:, lanes], ngt.at[:, lanes], ns.at[i], nr.at[i], {"mp": to})
        return remote(atg.at[lanes, :], atg.at[lanes, :], as_.at[i], ar.at[i], {"mp": to})

    def across(d):
        return lax.rem(chip + d, NM // 2) * 2 + core

    def gather_start():
        for j in range(CHUNKS):
            wide = hbuf[j].astype(F32) * rs[...] * gain[:, j * CW : (j + 1) * CW]
            ngt[j * CW : (j + 1) * CW, mp_lanes(m)] = wide.astype(BF16).T
        atg[mp_lanes(m), :] = att[...]
        for w in range(2):
            for d in range(1, NM // 2):
                gather_copy(w, m, d, across(d)).start()
            gather_copy(w, m, 0, sibling).start()

    def gather_forward():
        for d in range(1, NM // 2):
            source = across(NM // 2 - d)
            for w in range(2):
                gather_copy(w, source, d, across(d)).wait_recv()
                gather_copy(w, source, NM // 2 - 1 + d, sibling).start()

    def gather_finish(w):
        gather_copy(w, sibling, 0, sibling).wait_recv()
        for d in range(1, NM // 2):
            source = lax.rem(chip + NM // 2 - d, NM // 2) * 2 + 1 - core
            gather_copy(w, source, NM // 2 - 1 + d, sibling).wait_recv()

    @pl.when(s < NS - 1)
    def _():
        for j in SENT:
            project(j)
            forward_send(j)

    gather_start()

    @pl.when(s == 0)
    def _():
        gather_forward()

    def turn_weights():
        for j in range(CHUNKS):
            wqt[:, j * CW : (j + 1) * CW] = wq[j * CW : (j + 1) * CW, :].T

    @pl.when(s < 2)
    def _():
        turn_weights()

    @pl.when(s == 1)
    def _():
        relay(0)
        gather_forward()

    @pl.when(s == 0)
    def _():
        relay(2)
        relay(3)

    for i, (t, h) in enumerate(PAIRS):
        qm[i * ROWS : (i + 1) * ROWS, :] = packed[:, t * 128 : t * 128 + 128] * mk[i]
    for h in range(HEADS):
        ptl[:, h * ROWS : (h + 1) * ROWS] = ptb[h * ROWS : (h + 1) * ROWS, :]

    for j in range(CHUNKS):

        @pl.when(s < NS - 1)
        def _():
            back_arrived(j)
            attend_back(j)

        if j != FAR:

            @pl.when(s == 0)
            def _():
                turn_g(j)

    datt[...] = dacc[...].astype(BF16)

    for i, (t, h) in enumerate(PAIRS):
        dam[i * ROWS : (i + 1) * ROWS, :] = datt[:, t * 128 : t * 128 + 128] * mk[i]
    for h in range(HEADS):
        t0, t1 = span(h)
        dprob = nt(gathered(vm, h), datt[:, t0:t1]).astype(BF16).astype(F32)
        p = pt32[h]
        dsc = p * (dprob - jnp.sum(p * dprob, axis=0, keepdims=True))
        dsc = (dsc * SCALE).astype(BF16)
        dsr[h * ROWS : (h + 1) * ROWS, :] = dsc
        dsl[:, h * ROWS : (h + 1) * ROWS] = dsc
    for t in range(HW // 128):
        c = t * 128
        dp[:, 2 * HW + c : 2 * HW + c + 128] = nn(ptl[:, head_rows(t)], dam[pair_rows(t), :]).astype(BF16)
    for t in range(HW // 128):
        c = t * 128
        dp[:, HW + c : HW + c + 128] = nn(dsl[:, head_rows(t)], qm[pair_rows(t), :]).astype(BF16)
        dp[:, c : c + 128] = tn(dsr[head_rows(t), :], km[pair_rows(t), :]).astype(BF16)

    @pl.when(s == 0)
    def _():
        columns_q()
        turn_g(FAR)
        columns_g()

    spread = rs[...]
    inner = jnp.zeros((ROWS, 128), F32)
    for t in range(3 * HW // 128):
        cols = slice(t * 128, t * 128 + 128)
        inner = inner + dp[:, cols].astype(F32) * pacc[:, cols]
    pull = jnp.sum(inner, axis=-1, keepdims=True) * (1.0 / VD) * (spread * spread * spread)
    for j in SENT:
        dn = nn(dp[:, 0 : 3 * HW], wqt[:, j * CW : (j + 1) * CW]).astype(BF16).astype(F32)
        up = dn * gain[:, j * CW : (j + 1) * CW]
        back = gbuf[j].astype(F32) + spread * up - hbuf[j].astype(F32) * pull
        gout[j] = back.astype(BF16)

        @pl.when(s > 0)
        def _():
            back_send(j)

        lifted[j] = dn

    def store_act(j):
        return pltpu.make_async_copy(hout.at[j], act.at[:, cols_of(j)], o_sem.at[j])

    def store_gin(j):
        return pltpu.make_async_copy(gout.at[j], gin.at[:, cols_of(j)], o_sem.at[CHUNKS + j])

    for j in range(CHUNKS):
        store_gin(j).start()

    @pl.when(s > 0)
    def _():
        columns_q()

    @pl.when((s > 0) & (s < NS - 1))
    def _():
        for j in range(CHUNKS):
            turn_g(j)
        columns_g()

    for j in range(CHUNKS):
        part = lifted[j] * (hbuf[j].astype(F32) * rs[...])
        dgain[0, :, j * CW : (j + 1) * CW] = jnp.sum(part, axis=0, keepdims=True)

    @pl.when(s == NS - 1)
    def _():
        for j in range(CHUNKS):
            project(j)

    @pl.when(s >= NS - 2)
    def _():
        gather_forward()

    for j in range(CHUNKS):
        store_act(j).start()

    def gain_mp(d):
        return remote(dgain.at[0], dgrecv.at[d], vs.at[d], vr.at[d], {"mp": lax.rem(m + d, NM)})

    def gain_dp(d):
        return remote(dgz.at[0], dgzrecv.at[d], us.at[d], ur.at[d], {"dp": lax.rem(z + d, NZ)})

    for d in range(1, NM):
        gain_mp(d).start()

    def chunk_q(half):
        def chunk(k):
            rows = pl.ds(pl.multiple_of(k * ZR, 16), ZR)
            return nn(ngt[rows, :], dpg[half])

        return chunk

    def chunk_o(k):
        return opad[k]

    steps = (NZ - 1, 1, NZ - 2, 2, NZ - 1, 1, NZ - 2, 2)
    owners = (NZ - 3, 3, 4, 4, NZ - 1, 1, NZ - 2, 2)

    def peer(i):
        return {"dp": lax.rem(z + steps[i], NZ)}

    def tree_q(half):
        def copy(i):
            n = half * 8 + i
            if i == 2 or i == 3:
                top = pl.ds(0, ZR // 2)
                return remote(sq.at[half, i, top], zq.at[half, i, top], qs.at[n], qr.at[n], peer(i))
            return remote(sq.at[half, i], zq.at[half, i], qs.at[n], qr.at[n], peer(i))

        return copy

    def tree_o(i):
        to = {"dp": lax.rem(z + NZ - 2 + 4 * core, NZ)} if i == 2 else peer(i)
        return remote(so.at[i], zo.at[i], os_.at[i], or_.at[i], to)

    def whose(i):
        return lax.rem(z + owners[i], NZ)

    def leaf_o(i):
        so[i] = chunk_o(whose(i)).astype(BF16)
        tree_o(i).start()

    def branch_o(i):
        ro[...] = chunk_o(whose(i))
        tree_o(i - 6).wait_recv()
        ro[...] += zo[i - 6].astype(F32)

        @pl.when(core == i - 6)
        def _():
            tree_o(2).wait_recv()
            ro[...] += zo[2].astype(F32)

        so[i] = ro[...].astype(BF16)
        tree_o(i).start()

    def leaf_q(half, i):
        copy, buf = tree_q(half), sq.at[half]
        if i == 2:
            value = chunk_q(half)(whose(2)).astype(BF16)
            buf[2, 0 : ZR // 2] = value[0 : ZR // 2]
            buf[3, 0 : ZR // 2] = value[ZR // 2 : ZR]
            copy(2).start()
            copy(3).start()
        else:
            buf[i] = chunk_q(half)(whose(i)).astype(BF16)
            copy(i).start()

    def sum_of(half):
        return rq.at[0:ZR, half * 128 : half * 128 + 128]

    def branch_q(half, i):
        hold, copy = sum_of(half), tree_q(half)
        hold[...] = chunk_q(half)(whose(i))
        copy(i - 6).wait_recv()
        hold[...] += zq[half, i - 6].astype(F32)
        copy(i - 4).wait_recv()
        top = 0 if i == 6 else ZR // 2
        hold[top : top + ZR // 2] += zq[half, i - 4, 0 : ZR // 2].astype(F32)
        sq[half, i] = hold[...].astype(BF16)
        copy(i).start()

    gather_finish(0)
    for half in range(2):
        for d in range(1, NM):
            column_copy(half, d).wait_recv()
        for i in (2, 0, 1):
            leaf_q(half, i)
    for i in (4, 5):
        leaf_q(0, i)
    for i in (6, 7):
        branch_q(0, i)
    for i in (4, 5):
        leaf_q(1, i)

    gather_finish(1)
    for d in range(1, NM):
        g_copy(d).wait_recv()
    o32[0:ZR, :] = nn(gpg[...], atg[...])
    for k in range(NZ):
        opad[k, :, 0:HW] = o32[FR * k : FR * k + 16, :]
        for t in range(HW // 128):
            row, col = 4 * (t % 4), HW + t // 4 * 128
            opad[k, row : row + 4, col : col + 128] = o32[FR * k + 16 : FR * k + FR, t * 128 : t * 128 + 128]
    for i in (2, 0, 1):
        leaf_o(i)
    for i in (6, 7):
        branch_q(1, i)
    for i in (4, 5):
        leaf_o(i)
    for i in (6, 7):
        branch_o(i)

    def piece(half, to, slot, d):
        i = half * NM + d
        return remote(fin.at[half, to], finrecv.at[half, slot], fs.at[i], fr.at[i], {"mp": to})

    for half in range(2):
        hold = sum_of(half)
        hold[...] = chunk_q(half)(z)
        for i in (4, 5, 6, 7):
            tree_q(half)(i).wait_recv()
            hold[...] += zq[half, i].astype(F32)
        cols = slice(half * 128, half * 128 + 128)
        for i in range(NM):
            fin[half, i] = rq[FR * i : FR * i + 32, cols].astype(BF16)
        for d in range(1, NM):
            piece(half, lax.rem(m + d, NM), m, d).start()
        finrecv[half, m] = fin[half, m]

    sum_gain = dgain[0]
    for d in range(1, NM):
        gain_mp(d).wait_recv()
        sum_gain = sum_gain + dgrecv[d]
    dgz[0] = sum_gain
    for d in range(1, NZ):
        gain_dp(d).start()

    ro[...] = chunk_o(z)
    for i in (4, 5, 6, 7):
        tree_o(i).wait_recv()
        ro[...] += zo[i].astype(F32)
    oo[0:16, 0, :] = ro[:, 0:HW]
    for t in range(HW // 128):
        row, col = 4 * (t % 4), HW + t // 4 * 128
        oo[16:FR, 0, t * 128 : t * 128 + 128] = ro[row : row + 4, col : col + 128]
    store_o = pltpu.make_async_copy(oo, out_o, o_sem.at[2 * CHUNKS])
    store_o.start()

    sum_gain = dgz[0]
    for d in range(1, NZ):
        gain_dp(d).wait_recv()
        sum_gain = sum_gain + dgzrecv[d]
    dgz[1] = sum_gain
    store_gain = pltpu.make_async_copy(dgz.at[1], out_gain, o_sem.at[2 * CHUNKS + 1])
    store_gain.start()

    @pl.when(s < NS - 1)
    def _():
        for j in range(FAR):
            hop_forward(j).wait_send()
        far_forward(0).wait_send()
        near_forward().wait_send()

    @pl.when(s > 0)
    def _():
        for j in range(FAR):
            hop_back(j).wait_send()
        last_back().wait_send()
        near_back().wait_send()

    for where, slots in ((0, (2, 3)), (1, (0,)), (3, (0, 1))):

        @pl.when(s == where)
        def _():
            for slot in slots:
                pass_on(slot, 0).wait_send()

    for i in range(NM - 1):
        for w in range(2):
            gather_copy(w, m, i, sibling).wait_send()
    for d in range(1, NM):
        for half in range(2):
            column_copy(half, d).wait_send()
        g_copy(d).wait_send()
        gain_mp(d).wait_send()
    for d in range(1, NZ):
        gain_dp(d).wait_send()
    for i in range(8):
        tree_q(0)(i).wait_send()
        tree_q(1)(i).wait_send()
        if i != 3:
            tree_o(i).wait_send()
    for j in range(CHUNKS):
        store_act(j).wait()
        store_gin(j).wait()

    for half in range(2):
        for d in range(1, NM):
            source = lax.rem(m + NM - d, NM)
            piece(half, source, source, d).wait_recv()
        for i in range(NM):
            first = 256 * i + 128 * half
            if first < 3 * HW:
                oq[:, 0, first : first + 128] = finrecv[half, i].astype(F32)[0:FR]
    store_q = pltpu.make_async_copy(oq, out_q, o_sem.at[2 * CHUNKS + 2])
    store_q.start()
    for half in range(2):
        for d in range(1, NM):
            piece(half, lax.rem(m + d, NM), m, d).wait_send()
    store_o.wait()
    store_gain.wait()
    store_q.wait()


def finish(act, gin, out_q, out_o, gain, act2, gin2, out_q2, out_o2, gain2, a, b, c, d, e, f, sem):
    there = ((gain, e), (act, a), (gin, b), (out_q, c), (out_o, d))
    back = ((f, gain2), (a, act2), (b, gin2), (c, out_q2), (d, out_o2))
    reads = [pltpu.make_async_copy(x, y, sem.at[i]) for i, (x, y) in enumerate(there)]
    writes = [pltpu.make_async_copy(x, y, sem.at[5 + i]) for i, (x, y) in enumerate(back)]
    for r in reads:
        r.start()
    place = (lax.axis_index("dp") * NM + lax.axis_index("mp")) * FR
    for i, (r, w) in enumerate(zip(reads, writes)):
        r.wait()
        if i == 0:
            rows = jnp.broadcast_to(e[...], (8, VD))
            f[...] = pltpu.roll(rows, lax.rem(VD - place, VD), 1)[0:1, 0:FR]
        w.start()
    for w in writes:
        w.wait()


def on_device(patches, windows, gain, w_qkv, w_out, cotangent):
    hbm = pl.BlockSpec(memory_space=pl.ANY)
    dma = pltpu.SemaphoreType.DMA
    scratch = [
        pltpu.VMEM((VD, 3 * HW), BF16),
        pltpu.VMEM((HW, VD), BF16),
        pltpu.VMEM((1, ROWS), jnp.int32),
        pltpu.VMEM((1, VD), F32),
        pltpu.VMEM((CHUNKS, ROWS, CW), BF16),
        pltpu.VMEM((CHUNKS, ROWS, CW), BF16),
        pltpu.VMEM((CHUNKS, ROWS, CW), BF16),
        pltpu.VMEM((CHUNKS, ROWS, CW), BF16),
        pltpu.VMEM((ROWS, 3 * HW), F32),
        pltpu.VMEM((ROWS, HW), F32),
        pltpu.VMEM((ROWS, 3 * HW), BF16),
        pltpu.VMEM((HEADS, ROWS, ROWS), F32),
        pltpu.VMEM((HEADS * ROWS, ROWS), BF16),
        pltpu.VMEM((ROWS, HEADS * ROWS), BF16),
        pltpu.VMEM((ROWS, HW), BF16),
        pltpu.VMEM((len(PAIRS), ROWS, 128), BF16),
        pltpu.VMEM((len(PAIRS) * ROWS, 128), BF16),
        pltpu.VMEM((len(PAIRS) * ROWS, 128), BF16),
        pltpu.VMEM((len(PAIRS) * ROWS, 128), BF16),
        pltpu.VMEM((len(PAIRS) * ROWS, 128), BF16),
        pltpu.VMEM((HEADS * ROWS, ROWS), BF16),
        pltpu.VMEM((ROWS, HEADS * ROWS), BF16),
        pltpu.VMEM((ROWS, HW), BF16),
        pltpu.VMEM((ROWS, 2048), BF16),
        pltpu.VMEM((CHUNKS, ROWS, CW), F32),
        pltpu.VMEM((ROWS, 1), F32),
        pltpu.VMEM((3 * HW, VD), BF16),
        pltpu.VMEM((FR, 1, 3 * HW), F32),
        pltpu.VMEM((FR, 1, HW), F32),
        pltpu.VMEM((4, 2, HALF, CW), BF16),
        pltpu.VMEM((VD, NM * ROWS), BF16),
        pltpu.VMEM((NM * ROWS, HW), BF16),
        pltpu.VMEM((VD, ROWS), F32),
        pltpu.VMEM((VD, ROWS), F32),
        pltpu.VMEM((VD, ROWS), BF16),
        pltpu.VMEM((2, NM * ROWS, 128), BF16),
        pltpu.VMEM((ZR, NM * ROWS), BF16),
        pltpu.VMEM((ZR, HW), F32),
        pltpu.VMEM((NZ, 16, HW + 256), F32),
        pltpu.VMEM((1, 1, VD), F32),
        pltpu.VMEM((NM, 1, VD), F32),
        pltpu.VMEM((2, 1, VD), F32),
        pltpu.VMEM((NZ, 1, VD), F32),
        pltpu.VMEM((ZR + 32, 256), F32),
        pltpu.VMEM((16, HW + 256), F32),
        pltpu.VMEM((2, 8, ZR, 128), BF16),
        pltpu.VMEM((8, 16, HW + 256), BF16),
        pltpu.VMEM((2, 8, ZR, 128), BF16),
        pltpu.VMEM((8, 16, HW + 256), BF16),
        pltpu.VMEM((2, NM, 32, 128), BF16),
        pltpu.VMEM((2, NM, 32, 128), BF16),
        dma((8,)), dma((CHUNKS,)), dma((2 * CHUNKS + 3,)),
        dma((8,)), dma((8,)), dma((8,)), dma((8,)),
    ] + [dma((16,)) for _ in range(21)]
    shapes = (
        jax.ShapeDtypeStruct((ROWS, VD), BF16),
        jax.ShapeDtypeStruct((ROWS, VD), BF16),
        jax.ShapeDtypeStruct((FR, 1, 3 * HW), F32),
        jax.ShapeDtypeStruct((FR, 1, HW), F32),
        jax.ShapeDtypeStruct((1, VD), F32),
    )
    results = pl.pallas_call(
        kernel,
        out_shape=shapes,
        in_specs=[hbm] * 6,
        out_specs=(hbm,) * 5,
        scratch_shapes=scratch,
        compiler_params=pltpu.CompilerParams(
            collective_id=0, has_side_effects=True, vmem_limit_bytes=60 * 1024 * 1024
        ),
    )(patches[0], cotangent[0], windows, gain, w_qkv[0], w_out[0])
    act, gin, out_q, out_o, own_gain = pl.pallas_call(
        finish,
        out_shape=shapes[:4] + (jax.ShapeDtypeStruct((1, FR), F32),),
        in_specs=[hbm] * 5,
        out_specs=(hbm,) * 5,
        scratch_shapes=[pltpu.VMEM(x.shape, x.dtype) for x in shapes] + [pltpu.VMEM((1, FR), F32), dma((10,))],
        compiler_params=pltpu.CompilerParams(vmem_limit_bytes=60 * 1024 * 1024),
    )(*results)
    return (
        act[None, None],
        gin[None, None],
        out_q.transpose(1, 0, 2),
        out_o.transpose(1, 2, 0),
        own_gain,
    )


def solution(mesh):
    in_specs = (
        P(None, ("dp", "mp"), None),
        P(None, ("dp", "mp")),
        P("section", None),
        P("section", None, None),
        P("section", None, None),
        P(None, ("dp", "mp"), None),
    )
    out_specs = (
        P("section", None, ("dp", "mp"), None),
        P("section", None, ("dp", "mp"), None),
        P("section", ("dp", "mp"), None),
        P("section", None, ("dp", "mp")),
        P("section", ("dp", "mp")),
    )
    return jax.shard_map(
        on_device, mesh=mesh, in_specs=in_specs, out_specs=out_specs, check_vma=False
    )
```
